32 devices in a mesh: vel: 8 (over z, y), space: 4 (over x, core).
Axes of the slice: x: 2, y: 2, z: 4, core: 2. Of those that a mesh axis runs over, the one named last changes fastest.
Arguments:
- dist: float32 [4096, 32, 1024], P('vel', 'space'), may hold values from -6 to 6
- vel_index: int32 [3, 4096], P(None, 'vel'), may hold values from 0 to 15, as said below
- relax: float32 [32, 1024], P('space'), may hold values from 0.05 to 0.9
- wall_mask: int32 [32, 1024], P('space'), may hold values 0 or 1
- macro_inverse: float32 [13, 13], replicated, may hold values from -1.5 to 1.5
Outputs:
- dist_out: float32 [4096, 32, 1024], P('vel', 'space')
- macro_fields: float32 [13, 32, 1024], P(None, 'space', 'vel')
- change_norm: float32 [2], replicated
The draws below stay inside these ranges and needn't reach their ends.
Inputs may be any that keep to these rules, and one draw needn't show every extreme that they name: `vel_index`: each point of the velocity grid of 4096 points appears in exactly one column.
All inputs are finite; a program needn't handle non-finite values. No bound on the sum of `wall_mask` on one device may be relied on, other than what follows from the above.
Results may differ from the reference program's by a relative error of at most 0.0003.
Values sent between devices are 32-bit elements; how exact they have to be, the bound alone decides.
No kernel may reach another device: no remote copies, remote signals or barrier semaphores. Data moves between devices by JAX's collectives and lax.ppermute only.
A program may use at most 256 MiB of HBM per device.

```python
import math
import jax
import jax.numpy as jnp
from jax import lax

NVX = 16
NV = 4096
NY = 64
NZ = 16
NX = 32
NYZ = 1024
MOM = 13
SWEEPS = 3
ITERS = 2


def draw_vel_index(key, part):
    order = jax.random.permutation(key, NV).astype(jnp.int32)
    plane = NVX * NVX
    return jnp.stack([order // plane, order // NVX % NVX, order % NVX], 0).astype(jnp.int32)


def draw_macro_inverse(key, part):
    first, second = jax.random.split(jax.random.fold_in(key, 71))
    diagonal = jax.random.uniform(first, (MOM,), jnp.float32, 0.8, 1.2)
    spread = 0.35
    others = jnp.clip(jax.random.normal(second, (MOM, MOM), jnp.float32), -3.6, 3.6) * (spread / 3.6)
    identity = jnp.eye(MOM, dtype=jnp.float32)
    return (identity * diagonal[None, :] + others * (1.0 - identity)).astype(jnp.float32)


def place_ends(values, stream_key, smallest, largest):
    index_at = [jax.random.randint(jax.random.fold_in(stream_key, axis), (), 0, length) for axis, length in enumerate(values.shape)]
    longest = values.shape.index(max(values.shape))
    next_to = index_at[:longest] + [(index_at[longest] + 1) % values.shape[longest]] + index_at[longest + 1:]
    return values.at[tuple(index_at)].set(smallest).at[tuple(next_to)].set(largest)


def level_of(rng, shape, cuts, low, high):
    def one(axis_at, shards_of):
        heights = jax.random.uniform(jax.random.fold_in(jax.random.fold_in(rng, 6), axis_at), (shards_of,), jnp.float32, low / len(cuts), high / len(cuts))
        return jnp.repeat(jnp.exp(heights), shape[axis_at] // shards_of).reshape((-1,) + (1,) * (len(shape) - axis_at - 1))

    factor_of = one(*cuts[0])
    for cut in cuts[1:]:
        factor_of = factor_of * one(*cut)
    return factor_of


def bell_draw(own_key, extent, scale, most, shards=(), kind=jnp.bfloat16):
    array = scale * jax.random.normal(own_key, extent, jnp.float32)
    if shards:
        array = array * level_of(own_key, extent, shards, -0.22, 0.18)
    return jnp.clip(array, -most, most).astype(kind)


def setup_inputs(seed: int = 0) -> dict:
    seeds = jax.random.split(jax.random.key(seed), 6)
    return {
        "dist": bell_draw(seeds[0], (NV, NX, NYZ), 1.0, 6.0, ((0, 8), (1, 4)), jnp.float32),
        "vel_index": draw_vel_index(jax.random.fold_in(seeds[5], 71), 0),
        "relax": jnp.clip(jnp.exp(math.log(0.9) - 2.8903717 * jax.random.uniform(seeds[2], (NX, NYZ), jnp.float32) ** level_of(seeds[2], (NX, NYZ), ((0, 4),), -0.2, 0.2)), 0.05, 0.9),
        "wall_mask": place_ends((jax.random.randint(seeds[3], (NX, NYZ), 0, 8) < 1).astype(jnp.int32), jax.random.fold_in(seeds[3], 1), 0, 1),
        "macro_inverse": draw_macro_inverse(jax.random.fold_in(seeds[5], 71), 0),
    }


speed_range = 4.0
time_step = 0.08
coupling = 0.5

def velocities(vel_index):
    return speed_range * (2.0 * vel_index.astype(jnp.float32) + 1.0 - NVX) / NVX

def bases(velocity):
    cxv, cyv, czv = (velocity[0], velocity[1], velocity[2])
    square = cxv * cxv + cyv * cyv + czv * czv
    weights = (2.0 * speed_range / NVX) ** 3 * math.pi ** (-1.5) * jnp.exp(-square)
    heat = square - 2.5
    functions = jnp.stack([jnp.ones_like(cxv), cxv, cyv, czv, 2.0 * square / 3.0 - 1.0, 2.0 * cxv * cyv, 2.0 * cxv * czv, 2.0 * cyv * czv, cxv * cxv - cyv * cyv, cyv * cyv - czv * czv, cxv * heat, cyv * heat, czv * heat], 0)
    moment_rows = functions * weights[None, :]
    factor = 4.0 / 15.0
    shakhov = jnp.stack([jnp.ones_like(cxv), 2.0 * cxv, 2.0 * cyv, 2.0 * czv, square - 1.5, factor * cxv * heat, factor * cyv * heat, factor * czv * heat], 1)
    walls = jnp.stack([jnp.ones_like(cxv), square - 1.5], 1)
    return (moment_rows, shakhov, walls)

def upwind(block, speed, axis):
    lower = jnp.roll(block, 1, axis)
    higher = jnp.roll(block, -1, axis)
    return jnp.where(speed > 0, block - lower, higher - block)

def stream(block, velocity):
    cxv = velocity[0][:, None, None, None]
    cyv = velocity[1][:, None, None, None]
    czv = velocity[2][:, None, None, None]
    total = cxv * upwind(block, cxv, 1) + cyv * upwind(block, cyv, 2) + czv * upwind(block, czv, 3)
    return block - time_step * total

def smooth(source):
    field = source
    for sweep in range(SWEEPS):
        beside_all = jnp.zeros_like(field)
        for axis in (1, 2, 3):
            beside_all = beside_all + jnp.roll(field, 1, axis) + jnp.roll(field, -1, axis)
        field = (source + coupling * beside_all) / (1.0 + 6.0 * coupling)
    return field

def reference(dist, vel_index, relax, wall_mask, macro_inverse):
    highest = lax.Precision.HIGHEST
    blocksize = min(256, NV)
    nblocks = NV // blocksize
    cells = NX * NY * NZ
    velocity = velocities(vel_index)
    moment_rows, shakhov, walls = bases(velocity)
    vel_blocks = velocity.reshape(3, nblocks, blocksize).transpose(1, 0, 2)
    row_blocks = moment_rows.reshape(MOM, nblocks, blocksize).transpose(1, 0, 2)
    shak_blocks = shakhov.reshape(nblocks, blocksize, 8)
    wall_blocks = walls.reshape(nblocks, blocksize, 2)
    state = dist.reshape(nblocks, blocksize, NX, NY, NZ)
    relax_flat = relax.reshape(1, cells)
    wall_flat = wall_mask.reshape(1, cells)
    norms = []
    updated = None
    for step in range(ITERS):

        def accumulate(carry, pieces):
            block, vblock, rblock = pieces
            read = stream(block, vblock)
            return (carry + jnp.dot(rblock, read.reshape(blocksize, cells), precision=highest), None)
        moments = lax.scan(accumulate, jnp.zeros((MOM, cells), jnp.float32), (state, vel_blocks, row_blocks))[0]
        local = jnp.dot(macro_inverse, moments, precision=highest)
        smoothed = smooth(local[1:5].reshape(4, NX, NY, NZ)).reshape(4, cells)
        updated = jnp.concatenate([local[0:1], smoothed, local[5:]], 0)
        norms.append(jnp.sqrt(jnp.sum((updated - moments) ** 2)))
        fields = jnp.concatenate([updated[0:5], updated[10:13]], 0)
        wall_fields = jnp.stack([updated[0], updated[4]], 0)

        def renew(pieces):
            block, vblock, sblock, wblock = pieces
            read = stream(block, vblock).reshape(blocksize, cells)
            target = jnp.dot(sblock, fields, precision=highest)
            wall_value = jnp.dot(wblock, wall_fields, precision=highest)
            result = jnp.where(wall_flat > 0, wall_value, read + relax_flat * (target - read))
            return result.reshape(blocksize, NX, NY, NZ)
        state = lax.map(renew, (state, vel_blocks, shak_blocks, wall_blocks))
    return (state.reshape(NV, NX, NY * NZ), updated.reshape(MOM, NX, NY * NZ), jnp.stack(norms))
```

```python
import functools
import math

import jax
import jax.numpy as jnp
import numpy as np
from jax import lax
from jax.experimental import pallas as pl
from jax.experimental.pallas import tpu as pltpu
from jax.sharding import PartitionSpec as P

NVX = 16
NZ = 16
MOM = 13
SWEEPS = 3
LANES = 128
SUB = 8
SETS = 7
PICK = (0, 1, 2, 3, 4, 10, 11, 12)

speed_range = 4.0
time_step = 0.08
coupling = 0.5
MIB = 2**20

UP, M1, DOWN, AA, PAY = 0, 40, 144, 184, 288


def functions_of(cx, cy, cz):
    square = cx * cx + cy * cy + cz * cz
    heat = square - 2.5
    one = cx * 0.0 + 1.0
    rows = [
        one, cx, cy, cz, 2.0 * square / 3.0 - 1.0, 2.0 * cx * cy, 2.0 * cx * cz, 2.0 * cy * cz,
        cx * cx - cy * cy, cy * cy - cz * cz, cx * heat, cy * heat, cz * heat,
    ]
    factor = 4.0 / 15.0
    shakhov = [
        one, 2.0 * cx, 2.0 * cy, 2.0 * cz, square - 1.5,
        factor * cx * heat, factor * cy * heat, factor * cz * heat,
    ]
    return rows, shakhov, square


def half_speeds(cx, cy, cz):
    out = []
    for c in (cx, cy, cz):
        out.append(time_step * c * (c > 0))
        out.append(-time_step * c * (c < 0))
    return out


@functools.lru_cache(None)
def stream_matrices():
    line = speed_range * (2.0 * np.arange(NVX) + 1.0 - NVX) / NVX
    cx, cy, cz = (g.reshape(-1) for g in np.meshgrid(line, line, line, indexing="ij"))
    rows, shakhov, square = functions_of(cx, cy, cz)
    weight = (2.0 * speed_range / NVX) ** 3 * math.pi ** (-1.5) * np.exp(-square)
    rows = np.stack(rows) * weight
    shakhov = np.stack(shakhov)
    speeds = half_speeds(cx, cy, cz)
    stay = 1.0 - sum(speeds)
    out = np.stack([(rows * s) @ shakhov.T for s in [stay] + speeds])
    out[np.abs(out) < 1e-13] = 0.0
    return out


def split(value):
    high = value.astype(jnp.bfloat16)
    low = (value - high.astype(jnp.float32)).astype(jnp.bfloat16)
    return high, low


class Group:
    def __init__(self, tx, ty, tz):
        self.ax, self.ay, self.az = jnp.abs(tx), jnp.abs(ty), jnp.abs(tz)
        self.stay = 1.0 - self.ax - self.ay - self.az
        self.px = tx > 0
        py, pz = ty > 0, tz > 0
        lane = lax.broadcasted_iota(jnp.int32, tx.shape, 1)
        zl = lane & (NZ - 1)
        self.zfrom = jnp.where(
            pz,
            jnp.where(zl == 0, lane + (NZ - 1), lane - 1),
            jnp.where(zl == NZ - 1, lane - (NZ - 1), lane + 1),
        )
        self.yfrom = jnp.where(py, (lane - NZ) & (LANES - 1), (lane + NZ) & (LANES - 1))
        self.lower = py & (lane >= LANES - NZ)
        self.higher = jnp.logical_not(py) & (lane < NZ)

    def across(self, row):
        count = len(row)
        out = []
        for k in range(count):
            beside = jnp.where(
                self.lower, row[(k - 1) % count], jnp.where(self.higher, row[(k + 1) % count], row[k])
            )
            in_y = jnp.take_along_axis(beside, self.yfrom, axis=1)
            in_z = jnp.take_along_axis(row[k], self.zfrom, axis=1)
            out.append(self.stay * row[k] + self.ay * in_y + self.az * in_z)
        return out

    def stream(self, planes, width, put):
        before, now, after = None, planes(0), None
        for x in range(width):
            after = planes(x + 1) if x + 1 < width else None
            mid = self.across(now)
            out = []
            for k in range(len(now)):
                lo = before[k] if before is not None else jnp.zeros_like(now[k])
                hi = after[k] if after is not None else jnp.zeros_like(now[k])
                out.append(mid[k] + self.ax * jnp.where(self.px, lo, hi))
            put(x, out, now)
            before, now = now, after


def group_at(dtc_ref, rows):
    return Group(dtc_ref[0, rows, :], dtc_ref[1, rows, :], dtc_ref[2, rows, :])


def lane_blocks(value):
    return [value[:, k * LANES : (k + 1) * LANES] for k in range(value.shape[1] // LANES)]


def roll_y(value, sign):
    cells = value.shape[1]
    return pltpu.roll(value, NZ if sign > 0 else cells - NZ, axis=1)


def roll_z(value, sign):
    cells = value.shape[1]
    zl = lax.broadcasted_iota(jnp.int32, value.shape, 1) & (NZ - 1)
    if sign > 0:
        return jnp.where(zl == 0, pltpu.roll(value, cells - (NZ - 1), axis=1), pltpu.roll(value, 1, axis=1))
    return jnp.where(zl == NZ - 1, pltpu.roll(value, NZ - 1, axis=1), pltpu.roll(value, cells - 1, axis=1))


def outflow_kernel(dist_ref, dtc_ref, out_ref, *, count, blocks):
    px = dtc_ref[0] > 0
    stride = blocks * SUB
    for k in range(blocks):
        at = slice(k * LANES, (k + 1) * LANES)
        plane = [dist_ref[pl.ds(k * SUB + x, count, stride=stride), :] for x in (0, 1, SUB - 2, SUB - 1)]
        out_ref[0, :, at] = jnp.where(px, plane[3], plane[0])
        out_ref[1, :, at] = jnp.where(px, plane[2], plane[1])


def outflow(flat, dtc, vels, blocks):
    count = min(64, vels)
    rows = count * blocks * SUB
    cells = blocks * LANES
    return pl.pallas_call(
        functools.partial(outflow_kernel, count=count, blocks=blocks),
        grid=(vels // count,),
        in_specs=[
            pl.BlockSpec((rows, LANES), lambda i: (i, 0)),
            pl.BlockSpec((1, count, LANES), lambda i: (0, i, 0)),
        ],
        out_specs=pl.BlockSpec((2, count, cells), lambda i: (0, i, 0)),
        out_shape=jax.ShapeDtypeStruct((2, vels, cells), jnp.float32),
        compiler_params=pltpu.CompilerParams(vmem_limit_bytes=24 * MIB),
        cost_estimate=pl.CostEstimate(flops=0, bytes_accessed=20 * vels * blocks * SUB * LANES // 4, transcendentals=0),
        name="outflow_planes",
    )(flat, dtc)


def moments_kernel(me_ref, dist_ref, dtc_ref, index_ref, cst_ref, *refs, vels, blocks):
    outs = refs[:blocks]
    held, rhi, rlo, table, wst, acc, gacc, pay, sems = refs[blocks:]
    stride = blocks * SUB
    chunk = min(64, vels)
    chunks = vels // chunk
    copies = [
        pltpu.make_async_copy(
            dist_ref.at[pl.ds(c * chunk * stride, chunk * stride)],
            held.at[pl.ds(c * chunk * stride, chunk * stride)],
            sems.at[c],
        )
        for c in range(chunks)
    ]
    for copy in copies:
        copy.start()

    speed = [speed_range * (2.0 * index_ref[a : a + 1, :].astype(jnp.float32) + 1.0 - NVX) / NVX for a in range(3)]
    rows, _, square = functions_of(*speed)
    weight = (2.0 * speed_range / NVX) ** 3 * math.pi ** (-1.5) * jnp.exp(-square)
    table[...] = jnp.zeros_like(table)
    for m, row in enumerate(rows):
        table[m : m + 1, :] = row * weight
    base = table[...]
    speeds = []
    for c in speed:
        speeds.append(jnp.where(c > 0, time_step * c, 0.0))
        speeds.append(jnp.where(c < 0, -time_step * c, 0.0))
    full = jnp.concatenate([base] + [base * s for s in speeds], axis=0)
    span = SETS * 16
    for variant, factor in enumerate([None, speeds[0], speeds[1]]):
        high, low = split(full if factor is None else full * factor)
        wst[variant, 0:span, :] = high
        wst[variant, span : 2 * span, :] = low

    for c in range(chunks):
        copies[c].wait()

        @pl.loop(0, chunk // 16)
        def _(i, c=c):
            first = pl.multiple_of(c * chunk + i * 16, 16)
            here = pl.ds(first, 16)
            group = group_at(dtc_ref, here)
            origin = first * stride

            def planes(x):
                return [held[pl.ds(origin + k * SUB + x, 16, stride=stride), :] for k in range(blocks)]

            def put(x, blocks_out, now):
                for k, value in enumerate(blocks_out):
                    at = slice(k * LANES, (k + 1) * LANES)
                    high, low = split(value)
                    rhi[x, here, at] = high
                    rlo[x, here, at] = low
                if x in (0, SUB - 1):
                    slot = SUB if x == SUB - 1 else SUB + 1
                    for k, value in enumerate(now):
                        at = slice(k * LANES, (k + 1) * LANES)
                        high, low = split(value)
                        rhi[slot, here, at] = high
                        rlo[slot, here, at] = low

            group.stream(planes, SUB, put)

    wide = 2 * LANES

    @pl.loop(0, blocks // 2)
    def _(b):
        at = pl.ds(pl.multiple_of(b * wide, wide), wide)
        for slot in range(SUB + 2):
            variant = max(0, slot - SUB + 1)
            first = jnp.dot(wst[variant], rhi[slot, :, at], preferred_element_type=jnp.float32)
            second = jnp.dot(wst[variant, 0:span, :], rlo[slot, :, at], preferred_element_type=jnp.float32)
            total = first[0:span] + first[span:] + second
            if slot < SUB:
                for j in range(2):
                    acc[2 * b + j, pl.ds(slot, span, stride=SUB), :] = total[:, j * LANES : (j + 1) * LANES]
            else:
                gacc[slot - SUB, :, at] = total

    al = cst_ref[0, 0:SUB, :]
    beyond = cst_ref[0, SUB : SUB + 1, :]
    below = cst_ref[0, 2 * SUB - 1 : 2 * SUB, :]
    plane = lax.broadcasted_iota(jnp.int32, al.shape, 0)

    def own(i, m):
        first = (i * 16 + m) * SUB
        return jnp.concatenate([acc[k, first : first + SUB, :] for k in range(blocks)], axis=1)

    for m in range(MOM):
        sets = [own(i, m) for i in range(SETS)]
        value = al * (sets[0] - sum(sets[1:]))
        value = value + jnp.where(plane == 0, 0.0, pltpu.roll(al * sets[1], 1, axis=0))
        value = value + jnp.where(plane == SUB - 1, 0.0, pltpu.roll(al * sets[2], SUB - 1, axis=0))
        value = value + roll_y(al * sets[3], 1) + roll_y(al * sets[4], -1)
        value = value + roll_z(al * sets[5], 1) + roll_z(al * sets[6], -1)
        for k in range(blocks):
            at = slice(k * LANES, (k + 1) * LANES)
            pay[k, M1 + m * SUB : M1 + (m + 1) * SUB, :] = sets[0][:, at]
            pay[k, AA + m * SUB : AA + (m + 1) * SUB, :] = value[:, at]

    for side, (scale, edge, toward, start) in enumerate([(beyond, SUB - 1, 1, UP), (below, 0, 2, DOWN)]):
        sets = [gacc[side, i * 16 : (i + 1) * 16, :] for i in range(SETS)]
        near = scale * (sets[0] - sum(sets[1:]))
        near = near + roll_y(scale * sets[3], 1) + roll_y(scale * sets[4], -1)
        near = near + roll_z(scale * sets[5], 1) + roll_z(scale * sets[6], -1)
        out_of = jnp.concatenate(
            [acc[k, pl.ds(toward * 16 * SUB + edge, 16, stride=SUB), :] for k in range(blocks)], axis=1
        )
        near = near + al[edge : edge + 1, :] * out_of
        far = scale * sets[toward]
        for k in range(blocks):
            at = slice(k * LANES, (k + 1) * LANES)
            for j, value in enumerate((sets[0], near, far)):
                pay[k, start + j * MOM : start + (j + 1) * MOM, :] = value[0:MOM, at]
            pay[k, start + 3 * MOM : start + 3 * MOM + 1, :] = jnp.zeros((1, LANES), jnp.float32)

    mine = me_ref[0]
    for k in range(blocks):
        outs[k][...] = pay[lax.rem(mine + k, blocks)]


def both_moments(place, flat, dtc, vel_index, cst, vels, blocks):
    cells = blocks * LANES
    vmem = pl.BlockSpec(memory_space=pltpu.VMEM)
    span = SETS * 16
    chunks = vels // min(64, vels)
    return pl.pallas_call(
        functools.partial(moments_kernel, vels=vels, blocks=blocks),
        in_specs=[pl.BlockSpec(memory_space=pltpu.SMEM), pl.BlockSpec(memory_space=pl.ANY), vmem, vmem, vmem],
        out_specs=[vmem] * blocks,
        out_shape=[jax.ShapeDtypeStruct((PAY, LANES), jnp.float32)] * blocks,
        scratch_shapes=[
            pltpu.VMEM((vels * blocks * SUB, LANES), jnp.float32),
            pltpu.VMEM((SUB + 2, vels, cells), jnp.bfloat16),
            pltpu.VMEM((SUB + 2, vels, cells), jnp.bfloat16),
            pltpu.VMEM((16, vels), jnp.float32),
            pltpu.VMEM((3, 2 * span, vels), jnp.bfloat16),
            pltpu.VMEM((blocks, span * SUB, LANES), jnp.float32),
            pltpu.VMEM((2, span, cells), jnp.float32),
            pltpu.VMEM((blocks, PAY, LANES), jnp.float32),
            pltpu.SemaphoreType.DMA((chunks,)),
        ],
        compiler_params=pltpu.CompilerParams(vmem_limit_bytes=54 * MIB),
        cost_estimate=pl.CostEstimate(
            flops=2 * 336 * vels * 10 * cells, bytes_accessed=4 * vels * SUB * cells, transcendentals=0
        ),
        name="moments_of_both",
    )(place, flat, dtc, vel_index, cst)


def carried_kernel(dist_ref, dtc_ref, al_ref, out_ref, mid, *, count, blocks):
    stride = blocks * SUB

    @pl.loop(0, count // SUB)
    def _(i):
        first = pl.multiple_of(i * SUB, SUB)
        here = pl.ds(first, SUB)
        group = group_at(dtc_ref, here)
        origin = first * stride

        def planes(x):
            return [dist_ref[pl.ds(origin + k * SUB + x, SUB, stride=stride), :] for k in range(blocks)]

        def scaled(x, k):
            return al_ref[x : x + 1, k * LANES : (k + 1) * LANES]

        def put_mid(x, values, now):
            for k, value in enumerate(values):
                mid[x, k] = scaled(x, k) * value

        def put_out(x, values, now):
            for k, value in enumerate(values):
                out_ref[k, x, here, :] = scaled(x, k) * value

        group.stream(planes, SUB, put_mid)
        group.stream(lambda x: [mid[x, k] for k in range(blocks)], SUB, put_out)


def carried(flat, dtc, al, vels, blocks):
    count = min(64, vels)
    rows = count * blocks * SUB
    return pl.pallas_call(
        functools.partial(carried_kernel, count=count, blocks=blocks),
        grid=(vels // count,),
        in_specs=[
            pl.BlockSpec((rows, LANES), lambda i: (i, 0)),
            pl.BlockSpec((3, count, LANES), lambda i: (0, i, 0)),
            pl.BlockSpec((SUB, blocks * LANES), lambda i: (0, 0)),
        ],
        out_specs=pl.BlockSpec((blocks, SUB, count, LANES), lambda i: (0, 0, i, 0)),
        out_shape=jax.ShapeDtypeStruct((blocks, SUB, vels, LANES), jnp.float32),
        scratch_shapes=[pltpu.VMEM((SUB, blocks, SUB, LANES), jnp.float32)],
        compiler_params=pltpu.CompilerParams(vmem_limit_bytes=24 * MIB),
        cost_estimate=pl.CostEstimate(
            flops=40 * vels * blocks * SUB * LANES, bytes_accessed=8 * vels * blocks * SUB * LANES, transcendentals=0
        ),
        name="carried_part",
    )(flat, dtc, al)


def inflow_kernel(core_ref, swap_ref, first_ref, second_ref, dtc_ref, al_ref, out_ref, *, count, blocks, half):
    core = core_ref[0]
    mine = (pl.program_id(0) // half) == core

    @pl.loop(0, count // SUB)
    def _(i):
        here = pl.ds(pl.multiple_of(i * SUB, SUB), SUB)
        group = group_at(dtc_ref, here)
        from_far = group.px == (core == 0)

        def halo(depth):
            far = jnp.where(mine, first_ref[depth, here, :], second_ref[depth, here, :])
            near = swap_ref[depth, here, :]
            return [jnp.where(from_far, a, b) for a, b in zip(lane_blocks(far), lane_blocks(near))]

        def scale(k, when_up, when_down):
            at = slice(k * LANES, (k + 1) * LANES)
            return jnp.where(group.px, al_ref[when_up : when_up + 1, at], al_ref[when_down : when_down + 1, at])

        near, far = halo(0), halo(1)
        edge = [scale(k, 0, SUB - 1) * group.ax * near[k] for k in range(blocks)]
        beyond = group.across(near)
        inside = group.across(edge)
        for k in range(blocks):
            streamed = beyond[k] + group.ax * far[k]
            value = inside[k] + group.ax * scale(k, 2 * SUB - 1, SUB) * streamed
            out_ref[k, 0, here, :] = scale(k, 0, SUB - 1) * value
            out_ref[k, 1, here, :] = scale(k, 1, SUB - 2) * group.ax * edge[k]


def inflow(core, swap, first, second, dtc, al16, vels, blocks):
    halves = vels // first.shape[1]
    count = min(64, first.shape[1])
    half = first.shape[1] // count
    cells = blocks * LANES
    narrow = pl.BlockSpec((2, count, cells), lambda i: (0, i % half, 0))
    return pl.pallas_call(
        functools.partial(inflow_kernel, count=count, blocks=blocks, half=half),
        grid=(vels // count,),
        in_specs=[
            pl.BlockSpec(memory_space=pltpu.SMEM),
            pl.BlockSpec((2, count, cells), lambda i: (0, i, 0)),
            narrow,
            narrow,
            pl.BlockSpec((3, count, LANES), lambda i: (0, i, 0)),
            pl.BlockSpec((2 * SUB, cells), lambda i: (0, 0)),
        ],
        out_specs=pl.BlockSpec((blocks, 2, count, LANES), lambda i: (0, 0, i, 0)),
        out_shape=jax.ShapeDtypeStruct((blocks, 2, vels, LANES), jnp.float32),
        compiler_params=pltpu.CompilerParams(vmem_limit_bytes=24 * MIB),
        cost_estimate=pl.CostEstimate(flops=60 * vels * cells, bytes_accessed=24 * vels * cells, transcendentals=0),
        name="inflow_part",
    )(core, swap, first, second, dtc, al16)


def small_call(kernel, outs, name, specs, args, scratch=(), limit=16):
    vmem = pl.BlockSpec(memory_space=pltpu.VMEM)
    smem = pl.BlockSpec(memory_space=pltpu.SMEM)
    return pl.pallas_call(
        kernel,
        in_specs=[smem if s == "s" else vmem for s in specs],
        out_specs=[vmem] * len(outs),
        out_shape=[jax.ShapeDtypeStruct(o, jnp.float32) for o in outs],
        scratch_shapes=list(scratch),
        compiler_params=pltpu.CompilerParams(vmem_limit_bytes=limit * MIB),
        name=name,
    )(*args)


def total_kernel(*refs):
    parts, (all_ref, up_ref, down_ref) = refs[:-3], refs[-3:]
    value = parts[0][...]
    for part in parts[1:]:
        value = value + part[...]
    all_ref[...] = value
    up_ref[...] = value[UP:DOWN]
    down_ref[...] = value[M1:AA]


def mix(inverse, values):
    return [sum(inverse[k, j] * values[j] for j in range(MOM)) for k in range(MOM)]


def chunk_kernel(inv_ref, own_ref, low_ref, high_ref, send_ref, keep_ref):
    plane = lax.broadcasted_iota(jnp.int32, (SUB, LANES), 0)
    inverse = {(k, j): inv_ref[k, j] for k in range(MOM) for j in range(MOM)}
    inner, outer, later = [], [], []
    for m in range(MOM):

        def row(ref, at):
            return ref[at : at + 1, :]

        first = own_ref[M1 + m * SUB : M1 + (m + 1) * SUB, :]
        second = own_ref[AA + m * SUB : AA + (m + 1) * SUB, :]
        low = low_ref[M1 + m * SUB : M1 + (m + 1) * SUB, :]
        high = high_ref[m * SUB : (m + 1) * SUB, :]
        below = DOWN - M1 + m
        inner.append(
            first + jnp.where(plane == 0, row(low_ref, m), 0.0) + jnp.where(plane == SUB - 1, row(high_ref, below), 0.0)
        )
        outer.append(
            jnp.where(plane < SUB // 2, high, low)
            + jnp.where(plane == 0, row(own_ref, UP + m), 0.0)
            + jnp.where(plane == SUB - 1, row(own_ref, DOWN + m), 0.0)
        )
        later.append(
            second
            + jnp.where(plane == 0, row(low_ref, MOM + m), 0.0)
            + jnp.where(plane == 1, row(low_ref, 2 * MOM + m), 0.0)
            + jnp.where(plane == SUB - 1, row(high_ref, below + MOM), 0.0)
            + jnp.where(plane == SUB - 2, row(high_ref, below + 2 * MOM), 0.0)
        )
    local, around, ahead = (mix(inverse, v) for v in (inner, outer, later))
    for n, k in enumerate(PICK):
        send_ref[n * 16 : n * 16 + SUB, :] = local[k]
        send_ref[n * 16 + SUB : (n + 1) * 16, :] = around[k]
        send_ref[128 + n * SUB : 128 + (n + 1) * SUB, :] = ahead[k]
    for m in range(MOM):
        for n, values in enumerate((inner, local, later, ahead)):
            keep_ref[(n * MOM + m) * SUB : (n * MOM + m + 1) * SUB, :] = values[m]


def sweeps(source):
    rows = source.shape[0]
    field = source
    for _ in range(SWEEPS):
        beside = pltpu.roll(field, 1, axis=0) + pltpu.roll(field, rows - 1, axis=0)
        beside = beside + roll_y(field, 1) + roll_y(field, -1) + roll_z(field, 1) + roll_z(field, -1)
        field = (source + coupling * beside) * (1.0 / (1.0 + 6.0 * coupling))
    return field


def fields_kernel(place_ref, inv_ref, cst_ref, keep_ref, *refs, blocks):
    parts = refs[:blocks]
    h1_ref, next_ref, up_ref, down_ref, own_ref, norm_ref, whole, wide = refs[blocks:]
    mine = place_ref[0]
    for k in range(blocks):
        whole[lax.rem(mine + (blocks - k), blocks)] = parts[k][...]

    def rows(first, count):
        return jnp.concatenate([whole[k, first : first + count, :] for k in range(blocks)], axis=1)

    al = cst_ref[0, 0:SUB, :]
    updated, moved = [], []
    for n in range(8):
        value = rows(n * 16, 16)
        if 1 <= n <= 4:
            value = sweeps(value)
        updated.append(value[0:SUB])
        given = cst_ref[1 if n in (0, 4) else 2] * value
        inside = given[0:SUB]
        shifted = [
            inside,
            pltpu.roll(given, 1, axis=0)[0:SUB],
            pltpu.roll(given, 2 * SUB - 1, axis=0)[0:SUB],
            roll_y(inside, 1),
            roll_y(inside, -1),
            roll_z(inside, 1),
            roll_z(inside, -1),
        ]
        for s in range(SETS):
            value = al * shifted[s]
            for k in range(blocks):
                first = (s * 8 + n) * SUB
                h1_ref[k, first : first + SUB, :] = value[:, k * LANES : (k + 1) * LANES]
        moved.append(shifted)

    matrices = stream_matrices()
    added = []
    for m in range(MOM):
        value = None
        for s in range(SETS):
            for n in range(8):
                factor = float(matrices[s, m, n])
                if factor != 0.0:
                    term = factor * moved[n][s]
                    value = term if value is None else value + term
        added.append(value)
    inverse = {(k, j): inv_ref[k, j] for k in range(MOM) for j in range(MOM)}
    mixed = mix(inverse, added)

    for n, k in enumerate(PICK):
        value = rows(128 + n * SUB, SUB) + mixed[k]
        next_ref[n * SUB : (n + 1) * SUB, :] = value
        if 1 <= n <= 4:
            up_ref[(n - 1) * 4 : n * 4, :] = value[SUB // 2 :]
            down_ref[(n - 1) * 4 : n * 4, :] = value[: SUB // 2]

    def keep(n, m):
        return keep_ref[(n * MOM + m) * SUB : (n * MOM + m + 1) * SUB, :]

    def owned(value):
        for k in range(blocks):
            wide[k] = value[:, k * LANES : (k + 1) * LANES]
        return wide[mine]

    square = jnp.zeros((SUB, LANES), jnp.float32)
    for m in range(MOM):
        mine_now = owned(updated[m]) if 1 <= m <= 4 else keep(1, m)
        square = square + (mine_now - keep(0, m)) ** 2
        own_ref[m * SUB : (m + 1) * SUB, :] = keep(2, m) + owned(added[m])
        own_ref[(MOM + m) * SUB : (MOM + m + 1) * SUB, :] = keep(3, m) + owned(mixed[m])
    norm_ref[...] = square


def last_kernel(place_ref, cst_ref, next_ref, low_ref, high_ref, own_ref, h2_ref, out_ref, norm_ref, wide, *, blocks):
    mine = place_ref[0]
    square = jnp.zeros((SUB, LANES), jnp.float32)
    for n in range(8):
        value = next_ref[n * SUB : (n + 1) * SUB, :]
        if 1 <= n <= 4:
            at = slice((n - 1) * 4, n * 4)
            value = sweeps(jnp.concatenate([value, high_ref[at, :], low_ref[at, :]], axis=0))[0:SUB]
            for k in range(blocks):
                wide[n - 1, k] = value[:, k * LANES : (k + 1) * LANES]
        given = cst_ref[1 if n in (0, 4) else 2, 0:SUB, :] * value
        for k in range(blocks):
            h2_ref[k, n * SUB : (n + 1) * SUB, :] = given[:, k * LANES : (k + 1) * LANES]
    for m in range(MOM):
        moments = own_ref[m * SUB : (m + 1) * SUB, :]
        if 1 <= m <= 4:
            value = wide[m - 1, mine]
        else:
            value = own_ref[(MOM + m) * SUB : (MOM + m + 1) * SUB, :]
        out_ref[m] = value
        square = square + (value - moments) ** 2
    norm_ref[...] = square


def finish_kernel(carried_ref, inflow_ref, h1_ref, h2_ref, rows_ref, dtc_ref, out_ref, *, vels):
    out = out_ref.reshape(vels * SUB, LANES)
    px = dtc_ref[0] > 0
    for x in range(0, SUB, 2):
        field = jnp.concatenate(
            [
                jnp.concatenate(
                    [h1_ref[0, pl.ds(x + j, SETS * 8, stride=SUB), :], h2_ref[0, pl.ds(x + j, 8, stride=SUB), :]], axis=0
                )
                for j in range(2)
            ],
            axis=1,
        )
        high, low = split(field)
        term = jnp.dot(
            rows_ref[...], jnp.concatenate([high, low, high], axis=0), preferred_element_type=jnp.float32
        )
        for j in range(2):
            value = carried_ref[0, x + j] + term[:, j * LANES : (j + 1) * LANES]
            if x + j in (0, 1):
                value = value + jnp.where(px, inflow_ref[0, x + j], 0.0)
            elif x + j in (SUB - 2, SUB - 1):
                value = value + jnp.where(px, 0.0, inflow_ref[0, SUB - 1 - x - j])
            out[pl.ds(x + j, vels, stride=SUB), :] = value


def finish(carried_part, inflow_part, h1, h2, rows, dtc, vels, blocks):
    return pl.pallas_call(
        functools.partial(finish_kernel, vels=vels),
        grid=(blocks,),
        in_specs=[
            pl.BlockSpec((1, SUB, vels, LANES), lambda k: (k, 0, 0, 0)),
            pl.BlockSpec((1, 2, vels, LANES), lambda k: (k, 0, 0, 0)),
            pl.BlockSpec((1, SETS * 8 * SUB, LANES), lambda k: (k, 0, 0)),
            pl.BlockSpec((1, 8 * SUB, LANES), lambda k: (k, 0, 0)),
            pl.BlockSpec((vels, 3 * 64), lambda k: (0, 0)),
            pl.BlockSpec((1, vels, LANES), lambda k: (0, 0, 0)),
        ],
        out_specs=pl.BlockSpec((vels, 1, SUB, LANES), lambda k: (0, k, 0, 0)),
        out_shape=jax.ShapeDtypeStruct((vels, blocks, SUB, LANES), jnp.float32),
        compiler_params=pltpu.CompilerParams(vmem_limit_bytes=32 * MIB),
        cost_estimate=pl.CostEstimate(
            flops=2 * 192 * vels * blocks * SUB * LANES, bytes_accessed=8 * vels * blocks * SUB * LANES, transcendentals=0
        ),
        name="finish_dist",
    )(carried_part, inflow_part, h1, h2, rows, dtc)


def ring(axis, step):
    size = lax.axis_size(axis)
    return [(i, (i + step) % size) for i in range(size)]


def shards(dist, vel_index, relax, wall_mask, macro_inverse):
    vels, width, cells = dist.shape
    blocks = cells // LANES
    peers, slabs = lax.axis_size("vel"), lax.axis_size("space")
    assert width == SUB and peers % blocks == 0 and slabs == 4 and blocks % 2 == 0
    sub = peers // blocks
    me = lax.axis_index("vel")
    place = (me // sub).astype(jnp.int32).reshape(1)
    core = (lax.axis_index("space") % 2).astype(jnp.int32).reshape(1)

    flat = dist.reshape(vels, width, blocks, LANES).transpose(0, 2, 1, 3).reshape(vels * blocks * width, LANES)
    speed = speed_range * (2.0 * vel_index.astype(jnp.float32) + 1.0 - NVX) / NVX
    dtc = jnp.broadcast_to((time_step * speed)[:, :, None], (3, vels, LANES))

    leaving = outflow(flat, dtc, vels, blocks)
    swap = lax.ppermute(leaving, "space", [(i, i ^ 1) for i in range(slabs)])

    wall = wall_mask > 0
    coefficients = jnp.stack(
        [
            jnp.where(wall, 0.0, 1.0 - relax),
            jnp.where(wall, 1.0, relax),
            jnp.where(wall, 0.0, relax),
        ],
        0,
    )
    from_low = lax.ppermute(coefficients[:, SUB - 1 :], "space", ring("space", 1))
    from_high = lax.ppermute(coefficients[:, :1], "space", ring("space", -1))
    cst = jnp.concatenate(
        [coefficients, from_high, jnp.zeros((3, SUB - 2, cells), jnp.float32), from_low], 1
    )

    half = vels // 2
    start = core[0] * half
    mine = lax.dynamic_slice_in_dim(leaving, start, half, 1)
    other = lax.dynamic_slice_in_dim(swap, start, half, 1)
    plus = lax.dynamic_slice_in_dim(speed[0], start, half, 0) > 0
    across = jnp.where((plus == (core[0] == 1))[None, :, None], mine, other)
    first = lax.ppermute(across, "space", [(i, i ^ 2) for i in range(slabs)])
    second = lax.ppermute(first, "space", [(i, i ^ 1) for i in range(slabs)])

    parts = both_moments(place, flat, dtc, vel_index, cst, vels, blocks)
    got = [parts[0]] + [lax.ppermute(parts[k], "vel", ring("vel", k * sub)) for k in range(1, blocks)]
    if sub > 1:
        part = sum(got)
        got = [part]
        for k in range(1, sub):
            pairs = [(i, i // sub * sub + (i % sub + k) % sub) for i in range(peers)]
            got.append(lax.ppermute(part, "vel", pairs))
    chunk, up, down = small_call(
        total_kernel, [(PAY, LANES), (DOWN - UP, LANES), (AA - M1, LANES)], "sum_moments", "v" * len(got), got
    )
    low = lax.ppermute(up, "space", ring("space", 1))
    high = lax.ppermute(down, "space", ring("space", -1))
    send, keep = small_call(
        chunk_kernel, [(192, LANES), (4 * MOM * SUB, LANES)], "local_fields", "svvv", (macro_inverse, chunk, low, high)
    )
    pieces = [send] + [lax.ppermute(send, "vel", ring("vel", k * sub)) for k in range(1, blocks)]

    carried_part = carried(flat, dtc, coefficients[0], vels, blocks)

    h1, following, up2, down2, own, norm1 = small_call(
        functools.partial(fields_kernel, blocks=blocks),
        [
            (blocks, SETS * 8 * SUB, LANES),
            (8 * SUB, cells),
            (16, cells),
            (16, cells),
            (2 * MOM * SUB, LANES),
            (SUB, LANES),
        ],
        "first_fields",
        "ssvv" + "v" * blocks,
        (place, macro_inverse, cst, keep, *pieces),
        [pltpu.VMEM((blocks, 192, LANES), jnp.float32), pltpu.VMEM((blocks, SUB, LANES), jnp.float32)],
        32,
    )
    low2 = lax.ppermute(up2, "space", ring("space", 1))
    high2 = lax.ppermute(down2, "space", ring("space", -1))
    h2, owned, norm2 = small_call(
        functools.partial(last_kernel, blocks=blocks),
        [(blocks, 8 * SUB, LANES), (MOM, SUB, LANES), (SUB, LANES)],
        "last_fields",
        "svvvvv",
        (place, cst, following, low2, high2, own),
        [pltpu.VMEM((4, blocks, SUB, LANES), jnp.float32)],
        32,
    )
    squares = jnp.stack([jnp.sum(norm1), jnp.sum(norm2)]) / sub
    norms = jnp.sqrt(lax.psum(squares, ("vel", "space")))
    if sub > 1:
        owned = lax.dynamic_slice_in_dim(owned, (me % sub) * (LANES // sub), LANES // sub, 2)

    speeds = half_speeds(*[speed[a][:, None] for a in range(3)])
    basis = jnp.stack(functions_of(*speed)[1], 1)
    stay = 1.0 - sum(speeds)
    rows = jnp.concatenate([basis * s for s in [stay] + speeds] + [basis], 1)
    rows_high = lax.reduce_precision(rows, 8, 7)
    rows = jnp.concatenate([rows_high, rows_high, rows - rows_high], 1).astype(jnp.bfloat16)

    inflow_part = inflow(core, swap, first, second, dtc, cst[0], vels, blocks)
    out = finish(carried_part, inflow_part, h1, h2, rows, dtc, vels, blocks)
    out = out.transpose(0, 2, 1, 3).reshape(vels, width, cells)
    return (out, owned, norms)


def solution(mesh):
    return jax.shard_map(
        shards,
        mesh=mesh,
        in_specs=(P("vel", "space", None), P(None, "vel"), P("space", None), P("space", None), P()),
        out_specs=(P("vel", "space", None), P(None, "space", "vel"), P()),
        check_vma=False,
    )
```

```python
import functools
import math

import jax
import jax.numpy as jnp
import numpy as np
from jax import lax
from jax.experimental import pallas as pl
from jax.experimental.pallas import tpu as pltpu
from jax.sharding import PartitionSpec as P

NVX = 16
NZ = 16
MOM = 13
SWEEPS = 3
LANES = 128
SUB = 8
SETS = 7
PICK = (0, 1, 2, 3, 4, 10, 11, 12)

speed_range = 4.0
time_step = 0.08
coupling = 0.5
MIB = 2**20
PIECES = 8

UP, M1, DOWN, AA, PAY = 0, 40, 144, 184, 288
STILL = (0, 10, 11, 12)
MOVED, FIXED, EDGE, LATER, SQUARE, SENT = 64, 96, 128, 136, 240, 248


def functions_of(cx, cy, cz):
    square = cx * cx + cy * cy + cz * cz
    heat = square - 2.5
    one = cx * 0.0 + 1.0
    rows = [
        one, cx, cy, cz, 2.0 * square / 3.0 - 1.0, 2.0 * cx * cy, 2.0 * cx * cz, 2.0 * cy * cz,
        cx * cx - cy * cy, cy * cy - cz * cz, cx * heat, cy * heat, cz * heat,
    ]
    factor = 4.0 / 15.0
    shakhov = [
        one, 2.0 * cx, 2.0 * cy, 2.0 * cz, square - 1.5,
        factor * cx * heat, factor * cy * heat, factor * cz * heat,
    ]
    return rows, shakhov, square


def half_speeds(cx, cy, cz):
    out = []
    for c in (cx, cy, cz):
        out.append(time_step * c * (c > 0))
        out.append(-time_step * c * (c < 0))
    return out


@functools.lru_cache(None)
def stream_matrices():
    line = speed_range * (2.0 * np.arange(NVX) + 1.0 - NVX) / NVX
    cx, cy, cz = (g.reshape(-1) for g in np.meshgrid(line, line, line, indexing="ij"))
    rows, shakhov, square = functions_of(cx, cy, cz)
    weight = (2.0 * speed_range / NVX) ** 3 * math.pi ** (-1.5) * np.exp(-square)
    rows = np.stack(rows) * weight
    shakhov = np.stack(shakhov)
    speeds = half_speeds(cx, cy, cz)
    stay = 1.0 - sum(speeds)
    out = np.stack([(rows * s) @ shakhov.T for s in [stay] + speeds])
    out[np.abs(out) < 1e-13] = 0.0
    return out


def split(value):
    high = value.astype(jnp.bfloat16)
    low = (value - high.astype(jnp.float32)).astype(jnp.bfloat16)
    return high, low


def speeds_at(index):
    speed = speed_range * (2.0 * index.astype(jnp.float32) + 1.0 - NVX) / NVX
    return [time_step * speed[a : a + 1] for a in range(3)]


class Upwind:
    def __init__(self, index):
        tx, ty, tz = speeds_at(index)
        shape = (NZ, LANES)
        self.ax, self.ay, self.az = (jnp.broadcast_to(jnp.abs(t), shape) for t in (tx, ty, tz))
        self.stay = 1.0 - self.ax - self.ay - self.az
        self.px, self.py, self.pz = (jnp.broadcast_to(t, shape) > 0 for t in (tx, ty, tz))

    def across(self, read, y, count):
        here = read(y)
        in_y = jnp.where(self.py, read(lax.rem(y + count - 1, count)), read(lax.rem(y + 1, count)))
        in_z = jnp.where(self.pz, pltpu.roll(here, 1, axis=0), pltpu.roll(here, NZ - 1, axis=0))
        return self.stay * here + self.ay * in_y + self.az * in_z

    def stream(self, ref, x, y, count):
        mid = self.across(lambda j: ref[x + 1, rows_of(j), :], y, count)
        return mid + self.ax * jnp.where(self.px, ref[x, rows_of(y), :], ref[x + 2, rows_of(y), :])


def rows_of(y):
    return pl.ds(pl.multiple_of(y * NZ, NZ), NZ)


def each_y(count, body, step=16):
    @pl.loop(0, count // step)
    def _(i):
        for j in range(step):
            body(i * step + j)


def lane_copies(ref_row, target, blocks):
    for k in range(blocks):
        at = slice(k * LANES, (k + 1) * LANES)
        target[at, :] = jnp.broadcast_to(ref_row[:, at], (LANES, LANES)).T


def roll_y(value, sign):
    cells = value.shape[1]
    return pltpu.roll(value, NZ if sign > 0 else cells - NZ, axis=1)


def roll_z(value, sign):
    cells = value.shape[1]
    zl = lax.broadcasted_iota(jnp.int32, value.shape, 1) & (NZ - 1)
    if sign > 0:
        return jnp.where(zl == 0, pltpu.roll(value, cells - (NZ - 1), axis=1), pltpu.roll(value, 1, axis=1))
    return jnp.where(zl == NZ - 1, pltpu.roll(value, NZ - 1, axis=1), pltpu.roll(value, cells - 1, axis=1))


def outflow_kernel(dist_ref, dtc_ref, out_ref, *, count, blocks):
    px = dtc_ref[...] > 0
    stride = blocks * SUB
    for k in range(blocks):
        at = slice(k * LANES, (k + 1) * LANES)
        plane = [dist_ref[pl.ds(k * SUB + x, count, stride=stride), :] for x in (0, 1, SUB - 2, SUB - 1)]
        out_ref[0, :, at] = jnp.where(px, plane[3], plane[0])
        out_ref[1, :, at] = jnp.where(px, plane[2], plane[1])


def outflow(flat, dtc, vels, blocks):
    count = min(64, vels)
    rows = count * blocks * SUB
    cells = blocks * LANES
    return pl.pallas_call(
        functools.partial(outflow_kernel, count=count, blocks=blocks),
        grid=(vels // count,),
        in_specs=[
            pl.BlockSpec((rows, LANES), lambda i: (i, 0)),
            pl.BlockSpec((count, LANES), lambda i: (i, 0)),
        ],
        out_specs=pl.BlockSpec((2, count, cells), lambda i: (0, i, 0)),
        out_shape=jax.ShapeDtypeStruct((2, vels, cells), jnp.float32),
        compiler_params=pltpu.CompilerParams(vmem_limit_bytes=54 * MIB),
        cost_estimate=pl.CostEstimate(flops=0, bytes_accessed=20 * vels * blocks * SUB * LANES // 4, transcendentals=0),
        name="outflow_planes",
    )(flat, dtc)


def moments_kernel(me_ref, dist_ref, index_ref, cst_ref, high_ref, low_ref, *refs, vels, blocks):
    half = blocks // 2
    outs = refs[:half]
    held, turned, rhi, rlo, table, wst, acc, gacc, pay, sems, out_sems = refs[half:]
    stride = blocks * SUB
    chunks = vels // LANES
    part = LANES * stride
    span = SETS * 16
    ys = blocks * LANES // NZ

    piece = part // PIECES

    def fetch(c):
        return [
            pltpu.make_async_copy(
                dist_ref.at[pl.ds(c * part + p * piece, piece)],
                held.at[c % 2, pl.ds(p * piece, piece)],
                sems.at[c % 2, p],
            )
            for p in range(PIECES)
        ]

    for c in range(min(2, chunks)):
        for copy in fetch(c):
            copy.start()

    speed = [speed_range * (2.0 * index_ref[a : a + 1, :].astype(jnp.float32) + 1.0 - NVX) / NVX for a in range(3)]
    rows, _, square = functions_of(*speed)
    weight = (2.0 * speed_range / NVX) ** 3 * math.pi ** (-1.5) * jnp.exp(-square)
    table[...] = jnp.zeros_like(table)
    for m, row in enumerate(rows):
        table[m : m + 1, :] = row * weight
    base = table[...]
    speeds = []
    for c in speed:
        speeds.append(jnp.where(c > 0, time_step * c, 0.0))
        speeds.append(jnp.where(c < 0, -time_step * c, 0.0))
    full = jnp.concatenate([base] + [base * s for s in speeds] + [jnp.zeros_like(base)], axis=0)
    for variant, factor in enumerate([None, speeds[0], speeds[1]]):
        high, low = split((full if factor is None else full * factor).T)
        wst[variant, :, 0:LANES] = high
        wst[variant, :, LANES:] = low

    empty = jnp.zeros((ys * NZ, LANES), jnp.float32)
    turned[0] = empty
    turned[SUB + 1] = empty
    for c in range(chunks):
        for copy in fetch(c):
            copy.wait()
        lanes = slice(c * LANES, (c + 1) * LANES)

        @pl.loop(0, blocks)
        def _(k, c=c):
            for x in range(SUB):
                value = held[c % 2, pl.ds(k * SUB + x, LANES, stride=stride), :]
                turned[x + 1, pl.ds(pl.multiple_of(k * LANES, LANES), LANES), :] = value.T

        if c + 2 < chunks:
            for copy in fetch(c + 2):
                copy.start()
        upwind = Upwind(index_ref[:, lanes])

        @pl.loop(0, SUB)
        def _(x, upwind=upwind, lanes=lanes):
            def one(y):
                high, low = split(upwind.stream(turned, x, y, ys))
                rhi[x, rows_of(y), lanes] = high
                rlo[x, rows_of(y), lanes] = low

            each_y(ys, one)

        def edges(y, lanes=lanes):
            for slot, x in ((SUB, SUB - 1), (SUB + 1, 0)):
                high, low = split(turned[x + 1, rows_of(y), :])
                rhi[slot, rows_of(y), lanes] = high
                rlo[slot, rows_of(y), lanes] = low

        each_y(ys, edges)

    away = [
        pltpu.make_async_copy(rhi.at[pl.ds(0, SUB)], high_ref, out_sems.at[0]),
        pltpu.make_async_copy(rlo.at[pl.ds(0, SUB)], low_ref, out_sems.at[1]),
    ]
    for copy in away:
        copy.start()
    wide = 2 * LANES

    @pl.loop(0, blocks // 2)
    def _(b):
        at = pl.ds(pl.multiple_of(b * wide, wide), wide)
        for slot in range(SUB + 2):
            variant = max(0, slot - SUB + 1)
            first = jnp.dot(rhi[slot, at, :], wst[variant], preferred_element_type=jnp.float32)
            second = jnp.dot(rlo[slot, at, :], wst[variant, :, 0:LANES], preferred_element_type=jnp.float32)
            total = (first[:, 0:LANES] + first[:, LANES:] + second).T[0:span]
            if slot < SUB:
                for j in range(2):
                    acc[2 * b + j, pl.ds(slot, span, stride=SUB), :] = total[:, j * LANES : (j + 1) * LANES]
            else:
                gacc[slot - SUB, :, at] = total

    al = cst_ref[0, 0:SUB, :]
    beyond = cst_ref[0, SUB : SUB + 1, :]
    below = cst_ref[0, 2 * SUB - 1 : 2 * SUB, :]
    plane = lax.broadcasted_iota(jnp.int32, al.shape, 0)

    def own(i, m):
        first = (i * 16 + m) * SUB
        return jnp.concatenate([acc[k, first : first + SUB, :] for k in range(blocks)], axis=1)

    for m in range(MOM):
        sets = [own(i, m) for i in range(SETS)]
        value = al * (sets[0] - sum(sets[1:]))
        value = value + jnp.where(plane == 0, 0.0, pltpu.roll(al * sets[1], 1, axis=0))
        value = value + jnp.where(plane == SUB - 1, 0.0, pltpu.roll(al * sets[2], SUB - 1, axis=0))
        value = value + roll_y(al * sets[3], 1) + roll_y(al * sets[4], -1)
        value = value + roll_z(al * sets[5], 1) + roll_z(al * sets[6], -1)
        for k in range(blocks):
            at = slice(k * LANES, (k + 1) * LANES)
            pay[k, M1 + m * SUB : M1 + (m + 1) * SUB, :] = sets[0][:, at]
            pay[k, AA + m * SUB : AA + (m + 1) * SUB, :] = value[:, at]

    for side, (scale, edge, toward, start) in enumerate([(beyond, SUB - 1, 1, UP), (below, 0, 2, DOWN)]):
        sets = [gacc[side, i * 16 : (i + 1) * 16, :] for i in range(SETS)]
        near = scale * (sets[0] - sum(sets[1:]))
        near = near + roll_y(scale * sets[3], 1) + roll_y(scale * sets[4], -1)
        near = near + roll_z(scale * sets[5], 1) + roll_z(scale * sets[6], -1)
        out_of = jnp.concatenate(
            [acc[k, pl.ds(toward * 16 * SUB + edge, 16, stride=SUB), :] for k in range(blocks)], axis=1
        )
        near = near + al[edge : edge + 1, :] * out_of
        far = scale * sets[toward]
        for k in range(blocks):
            at = slice(k * LANES, (k + 1) * LANES)
            for j, value in enumerate((sets[0], near, far)):
                pay[k, start + j * MOM : start + (j + 1) * MOM, :] = value[0:MOM, at]
            pay[k, start + 3 * MOM : start + 3 * MOM + 1, :] = jnp.zeros((1, LANES), jnp.float32)

    mine = me_ref[0]
    for k in range(half):
        near = jnp.bitwise_xor(mine, k)
        outs[k][0:PAY, :] = pay[near]
        outs[k][PAY:, :] = pay[jnp.bitwise_xor(near, half)]
    for copy in away:
        copy.wait()


def both_moments(place, flat, vel_index, cst, vels, blocks):
    cells = blocks * LANES
    vmem = pl.BlockSpec(memory_space=pltpu.VMEM)
    span = SETS * 16
    anywhere = pl.BlockSpec(memory_space=pl.ANY)
    streamed = jax.ShapeDtypeStruct((SUB, cells, vels), jnp.bfloat16)
    return pl.pallas_call(
        functools.partial(moments_kernel, vels=vels, blocks=blocks),
        in_specs=[pl.BlockSpec(memory_space=pltpu.SMEM), anywhere, vmem, vmem],
        out_specs=[anywhere, anywhere] + [vmem] * (blocks // 2),
        out_shape=[streamed, streamed] + [jax.ShapeDtypeStruct((2 * PAY, LANES), jnp.float32)] * (blocks // 2),
        scratch_shapes=[
            pltpu.VMEM((2, LANES * blocks * SUB, LANES), jnp.float32),
            pltpu.VMEM((SUB + 2, cells, LANES), jnp.float32),
            pltpu.VMEM((SUB + 2, cells, vels), jnp.bfloat16),
            pltpu.VMEM((SUB + 2, cells, vels), jnp.bfloat16),
            pltpu.VMEM((16, vels), jnp.float32),
            pltpu.VMEM((3, vels, 2 * LANES), jnp.bfloat16),
            pltpu.VMEM((blocks, span * SUB, LANES), jnp.float32),
            pltpu.VMEM((2, span, cells), jnp.float32),
            pltpu.VMEM((blocks, PAY, LANES), jnp.float32),
            pltpu.SemaphoreType.DMA((2, PIECES)),
            pltpu.SemaphoreType.DMA((2,)),
        ],
        compiler_params=pltpu.CompilerParams(vmem_limit_bytes=54 * MIB),
        cost_estimate=pl.CostEstimate(
            flops=2 * 336 * vels * 10 * cells, bytes_accessed=8 * vels * SUB * cells, transcendentals=0
        ),
        name="moments_of_both",
    )(place, flat, vel_index, cst)


def carried_kernel(high_ref, low_ref, index_ref, al_ref, out_ref, mid, scale, *, blocks):
    ys = blocks * LANES // NZ

    @pl.when(pl.program_id(0) == 0)
    def _():
        for x in range(SUB):
            lane_copies(al_ref[x : x + 1, :], scale.at[x], blocks)
        empty = jnp.zeros((ys * NZ, LANES), jnp.float32)
        mid[0] = empty
        mid[SUB + 1] = empty

    upwind = Upwind(index_ref[...])

    @pl.loop(0, SUB)
    def _(x):
        def one(y):
            at = rows_of(y)
            value = high_ref[x, at, :].astype(jnp.float32) + low_ref[x, at, :].astype(jnp.float32)
            mid[x + 1, at, :] = scale[x, at, :] * value

        each_y(ys, one)

    @pl.loop(0, SUB)
    def _(x):
        def one(y):
            out_ref[x, rows_of(y), :] = scale[x, rows_of(y), :] * upwind.stream(mid, x, y, ys)

        each_y(ys, one)


def carried(high, low, vel_index, al, first, count, blocks):
    cells = blocks * LANES
    start = first // LANES
    block = pl.BlockSpec((SUB, cells, LANES), lambda i: (0, 0, i + start))
    return pl.pallas_call(
        functools.partial(carried_kernel, blocks=blocks),
        grid=(count // LANES,),
        in_specs=[
            block,
            block,
            pl.BlockSpec((3, LANES), lambda i: (0, i + start)),
            pl.BlockSpec((SUB, cells), lambda i: (0, 0)),
        ],
        out_specs=pl.BlockSpec((SUB, cells, LANES), lambda i: (0, 0, i)),
        out_shape=jax.ShapeDtypeStruct((SUB, cells, count), jnp.float32),
        scratch_shapes=[
            pltpu.VMEM((SUB + 2, cells, LANES), jnp.float32),
            pltpu.VMEM((SUB, cells, LANES), jnp.float32),
        ],
        compiler_params=pltpu.CompilerParams(vmem_limit_bytes=56 * MIB),
        cost_estimate=pl.CostEstimate(
            flops=40 * count * cells * SUB, bytes_accessed=8 * count * cells * SUB, transcendentals=0
        ),
        name="carried_part",
    )(high, low, vel_index, al)


def inflow_kernel(
    core_ref, swap_ref, first_ref, second_ref, sign_ref, index_ref, al_ref, out_ref, halo, edge, scale, *, blocks, half
):
    core = core_ref[0]
    ys = blocks * LANES // NZ

    @pl.when(pl.program_id(0) == 0)
    def _():
        for j, x in enumerate((0, SUB - 1, 1, SUB - 2, 2 * SUB - 1, SUB)):
            lane_copies(al_ref[x : x + 1, :], scale.at[j], blocks)

    from_far = (sign_ref[...] > 0) == (core == 0)
    if half >= LANES:
        mine = (pl.program_id(0) // (half // LANES)) == core
    for depth in range(2):
        for k in range(blocks):
            at = slice(k * LANES, (k + 1) * LANES)
            one, two = first_ref[depth, :, at], second_ref[depth, :, at]
            if half >= LANES:
                far = jnp.where(mine, one, two)
            else:
                far = jnp.where(core == 0, jnp.concatenate([one, two], axis=0), jnp.concatenate([two, one], axis=0))
            halo[depth, at, :] = jnp.where(from_far, far, swap_ref[depth, :, at]).T

    upwind = Upwind(index_ref[...])

    def scaled(pair, at):
        return jnp.where(upwind.px, scale[2 * pair, at, :], scale[2 * pair + 1, at, :])

    def start(y):
        at = rows_of(y)
        value = scaled(0, at) * upwind.ax * halo[0, at, :]
        edge[at, :] = value
        out_ref[1, at, :] = scaled(1, at) * upwind.ax * value

    each_y(ys, start)

    def finish_one(y):
        at = rows_of(y)
        inside = upwind.across(lambda j: edge[rows_of(j), :], y, ys)
        beyond = upwind.across(lambda j: halo[0, rows_of(j), :], y, ys) + upwind.ax * halo[1, at, :]
        out_ref[0, at, :] = scaled(0, at) * (inside + upwind.ax * scaled(2, at) * beyond)

    each_y(ys, finish_one)


def inflow(core, swap, first, second, sign, vel_index, al16, vels, blocks):
    half = first.shape[1]
    cells = blocks * LANES
    count = min(LANES, half)
    narrow = pl.BlockSpec((2, count, cells), lambda i: (0, i % (half // count), 0))
    return pl.pallas_call(
        functools.partial(inflow_kernel, blocks=blocks, half=half),
        grid=(vels // LANES,),
        in_specs=[
            pl.BlockSpec(memory_space=pltpu.SMEM),
            pl.BlockSpec((2, LANES, cells), lambda i: (0, i, 0)),
            narrow,
            narrow,
            pl.BlockSpec((LANES, LANES), lambda i: (i, 0)),
            pl.BlockSpec((3, LANES), lambda i: (0, i)),
            pl.BlockSpec((2 * SUB, cells), lambda i: (0, 0)),
        ],
        out_specs=pl.BlockSpec((2, cells, LANES), lambda i: (0, 0, i)),
        out_shape=jax.ShapeDtypeStruct((2, cells, vels), jnp.float32),
        scratch_shapes=[
            pltpu.VMEM((2, cells, LANES), jnp.float32),
            pltpu.VMEM((cells, LANES), jnp.float32),
            pltpu.VMEM((6, cells, LANES), jnp.float32),
        ],
        compiler_params=pltpu.CompilerParams(vmem_limit_bytes=24 * MIB),
        cost_estimate=pl.CostEstimate(flops=60 * vels * cells, bytes_accessed=24 * vels * cells, transcendentals=0),
        name="inflow_part",
    )(core, swap, first, second, sign, vel_index, al16)


def small_call(kernel, outs, name, specs, args, scratch=(), limit=16):
    vmem = pl.BlockSpec(memory_space=pltpu.VMEM)
    smem = pl.BlockSpec(memory_space=pltpu.SMEM)
    return pl.pallas_call(
        kernel,
        in_specs=[smem if s == "s" else vmem for s in specs],
        out_specs=[vmem] * len(outs),
        out_shape=[jax.ShapeDtypeStruct(o, jnp.float32) for o in outs],
        scratch_shapes=list(scratch),
        compiler_params=pltpu.CompilerParams(vmem_limit_bytes=limit * MIB),
        name=name,
    )(*args)


def pair_kernel(*refs):
    parts, (near_ref, far_ref) = refs[:-2], refs[-2:]
    value = parts[0][...]
    for part in parts[1:]:
        value = value + part[...]
    near_ref[...] = value[0:PAY]
    far_ref[...] = value[PAY:]


def total_kernel(*refs):
    parts, (all_ref, up_ref, down_ref) = refs[:-3], refs[-3:]
    value = parts[0][...]
    for part in parts[1:]:
        value = value + part[...]
    all_ref[...] = value
    up_ref[...] = value[UP:DOWN]
    down_ref[...] = value[M1:AA]


def mix(inverse, values):
    return [sum(inverse[k, j] * values[j] for j in range(MOM)) for k in range(MOM)]


def chunk_kernel(inv_ref, own_ref, low_ref, high_ref, send_ref):
    plane = lax.broadcasted_iota(jnp.int32, (SUB, LANES), 0)
    inverse = {(k, j): inv_ref[k, j] for k in range(MOM) for j in range(MOM)}
    inner, outer, later = [], [], []
    for m in range(MOM):

        def row(ref, at):
            return ref[at : at + 1, :]

        first = own_ref[M1 + m * SUB : M1 + (m + 1) * SUB, :]
        second = own_ref[AA + m * SUB : AA + (m + 1) * SUB, :]
        low = low_ref[M1 + m * SUB : M1 + (m + 1) * SUB, :]
        high = high_ref[m * SUB : (m + 1) * SUB, :]
        below = DOWN - M1 + m
        inner.append(
            first + jnp.where(plane == 0, row(low_ref, m), 0.0) + jnp.where(plane == SUB - 1, row(high_ref, below), 0.0)
        )
        outer.append(
            jnp.where(plane < SUB // 2, high, low)
            + jnp.where(plane == 0, row(own_ref, UP + m), 0.0)
            + jnp.where(plane == SUB - 1, row(own_ref, DOWN + m), 0.0)
        )
        later.append(
            second
            + jnp.where(plane == 0, row(low_ref, MOM + m), 0.0)
            + jnp.where(plane == 1, row(low_ref, 2 * MOM + m), 0.0)
            + jnp.where(plane == SUB - 1, row(high_ref, below + MOM), 0.0)
            + jnp.where(plane == SUB - 2, row(high_ref, below + 2 * MOM), 0.0)
        )
    local, around = mix(inverse, inner), mix(inverse, outer)
    for n in range(4):
        send_ref[n * 16 : n * 16 + SUB, :] = local[n + 1]
        send_ref[n * 16 + SUB : (n + 1) * 16, :] = around[n + 1]
        send_ref[MOVED + n * SUB : MOVED + (n + 1) * SUB, :] = inner[n + 1]
    for n, k in enumerate(STILL):
        send_ref[FIXED + n * SUB : FIXED + (n + 1) * SUB, :] = local[k]
        send_ref[EDGE + n : EDGE + n + 1, :] = around[k][0:1]
        send_ref[EDGE + 4 + n : EDGE + 5 + n, :] = around[k][SUB - 1 :]
    for m in range(MOM):
        send_ref[LATER + m * SUB : LATER + (m + 1) * SUB, :] = later[m]
    send_ref[SQUARE:SENT, :] = sum((local[m] - inner[m]) ** 2 for m in range(MOM) if not 1 <= m <= 4)


def sweeps(source):
    rows = source.shape[0]
    field = source
    for _ in range(SWEEPS):
        beside = pltpu.roll(field, 1, axis=0) + pltpu.roll(field, rows - 1, axis=0)
        beside = beside + roll_y(field, 1) + roll_y(field, -1) + roll_z(field, 1) + roll_z(field, -1)
        field = (source + coupling * beside) * (1.0 / (1.0 + 6.0 * coupling))
    return field


def fields_kernel(place_ref, inv_ref, cst_ref, *refs, blocks):
    parts = refs[:blocks]
    h1_ref, later_ref, next_ref, up_ref, down_ref, norm_ref, whole = refs[blocks:]
    mine = place_ref[0]
    for k in range(blocks):
        whole[jnp.bitwise_xor(mine, k)] = parts[k][...]

    def rows(first, count):
        return jnp.concatenate([whole[k, first : first + count, :] for k in range(blocks)], axis=1)

    def fold(value):
        return sum(value[:, k * LANES : (k + 1) * LANES] for k in range(blocks))

    square = sum(whole[k, SQUARE:SENT, :] for k in range(blocks))
    al = cst_ref[0, 0:SUB, :]
    edges = rows(EDGE, SUB)
    plane = lax.broadcasted_iota(jnp.int32, al.shape, 0)
    moved = []
    for n, m in enumerate(PICK):
        if 1 <= m <= 4:
            value = sweeps(rows((m - 1) * 16, 16))
            square = square + fold((value[0:SUB] - rows(MOVED + (m - 1) * SUB, SUB)) ** 2)
        else:
            k = STILL.index(m)
            around = jnp.where(
                plane == 0, edges[k : k + 1], jnp.where(plane == SUB - 1, edges[4 + k : 5 + k], 0.0)
            )
            value = jnp.concatenate([rows(FIXED + k * SUB, SUB), around], axis=0)
        given = cst_ref[1 if n in (0, 4) else 2] * value
        inside = given[0:SUB]
        shifted = [
            inside,
            pltpu.roll(given, 1, axis=0)[0:SUB],
            pltpu.roll(given, 2 * SUB - 1, axis=0)[0:SUB],
            roll_y(inside, 1),
            roll_y(inside, -1),
            roll_z(inside, 1),
            roll_z(inside, -1),
        ]
        for s in range(SETS):
            value = al * shifted[s]
            for k in range(blocks):
                first = (s * 8 + n) * SUB
                h1_ref[k, first : first + SUB, :] = value[:, k * LANES : (k + 1) * LANES]
        moved.append(shifted)
    norm_ref[...] = square

    matrices = stream_matrices()
    moments = []
    for m in range(MOM):
        value = rows(LATER + m * SUB, SUB)
        for s in range(SETS):
            for n in range(8):
                factor = float(matrices[s, m, n])
                if factor != 0.0:
                    value = value + factor * moved[n][s]
        later_ref[m * SUB : (m + 1) * SUB, :] = value
        moments.append(value)
    inverse = {(k, j): inv_ref[k, j] for k in range(MOM) for j in range(MOM)}
    for m, value in enumerate(mix(inverse, moments)):
        next_ref[m * SUB : (m + 1) * SUB, :] = value
        if 1 <= m <= 4:
            up_ref[(m - 1) * 4 : m * 4, :] = value[SUB // 2 :]
            down_ref[(m - 1) * 4 : m * 4, :] = value[: SUB // 2]


def last_kernel(place_ref, cst_ref, later_ref, next_ref, low_ref, high_ref, h2_ref, out_ref, norm_ref, wide, *, blocks):
    mine = place_ref[0]
    square = jnp.zeros((SUB, LANES), jnp.float32)
    for m in range(MOM):
        value = next_ref[m * SUB : (m + 1) * SUB, :]
        if 1 <= m <= 4:
            at = slice((m - 1) * 4, m * 4)
            value = sweeps(jnp.concatenate([value, high_ref[at, :], low_ref[at, :]], axis=0))[0:SUB]
        off = (value - later_ref[m * SUB : (m + 1) * SUB, :]) ** 2
        for k in range(blocks):
            wide[m, k] = value[:, k * LANES : (k + 1) * LANES]
            square = square + off[:, k * LANES : (k + 1) * LANES]
        out_ref[m] = wide[m, mine]
        if m in PICK:
            n = PICK.index(m)
            given = cst_ref[1 if n in (0, 4) else 2, 0:SUB, :] * value
            for k in range(blocks):
                h2_ref[k, n * SUB : (n + 1) * SUB, :] = given[:, k * LANES : (k + 1) * LANES]
    norm_ref[...] = square


def finish_kernel(*refs, vels, parts):
    carried_refs = refs[:parts]
    inflow_ref, h1_ref, h2_ref, index_ref, out_ref, rows, table = refs[parts:]

    @pl.when(pl.program_id(0) == 0)
    def _():
        speed = [speed_range * (2.0 * index_ref[a : a + 1, :].astype(jnp.float32) + 1.0 - NVX) / NVX for a in range(3)]
        for n, row in enumerate(functions_of(*speed)[1]):
            table[n : n + 1, :] = row
        base = table[...]
        speeds = []
        for c in speed:
            speeds.append(jnp.where(c > 0, time_step * c, 0.0))
            speeds.append(jnp.where(c < 0, -time_step * c, 0.0))
        full = jnp.concatenate([base * (1.0 - sum(speeds))] + [base * s for s in speeds] + [base], axis=0)
        high = full.astype(jnp.bfloat16).astype(jnp.float32)
        stacked = jnp.concatenate([high, high, full - high, jnp.zeros_like(full)], axis=0)
        rows[...] = stacked.T.astype(jnp.bfloat16)

    out = out_ref.reshape(vels * SUB, LANES)
    px = index_ref[0:1, :] * 2 >= NVX
    for x in range(0, SUB, 2):
        field = jnp.concatenate(
            [
                jnp.concatenate(
                    [h1_ref[0, pl.ds(x + j, SETS * 8, stride=SUB), :], h2_ref[0, pl.ds(x + j, 8, stride=SUB), :]], axis=0
                )
                for j in range(2)
            ],
            axis=1,
        )
        high, low = split(field)
        term = jnp.dot(
            rows[...],
            jnp.concatenate([high, low, high, jnp.zeros_like(high)], axis=0),
            preferred_element_type=jnp.float32,
        )
        for j in range(2):
            value = jnp.concatenate([ref[x + j] for ref in carried_refs], axis=1)
            if x + j in (0, 1):
                value = value + jnp.where(px, inflow_ref[x + j], 0.0)
            elif x + j in (SUB - 2, SUB - 1):
                value = value + jnp.where(px, 0.0, inflow_ref[SUB - 1 - x - j])
            out[pl.ds(x + j, vels, stride=SUB), :] = value.T + term[:, j * LANES : (j + 1) * LANES]


def finish(carried_parts, inflow_part, h1, h2, vel_index, vels, blocks):
    return pl.pallas_call(
        functools.partial(finish_kernel, vels=vels, parts=len(carried_parts)),
        grid=(blocks,),
        in_specs=[pl.BlockSpec((SUB, LANES, part.shape[2]), lambda k: (0, k, 0)) for part in carried_parts]
        + [
            pl.BlockSpec((2, LANES, vels), lambda k: (0, k, 0)),
            pl.BlockSpec((1, SETS * 8 * SUB, LANES), lambda k: (k, 0, 0)),
            pl.BlockSpec((1, 8 * SUB, LANES), lambda k: (k, 0, 0)),
            pl.BlockSpec((3, vels), lambda k: (0, 0)),
        ],
        out_specs=pl.BlockSpec((vels, 1, SUB, LANES), lambda k: (0, k, 0, 0)),
        out_shape=jax.ShapeDtypeStruct((vels, blocks, SUB, LANES), jnp.float32),
        scratch_shapes=[pltpu.VMEM((vels, 256), jnp.bfloat16), pltpu.VMEM((8, vels), jnp.float32)],
        compiler_params=pltpu.CompilerParams(vmem_limit_bytes=54 * MIB),
        cost_estimate=pl.CostEstimate(
            flops=2 * 256 * vels * blocks * SUB * LANES, bytes_accessed=8 * vels * blocks * SUB * LANES, transcendentals=0
        ),
        name="finish_dist",
    )(*carried_parts, inflow_part, h1, h2, vel_index)


def ring(axis, step):
    size = lax.axis_size(axis)
    return [(i, (i + step) % size) for i in range(size)]


def shards(dist, vel_index, relax, wall_mask, macro_inverse):
    vels, width, cells = dist.shape
    blocks = cells // LANES
    peers, slabs = lax.axis_size("vel"), lax.axis_size("space")
    assert width == SUB and peers % blocks == 0 and slabs == 4 and blocks % 2 == 0
    sub = peers // blocks
    me = lax.axis_index("vel")
    place = (me // sub).astype(jnp.int32).reshape(1)
    core = (lax.axis_index("space") % 2).astype(jnp.int32).reshape(1)

    flat = dist.reshape(vels, width, blocks, LANES).transpose(0, 2, 1, 3).reshape(vels * blocks * width, LANES)
    speed = speed_range * (2.0 * vel_index.astype(jnp.float32) + 1.0 - NVX) / NVX
    sign = jnp.broadcast_to(speed[0][:, None], (vels, LANES))

    wall = wall_mask > 0
    coefficients = jnp.stack(
        [
            jnp.where(wall, 0.0, 1.0 - relax),
            jnp.where(wall, 1.0, relax),
            jnp.where(wall, 0.0, relax),
        ],
        0,
    )
    from_low = lax.ppermute(coefficients[:, SUB - 1 :], "space", ring("space", 1))
    from_high = lax.ppermute(coefficients[:, :1], "space", ring("space", -1))

    leaving = outflow(flat, sign, vels, blocks)
    swap = lax.ppermute(leaving, "space", [(i, i ^ 1) for i in range(slabs)])
    cst = jnp.concatenate(
        [coefficients, from_high, jnp.zeros((3, SUB - 2, cells), jnp.float32), from_low], 1
    )

    (cst, leaving) = lax.optimization_barrier((cst, leaving))
    high_part, low_part, *parts = both_moments(place, flat, vel_index, cst, vels, blocks)
    (swap, parts) = lax.optimization_barrier((swap, parts))

    half = vels // 2
    start = core[0] * half
    mine = lax.dynamic_slice_in_dim(leaving, start, half, 1)
    other = lax.dynamic_slice_in_dim(swap, start, half, 1)
    plus = lax.dynamic_slice_in_dim(speed[0], start, half, 0) > 0
    across = jnp.where((plus == (core[0] == 1))[None, :, None], mine, other)
    (across, parts) = lax.optimization_barrier((across, parts))
    first = lax.ppermute(across, "space", [(i, i ^ 2) for i in range(slabs)])

    def beside(step):
        return [(i, (i // sub ^ step) * sub + i % sub) for i in range(peers)]

    spans = [(0, vels)] if vels < 2 * LANES else [(0, vels // 2), (vels // 2, vels - vels // 2)]

    def carry(span):
        return carried(high_part, low_part, vel_index, coefficients[0], span[0], span[1], blocks)

    got = [parts[0]] + [lax.ppermute(parts[k], "vel", beside(k)) for k in range(1, blocks // 2)]
    carried_parts = [carry(spans[0])]
    (got[1], carried_parts[0]) = lax.optimization_barrier((got[1], carried_parts[0]))
    near, far = small_call(pair_kernel, [(PAY, LANES)] * 2, "sum_near", "v" * len(got), got)
    got = [near, lax.ppermute(far, "vel", beside(blocks // 2))]
    if len(spans) > 1:
        (al, _) = lax.optimization_barrier((coefficients[0], near))
        carried_parts.append(carried(high_part, low_part, vel_index, al, *spans[1], blocks))
        (got[1], carried_parts[1]) = lax.optimization_barrier((got[1], carried_parts[1]))
    if sub > 1:
        part = sum(got)
        got = [part]
        for k in range(1, sub):
            pairs = [(i, i // sub * sub + (i % sub + k) % sub) for i in range(peers)]
            got.append(lax.ppermute(part, "vel", pairs))
    chunk, up, down = small_call(
        total_kernel, [(PAY, LANES), (DOWN - UP, LANES), (AA - M1, LANES)], "sum_moments", "v" * len(got), got
    )
    low = lax.ppermute(up, "space", ring("space", 1))
    high = lax.ppermute(down, "space", ring("space", -1))
    (send,) = small_call(
        chunk_kernel, [(SENT, LANES)], "local_fields", "svvv", (macro_inverse, chunk, low, high)
    )
    pieces = [send] + [lax.ppermute(send, "vel", beside(k)) for k in range(1, blocks // 2 + 1)]
    (first, send) = lax.optimization_barrier((first, send))
    second = lax.ppermute(first, "space", [(i, i ^ 1) for i in range(slabs)])
    pieces += [lax.ppermute(pieces[blocks // 2], "vel", beside(k)) for k in range(1, blocks // 2)]
    inflow_part = inflow(core, swap, first, second, sign, vel_index, cst[0], vels, blocks)
    (pieces[-1], inflow_part) = lax.optimization_barrier((pieces[-1], inflow_part))

    h1, later, following, up2, down2, norm1 = small_call(
        functools.partial(fields_kernel, blocks=blocks),
        [
            (blocks, SETS * 8 * SUB, LANES),
            (MOM * SUB, cells),
            (MOM * SUB, cells),
            (16, cells),
            (16, cells),
            (SUB, LANES),
        ],
        "first_fields",
        "ssv" + "v" * blocks,
        (place, macro_inverse, cst, *pieces),
        [pltpu.VMEM((blocks, SENT, LANES), jnp.float32)],
        16,
    )
    low2 = lax.ppermute(up2, "space", ring("space", 1))
    high2 = lax.ppermute(down2, "space", ring("space", -1))
    h2, owned, norm2 = small_call(
        functools.partial(last_kernel, blocks=blocks),
        [(blocks, 8 * SUB, LANES), (MOM, SUB, LANES), (SUB, LANES)],
        "last_fields",
        "svvvvv",
        (place, cst, later, following, low2, high2),
        [pltpu.VMEM((MOM, blocks, SUB, LANES), jnp.float32)],
        16,
    )

    squares = jnp.stack([jnp.sum(norm1), jnp.sum(norm2)])
    around = [lax.ppermute(squares, "space", ring("space", k)) for k in range(1, slabs)]
    if sub > 1:
        owned = lax.dynamic_slice_in_dim(owned, (me % sub) * (LANES // sub), LANES // sub, 2)

    out = finish(carried_parts, inflow_part, h1, h2, vel_index, vels, blocks)
    (around[0], out) = lax.optimization_barrier((around[0], out))
    slab = lax.axis_index("space")
    every = jnp.stack([squares] + around)
    norms = jnp.sqrt(jnp.sum(jnp.roll(every[::-1], slab + 1, axis=0), axis=0))
    out = out.transpose(0, 2, 1, 3).reshape(vels, width, cells)
    return (out, owned, norms)


def solution(mesh):
    return jax.shard_map(
        shards,
        mesh=mesh,
        in_specs=(P("vel", "space", None), P(None, "vel"), P("space", None), P("space", None), P()),
        out_specs=(P("vel", "space", None), P(None, "space", "vel"), P()),
        check_vma=False,
    )
```

```python
import functools
import math

import jax
import jax.numpy as jnp
import numpy as np
from jax import lax
from jax.experimental import pallas as pl
from jax.experimental.pallas import tpu as pltpu
from jax.sharding import PartitionSpec as P

NVX = 16
NZ = 16
MOM = 13
SWEEPS = 3
LANES = 128
SUB = 8
SETS = 7
PICK = (0, 1, 2, 3, 4, 10, 11, 12)

speed_range = 4.0
time_step = 0.08
coupling = 0.5
MIB = 2**20
PIECES = 8
RUN = 16

UP, M1, DOWN, AA, PAY = 0, 40, 144, 184, 288
STILL = (0, 10, 11, 12)
MOVED, FIXED, EDGE, LATER, SQUARE, SENT = 64, 96, 128, 136, 240, 248


def functions_of(cx, cy, cz):
    square = cx * cx + cy * cy + cz * cz
    heat = square - 2.5
    one = cx * 0.0 + 1.0
    rows = [
        one, cx, cy, cz, 2.0 * square / 3.0 - 1.0, 2.0 * cx * cy, 2.0 * cx * cz, 2.0 * cy * cz,
        cx * cx - cy * cy, cy * cy - cz * cz, cx * heat, cy * heat, cz * heat,
    ]
    factor = 4.0 / 15.0
    shakhov = [
        one, 2.0 * cx, 2.0 * cy, 2.0 * cz, square - 1.5,
        factor * cx * heat, factor * cy * heat, factor * cz * heat,
    ]
    return rows, shakhov, square


def half_speeds(cx, cy, cz):
    out = []
    for c in (cx, cy, cz):
        out.append(time_step * c * (c > 0))
        out.append(-time_step * c * (c < 0))
    return out


@functools.lru_cache(None)
def stream_matrices():
    line = speed_range * (2.0 * np.arange(NVX) + 1.0 - NVX) / NVX
    cx, cy, cz = (g.reshape(-1) for g in np.meshgrid(line, line, line, indexing="ij"))
    rows, shakhov, square = functions_of(cx, cy, cz)
    weight = (2.0 * speed_range / NVX) ** 3 * math.pi ** (-1.5) * np.exp(-square)
    rows = np.stack(rows) * weight
    shakhov = np.stack(shakhov)
    speeds = half_speeds(cx, cy, cz)
    stay = 1.0 - sum(speeds)
    out = np.stack([(rows * s) @ shakhov.T for s in [stay] + speeds])
    out[np.abs(out) < 1e-13] = 0.0
    return out


def split(value):
    high = value.astype(jnp.bfloat16)
    low = (value - high.astype(jnp.float32)).astype(jnp.bfloat16)
    return high, low


def speeds_at(index):
    speed = speed_range * (2.0 * index.astype(jnp.float32) + 1.0 - NVX) / NVX
    return [time_step * speed[a : a + 1] for a in range(3)]


class Upwind:
    def __init__(self, index):
        tx, ty, tz = speeds_at(index)
        shape = (NZ, LANES)
        self.ax, self.ay, self.az = (jnp.broadcast_to(jnp.abs(t), shape) for t in (tx, ty, tz))
        self.stay = 1.0 - self.ax - self.ay - self.az
        self.px, self.py, self.pz = (jnp.broadcast_to(t, shape) > 0 for t in (tx, ty, tz))

    def across(self, rows):
        out = []
        for before, here, after in zip(rows[:-2], rows[1:-1], rows[2:]):
            in_y = jnp.where(self.py, before, after)
            in_z = jnp.where(self.pz, pltpu.roll(here, 1, axis=0), pltpu.roll(here, NZ - 1, axis=0))
            out.append(self.stay * here + self.ay * in_y + self.az * in_z)
        return out

    def stream(self, ref, x, first, count):
        mid = self.across(run_of(lambda y: ref[x + 1, rows_of(y), :], first, count))
        out = []
        for j, value in enumerate(mid):
            at = rows_of(first + j)
            out.append(value + self.ax * jnp.where(self.px, ref[x, at, :], ref[x + 2, at, :]))
        return out


def run_of(read, first, count):
    ends = [lax.rem(first + count - 1, count), lax.rem(first + RUN, count)]
    return [read(ends[0])] + [read(first + j) for j in range(RUN)] + [read(ends[1])]


def rows_of(y):
    return pl.ds(pl.multiple_of(y * NZ, NZ), NZ)


def each_run(count, body):
    @pl.loop(0, count // RUN)
    def _(i):
        body(i * RUN)


def lane_copies(ref_row, target, blocks):
    for k in range(blocks):
        at = slice(k * LANES, (k + 1) * LANES)
        target[at, :] = jnp.broadcast_to(ref_row[:, at], (LANES, LANES)).T


def roll_y(value, sign):
    cells = value.shape[1]
    return pltpu.roll(value, NZ if sign > 0 else cells - NZ, axis=1)


def roll_z(value, sign):
    cells = value.shape[1]
    zl = lax.broadcasted_iota(jnp.int32, value.shape, 1) & (NZ - 1)
    if sign > 0:
        return jnp.where(zl == 0, pltpu.roll(value, cells - (NZ - 1), axis=1), pltpu.roll(value, 1, axis=1))
    return jnp.where(zl == NZ - 1, pltpu.roll(value, NZ - 1, axis=1), pltpu.roll(value, cells - 1, axis=1))


def stream_kernel(dist_ref, index_ref, leaving_ref, read_ref, held, even, odd, done, sems, out_sems, *, vels, blocks):
    stride = blocks * SUB
    chunks = vels // LANES
    part = LANES * stride
    piece = part // PIECES
    ys = blocks * LANES // NZ

    def fetch(c):
        return [
            pltpu.make_async_copy(
                dist_ref.at[pl.ds(c * part + p * piece, piece)],
                held.at[c % 2, pl.ds(p * piece, piece)],
                sems.at[c % 2, p],
            )
            for p in range(PIECES)
        ]

    def store(c):
        return pltpu.make_async_copy(done.at[c % 2], read_ref.at[c], out_sems.at[c % 2])

    def turn(c, k):
        target = odd if c % 2 else even
        for x in range(SUB):
            value = held[c % 2, pl.ds(k * SUB + x, LANES, stride=stride), :]
            target[x + 1, pl.ds(pl.multiple_of(k * LANES, LANES), LANES), :] = value.T

    for c in range(min(2, chunks)):
        for copy in fetch(c):
            copy.start()
    empty = jnp.zeros((ys * NZ, LANES), jnp.float32)
    for ref in (even, odd):
        ref[0] = empty
        ref[SUB + 1] = empty
    for copy in fetch(0):
        copy.wait()

    @pl.loop(0, blocks)
    def _(k):
        turn(0, k)

    for c in range(chunks):
        turned = odd if c % 2 else even
        if c + 2 < chunks:
            for copy in fetch(c + 2):
                copy.start()
        if c + 1 < chunks:
            for copy in fetch(c + 1):
                copy.wait()
        if c >= 2:
            store(c - 2).wait()
        upwind = Upwind(index_ref[:, c * LANES : (c + 1) * LANES])

        @pl.loop(0, SUB)
        def _(x, upwind=upwind, c=c, turned=turned):
            if c + 1 < chunks and blocks == SUB:
                turn(c + 1, x)
            for first in range(0, ys, RUN):
                for j, value in enumerate(upwind.stream(turned, x, first, ys)):
                    done[c % 2, x, rows_of(first + j), :] = value

        if c + 1 < chunks and blocks != SUB:

            @pl.loop(0, blocks)
            def _(k, c=c):
                turn(c + 1, k)

        def edges(first, upwind=upwind, c=c, turned=turned):
            for j in range(RUN):
                at = rows_of(first + j)
                bottom, top = turned[1, at, :], turned[SUB, at, :]
                done[c % 2, SUB, at, :] = top
                done[c % 2, SUB + 1, at, :] = bottom
                leaving_ref[c, 0, at, :] = jnp.where(upwind.px, top, bottom)
                leaving_ref[c, 1, at, :] = jnp.where(upwind.px, turned[SUB - 1, at, :], turned[2, at, :])

        each_run(ys, edges)
        store(c).start()
    for c in range(max(0, chunks - 2), chunks):
        store(c).wait()


def first_stream(flat, vel_index, vels, blocks):
    cells = blocks * LANES
    anywhere = pl.BlockSpec(memory_space=pl.ANY)
    vmem = pl.BlockSpec(memory_space=pltpu.VMEM)
    return pl.pallas_call(
        functools.partial(stream_kernel, vels=vels, blocks=blocks),
        in_specs=[anywhere, vmem],
        out_specs=[vmem, anywhere],
        out_shape=[
            jax.ShapeDtypeStruct((vels // LANES, 2, cells, LANES), jnp.float32),
            jax.ShapeDtypeStruct((vels // LANES, SUB + 2, cells, LANES), jnp.float32),
        ],
        scratch_shapes=[
            pltpu.VMEM((2, LANES * blocks * SUB, LANES), jnp.float32),
            pltpu.VMEM((SUB + 2, cells, LANES), jnp.float32),
            pltpu.VMEM((SUB + 2, cells, LANES), jnp.float32),
            pltpu.VMEM((2, SUB + 2, cells, LANES), jnp.float32),
            pltpu.SemaphoreType.DMA((2, PIECES)),
            pltpu.SemaphoreType.DMA((2,)),
        ],
        compiler_params=pltpu.CompilerParams(vmem_limit_bytes=54 * MIB),
        cost_estimate=pl.CostEstimate(
            flops=20 * vels * SUB * cells, bytes_accessed=8 * vels * SUB * cells, transcendentals=0
        ),
        name="first_stream",
    )(flat, vel_index)


def moments_kernel(me_ref, read_ref, index_ref, cst_ref, *refs, vels, blocks):
    half = blocks // 2
    outs = refs[:half]
    table, wst, acc, gacc, pay = refs[half:]
    span = SETS * 16
    step = pl.program_id(0)

    @pl.when(step == 0)
    def _():
        speed = [speed_range * (2.0 * index_ref[a : a + 1, :].astype(jnp.float32) + 1.0 - NVX) / NVX for a in range(3)]
        rows, _, square = functions_of(*speed)
        weight = (2.0 * speed_range / NVX) ** 3 * math.pi ** (-1.5) * jnp.exp(-square)
        table[...] = jnp.zeros_like(table)
        for m, row in enumerate(rows):
            table[m : m + 1, :] = row * weight
        base = table[...]
        speeds = []
        for c in speed:
            speeds.append(jnp.where(c > 0, time_step * c, 0.0))
            speeds.append(jnp.where(c < 0, -time_step * c, 0.0))
        full = jnp.concatenate([base] + [base * s for s in speeds] + [jnp.zeros_like(base)], axis=0)
        for variant, factor in enumerate([None, speeds[0], speeds[1]]):
            high, low = split((full if factor is None else full * factor).T)
            wst[variant, :, 0:LANES] = high
            wst[variant, :, LANES:] = low

    wide = 2 * LANES
    at = pl.ds(pl.multiple_of(step * wide, wide), wide)
    for slot in range(SUB + 2):
        variant = max(0, slot - SUB + 1)
        high, low = split(jnp.concatenate([read_ref[g, slot] for g in range(vels // LANES)], axis=1))
        first = jnp.dot(high, wst[variant], preferred_element_type=jnp.float32)
        second = jnp.dot(low, wst[variant, :, 0:LANES], preferred_element_type=jnp.float32)
        total = (first[:, 0:LANES] + first[:, LANES:] + second).T[0:span]
        if slot < SUB:
            for j in range(2):
                acc[2 * step + j, pl.ds(slot, span, stride=SUB), :] = total[:, j * LANES : (j + 1) * LANES]
        else:
            gacc[slot - SUB, :, at] = total

    @pl.when(step == pl.num_programs(0) - 1)
    def _():
        combine_moments(me_ref, cst_ref, outs, acc, gacc, pay, blocks)


def combine_moments(me_ref, cst_ref, outs, acc, gacc, pay, blocks):
    half = blocks // 2
    al = cst_ref[0, 0:SUB, :]
    beyond = cst_ref[0, SUB : SUB + 1, :]
    below = cst_ref[0, 2 * SUB - 1 : 2 * SUB, :]
    plane = lax.broadcasted_iota(jnp.int32, al.shape, 0)

    def own(i, m):
        first = (i * 16 + m) * SUB
        return jnp.concatenate([acc[k, first : first + SUB, :] for k in range(blocks)], axis=1)

    for m in range(MOM):
        sets = [own(i, m) for i in range(SETS)]
        value = al * (sets[0] - sum(sets[1:]))
        value = value + jnp.where(plane == 0, 0.0, pltpu.roll(al * sets[1], 1, axis=0))
        value = value + jnp.where(plane == SUB - 1, 0.0, pltpu.roll(al * sets[2], SUB - 1, axis=0))
        value = value + roll_y(al * sets[3], 1) + roll_y(al * sets[4], -1)
        value = value + roll_z(al * sets[5], 1) + roll_z(al * sets[6], -1)
        for k in range(blocks):
            at = slice(k * LANES, (k + 1) * LANES)
            pay[k, M1 + m * SUB : M1 + (m + 1) * SUB, :] = sets[0][:, at]
            pay[k, AA + m * SUB : AA + (m + 1) * SUB, :] = value[:, at]

    for side, (scale, edge, toward, start) in enumerate([(beyond, SUB - 1, 1, UP), (below, 0, 2, DOWN)]):
        sets = [gacc[side, i * 16 : (i + 1) * 16, :] for i in range(SETS)]
        near = scale * (sets[0] - sum(sets[1:]))
        near = near + roll_y(scale * sets[3], 1) + roll_y(scale * sets[4], -1)
        near = near + roll_z(scale * sets[5], 1) + roll_z(scale * sets[6], -1)
        out_of = jnp.concatenate(
            [acc[k, pl.ds(toward * 16 * SUB + edge, 16, stride=SUB), :] for k in range(blocks)], axis=1
        )
        near = near + al[edge : edge + 1, :] * out_of
        far = scale * sets[toward]
        for k in range(blocks):
            at = slice(k * LANES, (k + 1) * LANES)
            for j, value in enumerate((sets[0], near, far)):
                pay[k, start + j * MOM : start + (j + 1) * MOM, :] = value[0:MOM, at]
            pay[k, start + 3 * MOM : start + 3 * MOM + 1, :] = jnp.zeros((1, LANES), jnp.float32)

    mine = me_ref[0]
    for k in range(half):
        near = jnp.bitwise_xor(mine, k)
        outs[k][0:PAY, :] = pay[near]
        outs[k][PAY:, :] = pay[jnp.bitwise_xor(near, half)]


def both_moments(place, read, vel_index, cst, vels, blocks):
    cells = blocks * LANES
    vmem = pl.BlockSpec(memory_space=pltpu.VMEM)
    span = SETS * 16
    block = pl.BlockSpec((vels // LANES, SUB + 2, 2 * LANES, LANES), lambda i: (0, 0, i, 0))
    return pl.pallas_call(
        functools.partial(moments_kernel, vels=vels, blocks=blocks),
        grid=(blocks // 2,),
        in_specs=[pl.BlockSpec(memory_space=pltpu.SMEM), block, vmem, vmem],
        out_specs=[vmem] * (blocks // 2),
        out_shape=[jax.ShapeDtypeStruct((2 * PAY, LANES), jnp.float32)] * (blocks // 2),
        scratch_shapes=[
            pltpu.VMEM((16, vels), jnp.float32),
            pltpu.VMEM((3, vels, 2 * LANES), jnp.bfloat16),
            pltpu.VMEM((blocks, span * SUB, LANES), jnp.float32),
            pltpu.VMEM((2, span, cells), jnp.float32),
            pltpu.VMEM((blocks, PAY, LANES), jnp.float32),
        ],
        compiler_params=pltpu.CompilerParams(vmem_limit_bytes=56 * MIB),
        cost_estimate=pl.CostEstimate(
            flops=2 * 336 * vels * 10 * cells, bytes_accessed=4 * vels * 10 * cells, transcendentals=0
        ),
        name="moments_of_both",
    )(place, read, vel_index, cst)


def carried_kernel(read_ref, index_ref, al_ref, *refs, blocks):
    out_ref, mid, scale = refs[-3:]
    ys = blocks * LANES // NZ

    @pl.when(pl.program_id(0) == 0)
    def _():
        for x in range(SUB):
            lane_copies(al_ref[x : x + 1, :], scale.at[x], blocks)
        empty = jnp.zeros((ys * NZ, LANES), jnp.float32)
        mid[0] = empty
        mid[SUB + 1] = empty

    upwind = Upwind(index_ref[...])

    @pl.loop(0, SUB)
    def _(x):
        def run(first):
            for j in range(RUN):
                at = rows_of(first + j)
                mid[x + 1, at, :] = scale[x, at, :] * read_ref[0, x, at, :]

        each_run(ys, run)

    @pl.loop(0, SUB)
    def _(x):
        def run(first):
            for j, value in enumerate(upwind.stream(mid, x, first, ys)):
                at = rows_of(first + j)
                out_ref[0, x, at, :] = scale[x, at, :] * value

        each_run(ys, run)


def carried(read, vel_index, al, first, count, blocks, before=None):
    groups = read.shape[0]
    cells = blocks * LANES
    start = first // LANES
    block = pl.BlockSpec((1, SUB, cells, LANES), lambda i: (i + start, 0, 0, 0))
    held = [] if before is None else [before]
    return pl.pallas_call(
        functools.partial(carried_kernel, blocks=blocks),
        grid=(count // LANES,),
        in_specs=[
            block,
            pl.BlockSpec((3, LANES), lambda i: (0, i + start)),
            pl.BlockSpec((SUB, cells), lambda i: (0, 0)),
        ]
        + [pl.BlockSpec(memory_space=pl.ANY)] * len(held),
        out_specs=block,
        out_shape=jax.ShapeDtypeStruct((groups, SUB, cells, LANES), jnp.float32),
        scratch_shapes=[
            pltpu.VMEM((SUB + 2, cells, LANES), jnp.float32),
            pltpu.VMEM((SUB, cells, LANES), jnp.float32),
        ],
        input_output_aliases={3: 0} if held else {},
        compiler_params=pltpu.CompilerParams(vmem_limit_bytes=40 * MIB),
        cost_estimate=pl.CostEstimate(flops=1, bytes_accessed=1, transcendentals=0),
        name="carried_part",
    )(read, vel_index, al, *held)


def inflow_kernel(
    core_ref, swap_ref, first_ref, first1_ref, second_ref, second1_ref, index_ref, al_ref, out_ref,
    halo, edge, scale, *, blocks
):
    core = core_ref[0]
    ys = blocks * LANES // NZ

    @pl.when(pl.program_id(0) == 0)
    def _():
        for j, x in enumerate((0, SUB - 1, 1, SUB - 2, 2 * SUB - 1, SUB)):
            lane_copies(al_ref[x : x + 1, :], scale.at[j], blocks)

    upwind = Upwind(index_ref[...])
    from_far = upwind.px == (core == 0)
    @pl.loop(0, ys // 2)
    def _(y):
        at, up = rows_of(y), rows_of(y + ys // 2)
        for depth, (one, two) in enumerate(((first_ref, second_ref), (first1_ref, second1_ref))):
            a, b = one[0, 0, at, :], two[0, 0, at, :]
            halo[depth, at, :] = jnp.where(from_far, jnp.where(core == 0, a, b), swap_ref[0, depth, at, :])
            halo[depth, up, :] = jnp.where(from_far, jnp.where(core == 0, b, a), swap_ref[0, depth, up, :])

    def scaled(pair, at):
        return jnp.where(upwind.px, scale[2 * pair, at, :], scale[2 * pair + 1, at, :])

    def start(first):
        for j in range(RUN):
            at = rows_of(first + j)
            value = scaled(0, at) * upwind.ax * halo[0, at, :]
            edge[at, :] = value
            out_ref[0, 1, at, :] = scaled(1, at) * upwind.ax * value

    each_run(ys, start)

    def run(first):
        inside = upwind.across(run_of(lambda y: edge[rows_of(y), :], first, ys))
        beyond = upwind.across(run_of(lambda y: halo[0, rows_of(y), :], first, ys))
        for j in range(RUN):
            at = rows_of(first + j)
            streamed = beyond[j] + upwind.ax * halo[1, at, :]
            out_ref[0, 0, at, :] = scaled(0, at) * (inside[j] + upwind.ax * scaled(2, at) * streamed)

    each_run(ys, run)


def inflow(core, swap, first, first1, second, second1, vel_index, al16, vels, blocks):
    cells = blocks * LANES
    narrow = pl.BlockSpec((1, 1, cells // 2, LANES), lambda i: (i, 0, 0, 0))
    return pl.pallas_call(
        functools.partial(inflow_kernel, blocks=blocks),
        grid=(vels // LANES,),
        in_specs=[
            pl.BlockSpec(memory_space=pltpu.SMEM),
            pl.BlockSpec((1, 2, cells, LANES), lambda i: (i, 0, 0, 0)),
            narrow,
            narrow,
            narrow,
            narrow,
            pl.BlockSpec((3, LANES), lambda i: (0, i)),
            pl.BlockSpec((2 * SUB, cells), lambda i: (0, 0)),
        ],
        out_specs=pl.BlockSpec((1, 2, cells, LANES), lambda i: (i, 0, 0, 0)),
        out_shape=jax.ShapeDtypeStruct((vels // LANES, 2, cells, LANES), jnp.float32),
        scratch_shapes=[
            pltpu.VMEM((2, cells, LANES), jnp.float32),
            pltpu.VMEM((cells, LANES), jnp.float32),
            pltpu.VMEM((6, cells, LANES), jnp.float32),
        ],
        compiler_params=pltpu.CompilerParams(vmem_limit_bytes=24 * MIB),
        cost_estimate=pl.CostEstimate(flops=1, bytes_accessed=1, transcendentals=0),
        name="inflow_part",
    )(core, swap, first, first1, second, second1, vel_index, al16)


def small_call(kernel, outs, name, specs, args, scratch=(), limit=16):
    vmem = pl.BlockSpec(memory_space=pltpu.VMEM)
    smem = pl.BlockSpec(memory_space=pltpu.SMEM)
    return pl.pallas_call(
        kernel,
        in_specs=[smem if s == "s" else vmem for s in specs],
        out_specs=[vmem] * len(outs),
        out_shape=[jax.ShapeDtypeStruct(o, jnp.float32) for o in outs],
        scratch_shapes=list(scratch),
        compiler_params=pltpu.CompilerParams(vmem_limit_bytes=limit * MIB),
        name=name,
    )(*args)


def pair_kernel(*refs):
    parts, (near_ref, far_ref) = refs[:-2], refs[-2:]
    value = parts[0][...]
    for part in parts[1:]:
        value = value + part[...]
    near_ref[...] = value[0:PAY]
    far_ref[...] = value[PAY:]


def total_kernel(*refs):
    parts, (all_ref, up_ref, down_ref) = refs[:-3], refs[-3:]
    value = parts[0][...]
    for part in parts[1:]:
        value = value + part[...]
    all_ref[...] = value
    up_ref[...] = value[UP:DOWN]
    down_ref[...] = value[M1:AA]


def mix(inverse, values):
    return [sum(inverse[k, j] * values[j] for j in range(MOM)) for k in range(MOM)]


def chunk_kernel(inv_ref, own_ref, low_ref, high_ref, send_ref):
    plane = lax.broadcasted_iota(jnp.int32, (SUB, LANES), 0)
    inverse = {(k, j): inv_ref[k, j] for k in range(MOM) for j in range(MOM)}
    inner, outer, later = [], [], []
    for m in range(MOM):

        def row(ref, at):
            return ref[at : at + 1, :]

        first = own_ref[M1 + m * SUB : M1 + (m + 1) * SUB, :]
        second = own_ref[AA + m * SUB : AA + (m + 1) * SUB, :]
        low = low_ref[M1 + m * SUB : M1 + (m + 1) * SUB, :]
        high = high_ref[m * SUB : (m + 1) * SUB, :]
        below = DOWN - M1 + m
        inner.append(
            first + jnp.where(plane == 0, row(low_ref, m), 0.0) + jnp.where(plane == SUB - 1, row(high_ref, below), 0.0)
        )
        outer.append(
            jnp.where(plane < SUB // 2, high, low)
            + jnp.where(plane == 0, row(own_ref, UP + m), 0.0)
            + jnp.where(plane == SUB - 1, row(own_ref, DOWN + m), 0.0)
        )
        later.append(
            second
            + jnp.where(plane == 0, row(low_ref, MOM + m), 0.0)
            + jnp.where(plane == 1, row(low_ref, 2 * MOM + m), 0.0)
            + jnp.where(plane == SUB - 1, row(high_ref, below + MOM), 0.0)
            + jnp.where(plane == SUB - 2, row(high_ref, below + 2 * MOM), 0.0)
        )
    local, around = mix(inverse, inner), mix(inverse, outer)
    for n in range(4):
        send_ref[n * 16 : n * 16 + SUB, :] = local[n + 1]
        send_ref[n * 16 + SUB : (n + 1) * 16, :] = around[n + 1]
        send_ref[MOVED + n * SUB : MOVED + (n + 1) * SUB, :] = inner[n + 1]
    for n, k in enumerate(STILL):
        send_ref[FIXED + n * SUB : FIXED + (n + 1) * SUB, :] = local[k]
        send_ref[EDGE + n : EDGE + n + 1, :] = around[k][0:1]
        send_ref[EDGE + 4 + n : EDGE + 5 + n, :] = around[k][SUB - 1 :]
    for m in range(MOM):
        send_ref[LATER + m * SUB : LATER + (m + 1) * SUB, :] = later[m]
    send_ref[SQUARE:SENT, :] = sum((local[m] - inner[m]) ** 2 for m in range(MOM) if not 1 <= m <= 4)


def sweeps(source):
    rows = source.shape[0]
    field = source
    for _ in range(SWEEPS):
        beside = pltpu.roll(field, 1, axis=0) + pltpu.roll(field, rows - 1, axis=0)
        beside = beside + roll_y(field, 1) + roll_y(field, -1) + roll_z(field, 1) + roll_z(field, -1)
        field = (source + coupling * beside) * (1.0 / (1.0 + 6.0 * coupling))
    return field


def fields_kernel(place_ref, inv_ref, cst_ref, *refs, blocks):
    parts = refs[:blocks]
    h1_ref, later_ref, next_ref, up_ref, down_ref, norm_ref, whole = refs[blocks:]
    mine = place_ref[0]
    for k in range(blocks):
        whole[jnp.bitwise_xor(mine, k)] = parts[k][...]

    def rows(first, count):
        return jnp.concatenate([whole[k, first : first + count, :] for k in range(blocks)], axis=1)

    def fold(value):
        return sum(value[:, k * LANES : (k + 1) * LANES] for k in range(blocks))

    square = sum(whole[k, SQUARE:SENT, :] for k in range(blocks))
    al = cst_ref[0, 0:SUB, :]
    edges = rows(EDGE, SUB)
    plane = lax.broadcasted_iota(jnp.int32, al.shape, 0)
    moved = []
    for n, m in enumerate(PICK):
        if 1 <= m <= 4:
            value = sweeps(rows((m - 1) * 16, 16))
            square = square + fold((value[0:SUB] - rows(MOVED + (m - 1) * SUB, SUB)) ** 2)
        else:
            k = STILL.index(m)
            around = jnp.where(
                plane == 0, edges[k : k + 1], jnp.where(plane == SUB - 1, edges[4 + k : 5 + k], 0.0)
            )
            value = jnp.concatenate([rows(FIXED + k * SUB, SUB), around], axis=0)
        given = cst_ref[1 if n in (0, 4) else 2] * value
        inside = given[0:SUB]
        shifted = [
            inside,
            pltpu.roll(given, 1, axis=0)[0:SUB],
            pltpu.roll(given, 2 * SUB - 1, axis=0)[0:SUB],
            roll_y(inside, 1),
            roll_y(inside, -1),
            roll_z(inside, 1),
            roll_z(inside, -1),
        ]
        for s in range(SETS):
            value = al * shifted[s]
            for k in range(blocks):
                first = (s * 8 + n) * SUB
                h1_ref[k, first : first + SUB, :] = value[:, k * LANES : (k + 1) * LANES]
        moved.append(shifted)
    norm_ref[...] = square

    matrices = stream_matrices()
    moments = []
    for m in range(MOM):
        value = rows(LATER + m * SUB, SUB)
        for s in range(SETS):
            for n in range(8):
                factor = float(matrices[s, m, n])
                if factor != 0.0:
                    value = value + factor * moved[n][s]
        later_ref[m * SUB : (m + 1) * SUB, :] = value
        moments.append(value)
    inverse = {(k, j): inv_ref[k, j] for k in range(MOM) for j in range(MOM)}
    for m, value in enumerate(mix(inverse, moments)):
        next_ref[m * SUB : (m + 1) * SUB, :] = value
        if 1 <= m <= 4:
            up_ref[(m - 1) * 4 : m * 4, :] = value[SUB // 2 :]
            down_ref[(m - 1) * 4 : m * 4, :] = value[: SUB // 2]


def last_kernel(
    place_ref, cst_ref, later_ref, next_ref, low_ref, high_ref, norm1_ref, h2_ref, out_ref, norm_ref, wide, *, blocks
):
    mine = place_ref[0]
    square = jnp.zeros((SUB, LANES), jnp.float32)
    for m in range(MOM):
        value = next_ref[m * SUB : (m + 1) * SUB, :]
        if 1 <= m <= 4:
            at = slice((m - 1) * 4, m * 4)
            value = sweeps(jnp.concatenate([value, high_ref[at, :], low_ref[at, :]], axis=0))[0:SUB]
        off = (value - later_ref[m * SUB : (m + 1) * SUB, :]) ** 2
        for k in range(blocks):
            wide[m, k] = value[:, k * LANES : (k + 1) * LANES]
            square = square + off[:, k * LANES : (k + 1) * LANES]
        out_ref[m] = wide[m, mine]
        if m in PICK:
            n = PICK.index(m)
            given = cst_ref[1 if n in (0, 4) else 2, 0:SUB, :] * value
            for k in range(blocks):
                h2_ref[k, n * SUB : (n + 1) * SUB, :] = given[:, k * LANES : (k + 1) * LANES]
    norm_ref[0:1, :] = jnp.sum(norm1_ref[...], axis=0, keepdims=True)
    norm_ref[1:2, :] = jnp.sum(square, axis=0, keepdims=True)


def finish_kernel(carried_ref, inflow_ref, h1_ref, h2_ref, index_ref, out_ref, rows, fields, table, *, blocks):
    group = pl.program_id(0)

    @pl.when(group == 0)
    def _():
        speed = [speed_range * (2.0 * index_ref[a : a + 1, :].astype(jnp.float32) + 1.0 - NVX) / NVX for a in range(3)]
        for n, row in enumerate(functions_of(*speed)[1]):
            table[n : n + 1, :] = row
        base = table[...]
        speeds = []
        for c in speed:
            speeds.append(jnp.where(c > 0, time_step * c, 0.0))
            speeds.append(jnp.where(c < 0, -time_step * c, 0.0))
        full = jnp.concatenate([base * (1.0 - sum(speeds))] + [base * s for s in speeds] + [base], axis=0)
        high = full.astype(jnp.bfloat16).astype(jnp.float32)
        stacked = jnp.concatenate([high, high, full - high, jnp.zeros_like(full)], axis=0).astype(jnp.bfloat16)
        for g in range(rows.shape[0]):
            rows[g] = stacked[:, g * LANES : (g + 1) * LANES]
        left = lax.broadcasted_iota(jnp.int32, (LANES, LANES), 1) < LANES // 2

        @pl.loop(0, blocks)
        def _(k):
            at = pl.ds(pl.multiple_of(k * LANES, LANES), LANES)
            for x in range(SUB):
                first = h1_ref[k, pl.ds(x, SETS * 8, stride=SUB), :]
                second = h2_ref[k, pl.ds(x, 8, stride=SUB), :]
                value = jnp.concatenate([first, second, first, second], axis=0).T
                high = value.astype(jnp.bfloat16).astype(jnp.float32)
                fields[x, at, 0:LANES] = jnp.where(left, high, value - high).astype(jnp.bfloat16)
                fields[x, at, LANES:] = jnp.where(left, high, 0.0).astype(jnp.bfloat16)

    out = out_ref.reshape(LANES * blocks * SUB, LANES)
    here = index_ref[0:1, pl.ds(pl.multiple_of(group * LANES, LANES), LANES)]
    px = here * 2 >= NVX
    for x in range(SUB):
        value = carried_ref[0, x] + jnp.dot(fields[x], rows[group], preferred_element_type=jnp.float32)
        if x in (0, 1):
            value = value + jnp.where(px, inflow_ref[0, x], 0.0)
        elif x in (SUB - 2, SUB - 1):
            value = value + jnp.where(px, 0.0, inflow_ref[0, SUB - 1 - x])
        for k in range(blocks):
            out[pl.ds(k * SUB + x, LANES, stride=blocks * SUB), :] = value[k * LANES : (k + 1) * LANES].T


def finish(carried_part, inflow_part, h1, h2, vel_index, vels, blocks):
    cells = blocks * LANES
    groups = vels // LANES
    vmem = pl.BlockSpec(memory_space=pltpu.VMEM)
    return pl.pallas_call(
        functools.partial(finish_kernel, blocks=blocks),
        grid=(groups,),
        in_specs=[
            pl.BlockSpec((1, SUB, cells, LANES), lambda g: (g, 0, 0, 0)),
            pl.BlockSpec((1, 2, cells, LANES), lambda g: (g, 0, 0, 0)),
            vmem,
            vmem,
            vmem,
        ],
        out_specs=pl.BlockSpec((LANES, blocks, SUB, LANES), lambda g: (g, 0, 0, 0)),
        out_shape=jax.ShapeDtypeStruct((vels, blocks, SUB, LANES), jnp.float32),
        scratch_shapes=[
            pltpu.VMEM((groups, 256, LANES), jnp.bfloat16),
            pltpu.VMEM((SUB, cells, 256), jnp.bfloat16),
            pltpu.VMEM((8, vels), jnp.float32),
        ],
        compiler_params=pltpu.CompilerParams(vmem_limit_bytes=36 * MIB),
        cost_estimate=pl.CostEstimate(
            flops=2 * 256 * vels * blocks * SUB * LANES, bytes_accessed=8 * vels * blocks * SUB * LANES, transcendentals=0
        ),
        name="finish_dist",
    )(carried_part, inflow_part, h1, h2, vel_index)


def ring(axis, step):
    size = lax.axis_size(axis)
    return [(i, (i + step) % size) for i in range(size)]


def shards(dist, vel_index, relax, wall_mask, macro_inverse):
    vels, width, cells = dist.shape
    blocks = cells // LANES
    peers, slabs = lax.axis_size("vel"), lax.axis_size("space")
    assert width == SUB and peers % blocks == 0 and slabs == 4 and blocks % 2 == 0
    sub = peers // blocks
    me = lax.axis_index("vel")
    place = (me // sub).astype(jnp.int32).reshape(1)
    core = (lax.axis_index("space") % 2).astype(jnp.int32).reshape(1)

    flat = dist.reshape(vels, width, blocks, LANES).transpose(0, 2, 1, 3).reshape(vels * blocks * width, LANES)
    speed = speed_range * (2.0 * vel_index.astype(jnp.float32) + 1.0 - NVX) / NVX

    wall = wall_mask > 0
    coefficients = jnp.stack(
        [
            jnp.where(wall, 0.0, 1.0 - relax),
            jnp.where(wall, 1.0, relax),
            jnp.where(wall, 0.0, relax),
        ],
        0,
    )
    from_low = lax.ppermute(coefficients[:, SUB - 1 :], "space", ring("space", 1))
    from_high = lax.ppermute(coefficients[:, :1], "space", ring("space", -1))

    leaving, read = first_stream(flat, vel_index, vels, blocks)
    (leaving, from_low, from_high) = lax.optimization_barrier((leaving, from_low, from_high))
    swap = lax.ppermute(leaving, "space", [(i, i ^ 1) for i in range(slabs)])
    cst = jnp.concatenate(
        [coefficients, from_high, jnp.zeros((3, SUB - 2, cells), jnp.float32), from_low], 1
    )

    parts = both_moments(place, read, vel_index, cst, vels, blocks)
    (swap, parts) = lax.optimization_barrier((swap, parts))

    half = cells // 2
    start = core[0] * half
    mine = lax.dynamic_slice_in_dim(leaving, start, half, 2)
    other = lax.dynamic_slice_in_dim(swap, start, half, 2)
    plus = speed[0].reshape(vels // LANES, 1, 1, LANES) > 0
    across = jnp.where(plus == (core[0] == 1), mine, other)
    (across, parts) = lax.optimization_barrier((across, parts))
    over = [(i, i ^ 2) for i in range(slabs)]
    first = [lax.ppermute(across[:, 0:1], "space", over)]

    def beside(step):
        return [(i, (i // sub ^ step) * sub + i % sub) for i in range(peers)]

    spans = [(0, vels)] if vels < 2 * LANES else [(0, vels // 2), (vels // 2, vels - vels // 2)]

    got = [parts[0]] + [lax.ppermute(parts[k], "vel", beside(k)) for k in range(1, blocks // 2)]
    carried_part = carried(read, vel_index, coefficients[0], *spans[0], blocks)
    (got[1], carried_part) = lax.optimization_barrier((got[1], carried_part))
    near, far = small_call(pair_kernel, [(PAY, LANES)] * 2, "sum_near", "v" * len(got), got)
    got = [near, lax.ppermute(far, "vel", beside(blocks // 2))]
    if len(spans) > 1:
        (al, _) = lax.optimization_barrier((coefficients[0], near))
        carried_part = carried(read, vel_index, al, *spans[1], blocks, carried_part)
        (got[1], carried_part) = lax.optimization_barrier((got[1], carried_part))
    if sub > 1:
        part = sum(got)
        got = [part]
        for k in range(1, sub):
            pairs = [(i, i // sub * sub + (i % sub + k) % sub) for i in range(peers)]
            got.append(lax.ppermute(part, "vel", pairs))
    chunk, up, down = small_call(
        total_kernel, [(PAY, LANES), (DOWN - UP, LANES), (AA - M1, LANES)], "sum_moments", "v" * len(got), got
    )
    (first[0], up, down) = lax.optimization_barrier((first[0], up, down))
    low = lax.ppermute(up, "space", ring("space", 1))
    high = lax.ppermute(down, "space", ring("space", -1))
    (send,) = small_call(
        chunk_kernel, [(SENT, LANES)], "local_fields", "svvv", (macro_inverse, chunk, low, high)
    )
    pieces = [send] + [lax.ppermute(send, "vel", beside(k)) for k in range(1, blocks // 2 + 1)]
    across1, send = lax.optimization_barrier((across[:, 1:2], send))
    first.append(lax.ppermute(across1, "space", over))
    swap_chip = [(i, i ^ 1) for i in range(slabs)]
    second = [lax.ppermute(first[0], "space", swap_chip)]
    pieces += [lax.ppermute(pieces[blocks // 2], "vel", beside(k)) for k in range(1, blocks // 2)]

    h1, later, following, up2, down2, norm1 = small_call(
        functools.partial(fields_kernel, blocks=blocks),
        [
            (blocks, SETS * 8 * SUB, LANES),
            (MOM * SUB, cells),
            (MOM * SUB, cells),
            (16, cells),
            (16, cells),
            (SUB, LANES),
        ],
        "first_fields",
        "ssv" + "v" * blocks,
        (place, macro_inverse, cst, *pieces),
        [pltpu.VMEM((blocks, SENT, LANES), jnp.float32)],
        10,
    )
    (first[1], up2) = lax.optimization_barrier((first[1], up2))
    second.append(lax.ppermute(first[1], "space", swap_chip))
    low2 = lax.ppermute(up2, "space", ring("space", 1))
    high2 = lax.ppermute(down2, "space", ring("space", -1))
    h2, owned, squares = small_call(
        functools.partial(last_kernel, blocks=blocks),
        [(blocks, 8 * SUB, LANES), (MOM, SUB, LANES), (2, LANES)],
        "last_fields",
        "svvvvvv",
        (place, cst, later, following, low2, high2, norm1),
        [pltpu.VMEM((MOM, blocks, SUB, LANES), jnp.float32)],
        10,
    )

    around = [lax.ppermute(squares, "space", ring("space", k)) for k in range(1, slabs)]
    (second[1], h2) = lax.optimization_barrier((second[1], h2))
    inflow_part = inflow(core, swap, *first, *second, vel_index, cst[0], vels, blocks)
    if sub > 1:
        owned = lax.dynamic_slice_in_dim(owned, (me % sub) * (LANES // sub), LANES // sub, 2)

    out = finish(carried_part, inflow_part, h1, h2, vel_index, vels, blocks)
    (around[0], out) = lax.optimization_barrier((around[0], out))
    slab = lax.axis_index("space")
    every = [squares] + around
    ordered = [
        functools.reduce(lambda a, k: jnp.where((slab - k) % slabs == j, every[k], a), range(1, slabs), every[0])
        for j in range(slabs)
    ]
    norms = jnp.sqrt(jnp.sum(sum(ordered), axis=1))
    out = out.transpose(0, 2, 1, 3).reshape(vels, width, cells)
    return (out, owned, norms)


def solution(mesh):
    return jax.shard_map(
        shards,
        mesh=mesh,
        in_specs=(P("vel", "space", None), P(None, "vel"), P("space", None), P("space", None), P()),
        out_specs=(P("vel", "space", None), P(None, "space", "vel"), P()),
        check_vma=False,
    )
```

```python
import functools
import math

import jax
import jax.numpy as jnp
import numpy as np
from jax import lax
from jax.experimental import pallas as pl
from jax.experimental.pallas import tpu as pltpu
from jax.sharding import PartitionSpec as P

NVX = 16
NZ = 16
MOM = 13
SWEEPS = 3
LANES = 128
SUB = 8
SETS = 7
PICK = (0, 1, 2, 3, 4, 10, 11, 12)

speed_range = 4.0
time_step = 0.08
coupling = 0.5
MIB = 2**20
PIECES = 8
RUN = 16

UP, M1, DOWN, AA, PAY = 0, 40, 144, 184, 288
STILL = (0, 10, 11, 12)
MOVED, FIXED, EDGE, LATER, SQUARE, SENT = 64, 96, 128, 136, 240, 248


def functions_of(cx, cy, cz):
    square = cx * cx + cy * cy + cz * cz
    heat = square - 2.5
    one = cx * 0.0 + 1.0
    rows = [
        one, cx, cy, cz, 2.0 * square / 3.0 - 1.0, 2.0 * cx * cy, 2.0 * cx * cz, 2.0 * cy * cz,
        cx * cx - cy * cy, cy * cy - cz * cz, cx * heat, cy * heat, cz * heat,
    ]
    factor = 4.0 / 15.0
    shakhov = [
        one, 2.0 * cx, 2.0 * cy, 2.0 * cz, square - 1.5,
        factor * cx * heat, factor * cy * heat, factor * cz * heat,
    ]
    return rows, shakhov, square


def half_speeds(cx, cy, cz):
    out = []
    for c in (cx, cy, cz):
        out.append(time_step * c * (c > 0))
        out.append(-time_step * c * (c < 0))
    return out


@functools.lru_cache(None)
def stream_matrices():
    line = speed_range * (2.0 * np.arange(NVX) + 1.0 - NVX) / NVX
    cx, cy, cz = (g.reshape(-1) for g in np.meshgrid(line, line, line, indexing="ij"))
    rows, shakhov, square = functions_of(cx, cy, cz)
    weight = (2.0 * speed_range / NVX) ** 3 * math.pi ** (-1.5) * np.exp(-square)
    rows = np.stack(rows) * weight
    shakhov = np.stack(shakhov)
    speeds = half_speeds(cx, cy, cz)
    stay = 1.0 - sum(speeds)
    out = np.stack([(rows * s) @ shakhov.T for s in [stay] + speeds])
    out[np.abs(out) < 1e-13] = 0.0
    return out


def split(value):
    high = value.astype(jnp.bfloat16)
    low = (value - high.astype(jnp.float32)).astype(jnp.bfloat16)
    return high, low


def speeds_at(index):
    speed = speed_range * (2.0 * index.astype(jnp.float32) + 1.0 - NVX) / NVX
    return [time_step * speed[a : a + 1] for a in range(3)]


class Upwind:
    def __init__(self, index):
        tx, ty, tz = speeds_at(index)
        shape = (NZ, LANES)
        self.ax, self.ay, self.az = (jnp.broadcast_to(jnp.abs(t), shape) for t in (tx, ty, tz))
        self.stay = 1.0 - self.ax - self.ay - self.az
        self.px, self.py, self.pz = (jnp.broadcast_to(t, shape) > 0 for t in (tx, ty, tz))

    def across(self, rows):
        out = []
        for before, here, after in zip(rows[:-2], rows[1:-1], rows[2:]):
            in_y = jnp.where(self.py, before, after)
            in_z = jnp.where(self.pz, pltpu.roll(here, 1, axis=0), pltpu.roll(here, NZ - 1, axis=0))
            out.append(self.stay * here + self.ay * in_y + self.az * in_z)
        return out

    def stream(self, ref, x, first, count):
        mid = self.across(run_of(lambda y: ref[x + 1, rows_of(y), :], first, count))
        out = []
        for j, value in enumerate(mid):
            at = rows_of(first + j)
            out.append(value + self.ax * jnp.where(self.px, ref[x, at, :], ref[x + 2, at, :]))
        return out


def run_of(read, first, count):
    ends = [lax.rem(first + count - 1, count), lax.rem(first + RUN, count)]
    return [read(ends[0])] + [read(first + j) for j in range(RUN)] + [read(ends[1])]


def rows_of(y):
    return pl.ds(pl.multiple_of(y * NZ, NZ), NZ)


def each_run(count, body):
    @pl.loop(0, count // RUN)
    def _(i):
        body(i * RUN)


def lane_copies(ref_row, target, blocks):
    for k in range(blocks):
        at = slice(k * LANES, (k + 1) * LANES)
        target[at, :] = jnp.broadcast_to(ref_row[:, at], (LANES, LANES)).T


def roll_y(value, sign):
    cells = value.shape[1]
    return pltpu.roll(value, NZ if sign > 0 else cells - NZ, axis=1)


def roll_z(value, sign):
    cells = value.shape[1]
    zl = lax.broadcasted_iota(jnp.int32, value.shape, 1) & (NZ - 1)
    if sign > 0:
        return jnp.where(zl == 0, pltpu.roll(value, cells - (NZ - 1), axis=1), pltpu.roll(value, 1, axis=1))
    return jnp.where(zl == NZ - 1, pltpu.roll(value, NZ - 1, axis=1), pltpu.roll(value, cells - 1, axis=1))


def stream_kernel(dist_ref, index_ref, leaving_ref, read_ref, held, even, odd, done, sems, out_sems, *, vels, blocks):
    stride = blocks * SUB
    chunks = vels // LANES
    part = LANES * stride
    piece = part // PIECES
    ys = blocks * LANES // NZ

    def fetch(c):
        return [
            pltpu.make_async_copy(
                dist_ref.at[pl.ds(c * part + p * piece, piece)],
                held.at[c % 2, pl.ds(p * piece, piece)],
                sems.at[c % 2, p],
            )
            for p in range(PIECES)
        ]

    def store(c):
        return pltpu.make_async_copy(done.at[c % 2], read_ref.at[c], out_sems.at[c % 2])

    def turn(c, k):
        target = odd if c % 2 else even
        for x in range(SUB):
            value = held[c % 2, pl.ds(k * SUB + x, LANES, stride=stride), :]
            target[x + 1, pl.ds(pl.multiple_of(k * LANES, LANES), LANES), :] = value.T

    for c in range(min(2, chunks)):
        for copy in fetch(c):
            copy.start()
    empty = jnp.zeros((ys * NZ, LANES), jnp.float32)
    for ref in (even, odd):
        ref[0] = empty
        ref[SUB + 1] = empty
    for copy in fetch(0):
        copy.wait()

    @pl.loop(0, blocks)
    def _(k):
        turn(0, k)

    for c in range(chunks):
        turned = odd if c % 2 else even
        if c + 2 < chunks:
            for copy in fetch(c + 2):
                copy.start()
        if c + 1 < chunks:
            for copy in fetch(c + 1):
                copy.wait()
        if c >= 2:
            store(c - 2).wait()
        upwind = Upwind(index_ref[:, c * LANES : (c + 1) * LANES])

        @pl.loop(0, SUB)
        def _(x, upwind=upwind, c=c, turned=turned):
            if c + 1 < chunks and blocks == SUB:
                turn(c + 1, x)
            for first in range(0, ys, RUN):
                for j, value in enumerate(upwind.stream(turned, x, first, ys)):
                    done[c % 2, x, rows_of(first + j), :] = value

        if c + 1 < chunks and blocks != SUB:

            @pl.loop(0, blocks)
            def _(k, c=c):
                turn(c + 1, k)

        def edges(first, upwind=upwind, c=c, turned=turned):
            for j in range(RUN):
                at = rows_of(first + j)
                bottom, top = turned[1, at, :], turned[SUB, at, :]
                leaving_ref[c, 0, at, :] = jnp.where(upwind.px, top, bottom)
                leaving_ref[c, 1, at, :] = jnp.where(upwind.px, turned[SUB - 1, at, :], turned[2, at, :])

        each_run(ys, edges)
        store(c).start()
    for c in range(max(0, chunks - 2), chunks):
        store(c).wait()


def first_stream(flat, vel_index, vels, blocks):
    cells = blocks * LANES
    anywhere = pl.BlockSpec(memory_space=pl.ANY)
    vmem = pl.BlockSpec(memory_space=pltpu.VMEM)
    return pl.pallas_call(
        functools.partial(stream_kernel, vels=vels, blocks=blocks),
        in_specs=[anywhere, vmem],
        out_specs=[vmem, anywhere],
        out_shape=[
            jax.ShapeDtypeStruct((vels // LANES, 2, cells, LANES), jnp.float32),
            jax.ShapeDtypeStruct((vels // LANES, SUB, cells, LANES), jnp.float32),
        ],
        scratch_shapes=[
            pltpu.VMEM((2, LANES * blocks * SUB, LANES), jnp.float32),
            pltpu.VMEM((SUB + 2, cells, LANES), jnp.float32),
            pltpu.VMEM((SUB + 2, cells, LANES), jnp.float32),
            pltpu.VMEM((2, SUB, cells, LANES), jnp.float32),
            pltpu.SemaphoreType.DMA((2, PIECES)),
            pltpu.SemaphoreType.DMA((2,)),
        ],
        compiler_params=pltpu.CompilerParams(vmem_limit_bytes=54 * MIB),
        cost_estimate=pl.CostEstimate(
            flops=20 * vels * SUB * cells, bytes_accessed=8 * vels * SUB * cells, transcendentals=0
        ),
        name="first_stream",
    )(flat, vel_index)


def moments_kernel(me_ref, read_ref, leaving_ref, index_ref, cst_ref, *refs, vels, blocks):
    half = blocks // 2
    outs = refs[:half]
    table, wst, acc, gacc, pay = refs[half:]
    span = SETS * 16
    step = pl.program_id(0)

    @pl.when(step == 0)
    def _():
        speed = [speed_range * (2.0 * index_ref[a : a + 1, :].astype(jnp.float32) + 1.0 - NVX) / NVX for a in range(3)]
        rows, _, square = functions_of(*speed)
        weight = (2.0 * speed_range / NVX) ** 3 * math.pi ** (-1.5) * jnp.exp(-square)
        table[...] = jnp.zeros_like(table)
        for m, row in enumerate(rows):
            table[m : m + 1, :] = row * weight
        base = table[...]
        speeds = []
        for c in speed:
            speeds.append(jnp.where(c > 0, time_step * c, 0.0))
            speeds.append(jnp.where(c < 0, -time_step * c, 0.0))
        full = jnp.concatenate([base] + [base * s for s in speeds] + [jnp.zeros_like(base)], axis=0)
        for variant, factor in enumerate([None, speeds[0], speeds[1]]):
            high, low = split((full if factor is None else full * factor).T)
            wst[variant, :, 0:LANES] = high
            wst[variant, :, LANES:] = low

    wide = 2 * LANES
    at = pl.ds(pl.multiple_of(step * wide, wide), wide)
    groups = range(vels // LANES)

    def reduced(high, low, variant):
        first = jnp.dot(high, wst[variant], preferred_element_type=jnp.float32)
        second = jnp.dot(low, wst[variant, :, 0:LANES], preferred_element_type=jnp.float32)
        return (first[:, 0:LANES] + first[:, LANES:] + second).T[0:span]

    for x in range(SUB):
        total = reduced(*split(jnp.concatenate([read_ref[g, x] for g in groups], axis=1)), 0)
        for j in range(2):
            acc[2 * step + j, pl.ds(x, span, stride=SUB), :] = total[:, j * LANES : (j + 1) * LANES]
    edge = split(jnp.concatenate([leaving_ref[g, 0] for g in groups], axis=1))
    for side in range(2):
        gacc[side, :, at] = reduced(*edge, side + 1)

    @pl.when(step == pl.num_programs(0) - 1)
    def _():
        combine_moments(me_ref, cst_ref, outs, acc, gacc, pay, blocks)


def combine_moments(me_ref, cst_ref, outs, acc, gacc, pay, blocks):
    half = blocks // 2
    al = cst_ref[0, 0:SUB, :]
    beyond = cst_ref[0, SUB : SUB + 1, :]
    below = cst_ref[0, 2 * SUB - 1 : 2 * SUB, :]
    plane = lax.broadcasted_iota(jnp.int32, al.shape, 0)

    def own(i, m):
        first = (i * 16 + m) * SUB
        return jnp.concatenate([acc[k, first : first + SUB, :] for k in range(blocks)], axis=1)

    for m in range(MOM):
        sets = [own(i, m) for i in range(SETS)]
        value = al * (sets[0] - sum(sets[1:]))
        value = value + jnp.where(plane == 0, 0.0, pltpu.roll(al * sets[1], 1, axis=0))
        value = value + jnp.where(plane == SUB - 1, 0.0, pltpu.roll(al * sets[2], SUB - 1, axis=0))
        value = value + roll_y(al * sets[3], 1) + roll_y(al * sets[4], -1)
        value = value + roll_z(al * sets[5], 1) + roll_z(al * sets[6], -1)
        for k in range(blocks):
            at = slice(k * LANES, (k + 1) * LANES)
            pay[k, M1 + m * SUB : M1 + (m + 1) * SUB, :] = sets[0][:, at]
            pay[k, AA + m * SUB : AA + (m + 1) * SUB, :] = value[:, at]

    for side, (scale, edge, toward, start) in enumerate([(beyond, SUB - 1, 1, UP), (below, 0, 2, DOWN)]):
        sets = [gacc[side, i * 16 : (i + 1) * 16, :] for i in range(SETS)]
        near = scale * (sets[0] - sum(sets[1:]))
        near = near + roll_y(scale * sets[3], 1) + roll_y(scale * sets[4], -1)
        near = near + roll_z(scale * sets[5], 1) + roll_z(scale * sets[6], -1)
        out_of = jnp.concatenate(
            [acc[k, pl.ds(toward * 16 * SUB + edge, 16, stride=SUB), :] for k in range(blocks)], axis=1
        )
        near = near + al[edge : edge + 1, :] * out_of
        far = scale * sets[toward]
        for k in range(blocks):
            at = slice(k * LANES, (k + 1) * LANES)
            for j, value in enumerate((sets[0], near, far)):
                pay[k, start + j * MOM : start + (j + 1) * MOM, :] = value[0:MOM, at]
            pay[k, start + 3 * MOM : start + 3 * MOM + 1, :] = jnp.zeros((1, LANES), jnp.float32)

    mine = me_ref[0]
    for k in range(half):
        near = jnp.bitwise_xor(mine, k)
        outs[k][0:PAY, :] = pay[near]
        outs[k][PAY:, :] = pay[jnp.bitwise_xor(near, half)]


def both_moments(place, read, leaving, vel_index, cst, vels, blocks):
    cells = blocks * LANES
    vmem = pl.BlockSpec(memory_space=pltpu.VMEM)
    span = SETS * 16
    block = pl.BlockSpec((vels // LANES, SUB, 2 * LANES, LANES), lambda i: (0, 0, i, 0))
    edge = pl.BlockSpec((vels // LANES, 1, 2 * LANES, LANES), lambda i: (0, 0, i, 0))
    return pl.pallas_call(
        functools.partial(moments_kernel, vels=vels, blocks=blocks),
        grid=(blocks // 2,),
        in_specs=[pl.BlockSpec(memory_space=pltpu.SMEM), block, edge, vmem, vmem],
        out_specs=[vmem] * (blocks // 2),
        out_shape=[jax.ShapeDtypeStruct((2 * PAY, LANES), jnp.float32)] * (blocks // 2),
        scratch_shapes=[
            pltpu.VMEM((16, vels), jnp.float32),
            pltpu.VMEM((3, vels, 2 * LANES), jnp.bfloat16),
            pltpu.VMEM((blocks, span * SUB, LANES), jnp.float32),
            pltpu.VMEM((2, span, cells), jnp.float32),
            pltpu.VMEM((blocks, PAY, LANES), jnp.float32),
        ],
        compiler_params=pltpu.CompilerParams(vmem_limit_bytes=56 * MIB),
        cost_estimate=pl.CostEstimate(
            flops=2 * 336 * vels * 10 * cells, bytes_accessed=4 * vels * 10 * cells, transcendentals=0
        ),
        name="moments_of_both",
    )(place, read, leaving, vel_index, cst)


def carried_kernel(read_ref, index_ref, al_ref, *refs, blocks):
    out_ref, mid, scale = refs[-3:]
    ys = blocks * LANES // NZ

    @pl.when(pl.program_id(0) == 0)
    def _():
        for x in range(SUB):
            lane_copies(al_ref[x : x + 1, :], scale.at[x], blocks)
        empty = jnp.zeros((ys * NZ, LANES), jnp.float32)
        mid[0] = empty
        mid[SUB + 1] = empty

    upwind = Upwind(index_ref[...])

    @pl.loop(0, SUB)
    def _(x):
        def run(first):
            for j in range(RUN):
                at = rows_of(first + j)
                mid[x + 1, at, :] = scale[x, at, :] * read_ref[0, x, at, :]

        each_run(ys, run)

    @pl.loop(0, SUB)
    def _(x):
        def run(first):
            for j, value in enumerate(upwind.stream(mid, x, first, ys)):
                at = rows_of(first + j)
                out_ref[0, x, at, :] = scale[x, at, :] * value

        each_run(ys, run)


def carried(read, vel_index, al, first, count, blocks, before=None):
    groups = read.shape[0]
    cells = blocks * LANES
    start = first // LANES
    block = pl.BlockSpec((1, SUB, cells, LANES), lambda i: (i + start, 0, 0, 0))
    held = [] if before is None else [before]
    return pl.pallas_call(
        functools.partial(carried_kernel, blocks=blocks),
        grid=(count // LANES,),
        in_specs=[
            block,
            pl.BlockSpec((3, LANES), lambda i: (0, i + start)),
            pl.BlockSpec((SUB, cells), lambda i: (0, 0)),
        ]
        + [pl.BlockSpec(memory_space=pl.ANY)] * len(held),
        out_specs=block,
        out_shape=jax.ShapeDtypeStruct((groups, SUB, cells, LANES), jnp.float32),
        scratch_shapes=[
            pltpu.VMEM((SUB + 2, cells, LANES), jnp.float32),
            pltpu.VMEM((SUB, cells, LANES), jnp.float32),
        ],
        input_output_aliases={3: 0} if held else {},
        compiler_params=pltpu.CompilerParams(vmem_limit_bytes=40 * MIB),
        cost_estimate=pl.CostEstimate(flops=1, bytes_accessed=1, transcendentals=0),
        name="carried_part",
    )(read, vel_index, al, *held)


def halo_rows(refs, core, from_far, depth, blocks, put):
    swap_ref, first_ref, second_ref = refs
    ys = blocks * LANES // NZ

    @pl.loop(0, ys // 2)
    def _(y):
        at, up = rows_of(y), rows_of(y + ys // 2)
        a, b = first_ref[0, 0, at, :], second_ref[0, 0, at, :]
        put(at, jnp.where(from_far, jnp.where(core == 0, a, b), swap_ref[0, depth, at, :]))
        put(up, jnp.where(from_far, jnp.where(core == 0, b, a), swap_ref[0, depth, up, :]))


def near_kernel(core_ref, swap_ref, first_ref, second_ref, index_ref, al_ref, out_ref, halo, edge, scale, *, blocks):
    core = core_ref[0]
    ys = blocks * LANES // NZ

    @pl.when(pl.program_id(0) == 0)
    def _():
        for j, x in enumerate((0, SUB - 1, 1, SUB - 2, 2 * SUB - 1, SUB)):
            lane_copies(al_ref[x : x + 1, :], scale.at[j], blocks)

    upwind = Upwind(index_ref[...])

    def put(at, value):
        halo[at, :] = value

    halo_rows((swap_ref, first_ref, second_ref), core, upwind.px == (core == 0), 0, blocks, put)

    def scaled(pair, at):
        return jnp.where(upwind.px, scale[2 * pair, at, :], scale[2 * pair + 1, at, :])

    def start(first):
        for j in range(RUN):
            at = rows_of(first + j)
            value = scaled(0, at) * upwind.ax * halo[at, :]
            edge[at, :] = value
            out_ref[0, 1, at, :] = scaled(1, at) * upwind.ax * value

    each_run(ys, start)

    def run(first):
        inside = upwind.across(run_of(lambda y: edge[rows_of(y), :], first, ys))
        beyond = upwind.across(run_of(lambda y: halo[rows_of(y), :], first, ys))
        for j in range(RUN):
            at = rows_of(first + j)
            near = scaled(0, at)
            far = near * upwind.ax * scaled(2, at)
            out_ref[0, 0, at, :] = near * inside[j] + far * beyond[j]
            out_ref[0, 2, at, :] = far * upwind.ax

    each_run(ys, run)


def inflow_specs(cells):
    narrow = pl.BlockSpec((1, 1, cells // 2, LANES), lambda i: (i, 0, 0, 0))
    return [
        pl.BlockSpec(memory_space=pltpu.SMEM),
        pl.BlockSpec((1, 2, cells, LANES), lambda i: (i, 0, 0, 0)),
        narrow,
        narrow,
        pl.BlockSpec((3, LANES), lambda i: (0, i)),
    ]


def inflow_near(core, swap, first, second, vel_index, al16, vels, blocks):
    cells = blocks * LANES
    return pl.pallas_call(
        functools.partial(near_kernel, blocks=blocks),
        grid=(vels // LANES,),
        in_specs=inflow_specs(cells) + [pl.BlockSpec((2 * SUB, cells), lambda i: (0, 0))],
        out_specs=pl.BlockSpec((1, 3, cells, LANES), lambda i: (i, 0, 0, 0)),
        out_shape=pltpu.HBM((vels // LANES, 3, cells, LANES), jnp.float32),
        scratch_shapes=[
            pltpu.VMEM((cells, LANES), jnp.float32),
            pltpu.VMEM((cells, LANES), jnp.float32),
            pltpu.VMEM((6, cells, LANES), jnp.float32),
        ],
        compiler_params=pltpu.CompilerParams(vmem_limit_bytes=16 * MIB),
        cost_estimate=pl.CostEstimate(flops=1, bytes_accessed=1, transcendentals=0),
        name="inflow_near",
    )(core, swap, first, second, vel_index, al16)


def small_call(kernel, outs, name, specs, args, scratch=(), limit=16):
    vmem = pl.BlockSpec(memory_space=pltpu.VMEM)
    smem = pl.BlockSpec(memory_space=pltpu.SMEM)
    return pl.pallas_call(
        kernel,
        in_specs=[smem if s == "s" else vmem for s in specs],
        out_specs=[vmem] * len(outs),
        out_shape=[jax.ShapeDtypeStruct(o, jnp.float32) for o in outs],
        scratch_shapes=list(scratch),
        compiler_params=pltpu.CompilerParams(vmem_limit_bytes=limit * MIB),
        name=name,
    )(*args)


def pair_kernel(*refs):
    parts, (near_ref, far_ref) = refs[:-2], refs[-2:]
    value = parts[0][...]
    for part in parts[1:]:
        value = value + part[...]
    near_ref[...] = value[0:PAY]
    far_ref[...] = value[PAY:]


def total_kernel(*refs):
    parts, (all_ref, up_ref, down_ref) = refs[:-3], refs[-3:]
    value = parts[0][...]
    for part in parts[1:]:
        value = value + part[...]
    all_ref[...] = value
    up_ref[...] = value[UP:DOWN]
    down_ref[...] = value[M1:AA]


def mix(inverse, values):
    return [sum(inverse[k, j] * values[j] for j in range(MOM)) for k in range(MOM)]


def chunk_kernel(inv_ref, own_ref, low_ref, high_ref, send_ref):
    plane = lax.broadcasted_iota(jnp.int32, (SUB, LANES), 0)
    inverse = {(k, j): inv_ref[k, j] for k in range(MOM) for j in range(MOM)}
    inner, outer, later = [], [], []
    for m in range(MOM):

        def row(ref, at):
            return ref[at : at + 1, :]

        first = own_ref[M1 + m * SUB : M1 + (m + 1) * SUB, :]
        second = own_ref[AA + m * SUB : AA + (m + 1) * SUB, :]
        low = low_ref[M1 + m * SUB : M1 + (m + 1) * SUB, :]
        high = high_ref[m * SUB : (m + 1) * SUB, :]
        below = DOWN - M1 + m
        inner.append(
            first + jnp.where(plane == 0, row(low_ref, m), 0.0) + jnp.where(plane == SUB - 1, row(high_ref, below), 0.0)
        )
        outer.append(
            jnp.where(plane < SUB // 2, high, low)
            + jnp.where(plane == 0, row(own_ref, UP + m), 0.0)
            + jnp.where(plane == SUB - 1, row(own_ref, DOWN + m), 0.0)
        )
        later.append(
            second
            + jnp.where(plane == 0, row(low_ref, MOM + m), 0.0)
            + jnp.where(plane == 1, row(low_ref, 2 * MOM + m), 0.0)
            + jnp.where(plane == SUB - 1, row(high_ref, below + MOM), 0.0)
            + jnp.where(plane == SUB - 2, row(high_ref, below + 2 * MOM), 0.0)
        )
    local, around = mix(inverse, inner), mix(inverse, outer)
    for n in range(4):
        send_ref[n * 16 : n * 16 + SUB, :] = local[n + 1]
        send_ref[n * 16 + SUB : (n + 1) * 16, :] = around[n + 1]
        send_ref[MOVED + n * SUB : MOVED + (n + 1) * SUB, :] = inner[n + 1]
    for n, k in enumerate(STILL):
        send_ref[FIXED + n * SUB : FIXED + (n + 1) * SUB, :] = local[k]
        send_ref[EDGE + n : EDGE + n + 1, :] = around[k][0:1]
        send_ref[EDGE + 4 + n : EDGE + 5 + n, :] = around[k][SUB - 1 :]
    for m in range(MOM):
        send_ref[LATER + m * SUB : LATER + (m + 1) * SUB, :] = later[m]
    send_ref[SQUARE:SENT, :] = sum((local[m] - inner[m]) ** 2 for m in range(MOM) if not 1 <= m <= 4)


def sweeps(source):
    rows = source.shape[0]
    field = source
    for _ in range(SWEEPS):
        beside = pltpu.roll(field, 1, axis=0) + pltpu.roll(field, rows - 1, axis=0)
        beside = beside + roll_y(field, 1) + roll_y(field, -1) + roll_z(field, 1) + roll_z(field, -1)
        field = (source + coupling * beside) * (1.0 / (1.0 + 6.0 * coupling))
    return field


def fields_kernel(place_ref, inv_ref, cst_ref, *refs, blocks):
    parts = refs[:blocks]
    h1_ref, later_ref, next_ref, up_ref, down_ref, norm_ref, whole = refs[blocks:]
    mine = place_ref[0]
    for k in range(blocks):
        whole[jnp.bitwise_xor(mine, k)] = parts[k][...]

    def rows(first, count):
        return jnp.concatenate([whole[k, first : first + count, :] for k in range(blocks)], axis=1)

    def fold(value):
        return sum(value[:, k * LANES : (k + 1) * LANES] for k in range(blocks))

    square = sum(whole[k, SQUARE:SENT, :] for k in range(blocks))
    al = cst_ref[0, 0:SUB, :]
    edges = rows(EDGE, SUB)
    plane = lax.broadcasted_iota(jnp.int32, al.shape, 0)
    moved = []
    for n, m in enumerate(PICK):
        if 1 <= m <= 4:
            value = sweeps(rows((m - 1) * 16, 16))
            square = square + fold((value[0:SUB] - rows(MOVED + (m - 1) * SUB, SUB)) ** 2)
        else:
            k = STILL.index(m)
            around = jnp.where(
                plane == 0, edges[k : k + 1], jnp.where(plane == SUB - 1, edges[4 + k : 5 + k], 0.0)
            )
            value = jnp.concatenate([rows(FIXED + k * SUB, SUB), around], axis=0)
        given = cst_ref[1 if n in (0, 4) else 2] * value
        inside = given[0:SUB]
        shifted = [
            inside,
            pltpu.roll(given, 1, axis=0)[0:SUB],
            pltpu.roll(given, 2 * SUB - 1, axis=0)[0:SUB],
            roll_y(inside, 1),
            roll_y(inside, -1),
            roll_z(inside, 1),
            roll_z(inside, -1),
        ]
        for s in range(SETS):
            value = al * shifted[s]
            for k in range(blocks):
                first = (s * 8 + n) * SUB
                h1_ref[k, first : first + SUB, :] = value[:, k * LANES : (k + 1) * LANES]
        moved.append(shifted)
    norm_ref[...] = square

    matrices = stream_matrices()
    moments = []
    for m in range(MOM):
        value = rows(LATER + m * SUB, SUB)
        for s in range(SETS):
            for n in range(8):
                factor = float(matrices[s, m, n])
                if factor != 0.0:
                    value = value + factor * moved[n][s]
        later_ref[m * SUB : (m + 1) * SUB, :] = value
        moments.append(value)
    inverse = {(k, j): inv_ref[k, j] for k in range(MOM) for j in range(MOM)}
    for m, value in enumerate(mix(inverse, moments)):
        next_ref[m * SUB : (m + 1) * SUB, :] = value
        if 1 <= m <= 4:
            up_ref[(m - 1) * 4 : m * 4, :] = value[SUB // 2 :]
            down_ref[(m - 1) * 4 : m * 4, :] = value[: SUB // 2]


def last_kernel(
    place_ref, cst_ref, later_ref, next_ref, low_ref, high_ref, norm1_ref, h2_ref, out_ref, norm_ref, wide, *, blocks
):
    mine = place_ref[0]
    square = jnp.zeros((SUB, LANES), jnp.float32)
    for m in range(MOM):
        value = next_ref[m * SUB : (m + 1) * SUB, :]
        if 1 <= m <= 4:
            at = slice((m - 1) * 4, m * 4)
            value = sweeps(jnp.concatenate([value, high_ref[at, :], low_ref[at, :]], axis=0))[0:SUB]
        off = (value - later_ref[m * SUB : (m + 1) * SUB, :]) ** 2
        for k in range(blocks):
            wide[m, k] = value[:, k * LANES : (k + 1) * LANES]
            square = square + off[:, k * LANES : (k + 1) * LANES]
        out_ref[m] = wide[m, mine]
        if m in PICK:
            n = PICK.index(m)
            given = cst_ref[1 if n in (0, 4) else 2, 0:SUB, :] * value
            for k in range(blocks):
                h2_ref[k, n * SUB : (n + 1) * SUB, :] = given[:, k * LANES : (k + 1) * LANES]
    norm_ref[0:1, :] = jnp.sum(norm1_ref[...], axis=0, keepdims=True)
    norm_ref[1:2, :] = jnp.sum(square, axis=0, keepdims=True)


def finish_kernel(
    core_ref, carried_ref, inflow_ref, swap_ref, first_ref, second_ref, h1_ref, h2_ref, index_ref, out_ref,
    rows, fields, table, far, *, blocks
):
    group = pl.program_id(0)

    @pl.when(group == 0)
    def _():
        speed = [speed_range * (2.0 * index_ref[a : a + 1, :].astype(jnp.float32) + 1.0 - NVX) / NVX for a in range(3)]
        for n, row in enumerate(functions_of(*speed)[1]):
            table[n : n + 1, :] = row
        base = table[...]
        speeds = []
        for c in speed:
            speeds.append(jnp.where(c > 0, time_step * c, 0.0))
            speeds.append(jnp.where(c < 0, -time_step * c, 0.0))
        full = jnp.concatenate([base * (1.0 - sum(speeds))] + [base * s for s in speeds] + [base], axis=0)
        high = full.astype(jnp.bfloat16).astype(jnp.float32)
        stacked = jnp.concatenate([high, high, full - high, jnp.zeros_like(full)], axis=0).astype(jnp.bfloat16)
        for g in range(rows.shape[0]):
            rows[g] = stacked[:, g * LANES : (g + 1) * LANES]
        left = lax.broadcasted_iota(jnp.int32, (LANES, LANES), 1) < LANES // 2

        @pl.loop(0, blocks)
        def _(k):
            at = pl.ds(pl.multiple_of(k * LANES, LANES), LANES)
            for x in range(SUB):
                first = h1_ref[k, pl.ds(x, SETS * 8, stride=SUB), :]
                second = h2_ref[k, pl.ds(x, 8, stride=SUB), :]
                value = jnp.concatenate([first, second, first, second], axis=0).T
                high = value.astype(jnp.bfloat16).astype(jnp.float32)
                fields[x, at, 0:LANES] = jnp.where(left, high, value - high).astype(jnp.bfloat16)
                fields[x, at, LANES:] = jnp.where(left, high, 0.0).astype(jnp.bfloat16)

    out = out_ref.reshape(LANES * blocks * SUB, LANES)
    here = index_ref[0:1, pl.ds(pl.multiple_of(group * LANES, LANES), LANES)]
    px = here * 2 >= NVX
    core = core_ref[0]

    def put(at, value):
        far[at, :] = inflow_ref[0, 0, at, :] + inflow_ref[0, 2, at, :] * value

    from_far = jnp.broadcast_to(px, (NZ, LANES)) == (core == 0)
    halo_rows((swap_ref, first_ref, second_ref), core, from_far, 0, blocks, put)
    inflow = (lambda: far[...], lambda: inflow_ref[0, 1])
    for x in range(SUB):
        value = carried_ref[0, x] + jnp.dot(fields[x], rows[group], preferred_element_type=jnp.float32)
        if x in (0, 1):
            value = value + jnp.where(px, inflow[x](), 0.0)
        elif x in (SUB - 2, SUB - 1):
            value = value + jnp.where(px, 0.0, inflow[SUB - 1 - x]())
        for k in range(blocks):
            out[pl.ds(k * SUB + x, LANES, stride=blocks * SUB), :] = value[k * LANES : (k + 1) * LANES].T


def finish(core, carried_part, inflow_part, swap, first, second, h1, h2, vel_index, vels, blocks):
    cells = blocks * LANES
    groups = vels // LANES
    vmem = pl.BlockSpec(memory_space=pltpu.VMEM)
    return pl.pallas_call(
        functools.partial(finish_kernel, blocks=blocks),
        grid=(groups,),
        in_specs=[
            pl.BlockSpec(memory_space=pltpu.SMEM),
            pl.BlockSpec((1, SUB, cells, LANES), lambda g: (g, 0, 0, 0)),
            pl.BlockSpec((1, 3, cells, LANES), lambda g: (g, 0, 0, 0)),
            pl.BlockSpec((1, 1, cells, LANES), lambda g: (g, 1, 0, 0)),
            pl.BlockSpec((1, 1, cells // 2, LANES), lambda g: (g, 0, 0, 0)),
            pl.BlockSpec((1, 1, cells // 2, LANES), lambda g: (g, 0, 0, 0)),
            vmem,
            vmem,
            vmem,
        ],
        out_specs=pl.BlockSpec((LANES, blocks, SUB, LANES), lambda g: (g, 0, 0, 0)),
        out_shape=jax.ShapeDtypeStruct((vels, blocks, SUB, LANES), jnp.float32),
        scratch_shapes=[
            pltpu.VMEM((groups, 256, LANES), jnp.bfloat16),
            pltpu.VMEM((SUB, cells, 256), jnp.bfloat16),
            pltpu.VMEM((8, vels), jnp.float32),
            pltpu.VMEM((cells, LANES), jnp.float32),
        ],
        compiler_params=pltpu.CompilerParams(vmem_limit_bytes=40 * MIB),
        cost_estimate=pl.CostEstimate(
            flops=2 * 256 * vels * blocks * SUB * LANES, bytes_accessed=8 * vels * blocks * SUB * LANES, transcendentals=0
        ),
        name="finish_dist",
    )(core, carried_part, inflow_part, swap, first, second, h1, h2, vel_index)


def ring(axis, step):
    size = lax.axis_size(axis)
    return [(i, (i + step) % size) for i in range(size)]


def shards(dist, vel_index, relax, wall_mask, macro_inverse):
    vels, width, cells = dist.shape
    blocks = cells // LANES
    peers, slabs = lax.axis_size("vel"), lax.axis_size("space")
    assert width == SUB and peers % blocks == 0 and slabs == 4 and blocks % 2 == 0
    sub = peers // blocks
    me = lax.axis_index("vel")
    place = (me // sub).astype(jnp.int32).reshape(1)
    core = (lax.axis_index("space") % 2).astype(jnp.int32).reshape(1)

    flat = dist.reshape(vels, width, blocks, LANES).transpose(0, 2, 1, 3).reshape(vels * blocks * width, LANES)
    speed = speed_range * (2.0 * vel_index.astype(jnp.float32) + 1.0 - NVX) / NVX

    wall = wall_mask > 0
    coefficients = jnp.stack(
        [
            jnp.where(wall, 0.0, 1.0 - relax),
            jnp.where(wall, 1.0, relax),
            jnp.where(wall, 0.0, relax),
        ],
        0,
    )
    from_low = lax.ppermute(coefficients[:, SUB - 1 :], "space", ring("space", 1))
    from_high = lax.ppermute(coefficients[:, :1], "space", ring("space", -1))

    leaving, read = first_stream(flat, vel_index, vels, blocks)
    (leaving, from_low, from_high) = lax.optimization_barrier((leaving, from_low, from_high))
    swap = lax.ppermute(leaving, "space", [(i, i ^ 1) for i in range(slabs)])
    cst = jnp.concatenate(
        [coefficients, from_high, jnp.zeros((3, SUB - 2, cells), jnp.float32), from_low], 1
    )

    parts = both_moments(place, read, leaving, vel_index, cst, vels, blocks)
    (swap, parts) = lax.optimization_barrier((swap, parts))

    half = cells // 2
    start = core[0] * half
    mine = lax.dynamic_slice_in_dim(leaving, start, half, 2)
    other = lax.dynamic_slice_in_dim(swap, start, half, 2)
    plus = speed[0].reshape(vels // LANES, 1, 1, LANES) > 0
    across = jnp.where(plus == (core[0] == 1), mine, other)
    (across, parts) = lax.optimization_barrier((across, parts))
    over = [(i, i ^ 2) for i in range(slabs)]
    first = [lax.ppermute(across[:, 0:1], "space", over)]

    def beside(step):
        return [(i, (i // sub ^ step) * sub + i % sub) for i in range(peers)]

    spans = [(0, vels)] if vels < 2 * LANES else [(0, vels // 2), (vels // 2, vels - vels // 2)]

    got = [parts[0]] + [lax.ppermute(parts[k], "vel", beside(k)) for k in range(1, blocks // 2)]
    carried_part = carried(read, vel_index, coefficients[0], *spans[0], blocks)
    (got[1], carried_part) = lax.optimization_barrier((got[1], carried_part))
    near, far = small_call(pair_kernel, [(PAY, LANES)] * 2, "sum_near", "v" * len(got), got)
    got = [near, lax.ppermute(far, "vel", beside(blocks // 2))]
    if len(spans) > 1:
        (al, _) = lax.optimization_barrier((coefficients[0], near))
        carried_part = carried(read, vel_index, al, *spans[1], blocks, carried_part)
        (got[1], carried_part) = lax.optimization_barrier((got[1], carried_part))
    if sub > 1:
        part = sum(got)
        got = [part]
        for k in range(1, sub):
            pairs = [(i, i // sub * sub + (i % sub + k) % sub) for i in range(peers)]
            got.append(lax.ppermute(part, "vel", pairs))
    chunk, up, down = small_call(
        total_kernel, [(PAY, LANES), (DOWN - UP, LANES), (AA - M1, LANES)], "sum_moments", "v" * len(got), got
    )
    (first[0], up, down) = lax.optimization_barrier((first[0], up, down))
    low = lax.ppermute(up, "space", ring("space", 1))
    high = lax.ppermute(down, "space", ring("space", -1))
    (send,) = small_call(
        chunk_kernel, [(SENT, LANES)], "local_fields", "svvv", (macro_inverse, chunk, low, high)
    )
    pieces = [send] + [lax.ppermute(send, "vel", beside(k)) for k in range(1, blocks // 2 + 1)]
    across1, send = lax.optimization_barrier((across[:, 1:2], send))
    first.append(lax.ppermute(across1, "space", over))
    swap_chip = [(i, i ^ 1) for i in range(slabs)]
    second = [lax.ppermute(first[0], "space", swap_chip)]
    (second[0], send) = lax.optimization_barrier((second[0], send))
    inflow_part = inflow_near(core, swap, first[0], second[0], vel_index, cst[0], vels, blocks)
    (pieces[blocks // 2], inflow_part) = lax.optimization_barrier((pieces[blocks // 2], inflow_part))
    pieces += [lax.ppermute(pieces[blocks // 2], "vel", beside(k)) for k in range(1, blocks // 2)]

    h1, later, following, up2, down2, norm1 = small_call(
        functools.partial(fields_kernel, blocks=blocks),
        [
            (blocks, SETS * 8 * SUB, LANES),
            (MOM * SUB, cells),
            (MOM * SUB, cells),
            (16, cells),
            (16, cells),
            (SUB, LANES),
        ],
        "first_fields",
        "ssv" + "v" * blocks,
        (place, macro_inverse, cst, *pieces),
        [pltpu.VMEM((blocks, SENT, LANES), jnp.float32)],
        10,
    )
    (first[1], up2) = lax.optimization_barrier((first[1], up2))
    second.append(lax.ppermute(first[1], "space", swap_chip))
    low2 = lax.ppermute(up2, "space", ring("space", 1))
    high2 = lax.ppermute(down2, "space", ring("space", -1))
    h2, owned, squares = small_call(
        functools.partial(last_kernel, blocks=blocks),
        [(blocks, 8 * SUB, LANES), (MOM, SUB, LANES), (2, LANES)],
        "last_fields",
        "svvvvvv",
        (place, cst, later, following, low2, high2, norm1),
        [pltpu.VMEM((MOM, blocks, SUB, LANES), jnp.float32)],
        10,
    )

    around = [lax.ppermute(squares, "space", ring("space", k)) for k in range(1, slabs)]
    (second[1], h2) = lax.optimization_barrier((second[1], h2))
    if sub > 1:
        owned = lax.dynamic_slice_in_dim(owned, (me % sub) * (LANES // sub), LANES // sub, 2)

    out = finish(
        core, carried_part, inflow_part, swap, first[1], second[1], h1, h2, vel_index, vels, blocks
    )
    (around[0], out) = lax.optimization_barrier((around[0], out))
    slab = lax.axis_index("space")
    every = [squares] + around
    ordered = [
        functools.reduce(lambda a, k: jnp.where((slab - k) % slabs == j, every[k], a), range(1, slabs), every[0])
        for j in range(slabs)
    ]
    norms = jnp.sqrt(jnp.sum(sum(ordered), axis=1))
    out = out.transpose(0, 2, 1, 3).reshape(vels, width, cells)
    return (out, owned, norms)


def solution(mesh):
    return jax.shard_map(
        shards,
        mesh=mesh,
        in_specs=(P("vel", "space", None), P(None, "vel"), P("space", None), P("space", None), P()),
        out_specs=(P("vel", "space", None), P(None, "space", "vel"), P()),
        check_vma=False,
    )
```

```python
import functools
import math

import jax
import jax.numpy as jnp
import numpy as np
from jax import lax
from jax.experimental import pallas as pl
from jax.experimental.pallas import tpu as pltpu
from jax.sharding import PartitionSpec as P

NVX = 16
NZ = 16
MOM = 13
SWEEPS = 3
LANES = 128
SUB = 8
SETS = 7
PICK = (0, 1, 2, 3, 4, 10, 11, 12)

speed_range = 4.0
time_step = 0.08
coupling = 0.5
MIB = 2**20
PIECES = 8
RUN = 16
PAD = 8

UP, M1, DOWN, AA, PAY = 0, 40, 144, 184, 288
STILL = (0, 10, 11, 12)
MOVED, FIXED, EDGE, LATER, SQUARE, SENT = 64, 96, 128, 136, 240, 248


def functions_of(cx, cy, cz):
    square = cx * cx + cy * cy + cz * cz
    heat = square - 2.5
    one = cx * 0.0 + 1.0
    rows = [
        one, cx, cy, cz, 2.0 * square / 3.0 - 1.0, 2.0 * cx * cy, 2.0 * cx * cz, 2.0 * cy * cz,
        cx * cx - cy * cy, cy * cy - cz * cz, cx * heat, cy * heat, cz * heat,
    ]
    factor = 4.0 / 15.0
    shakhov = [
        one, 2.0 * cx, 2.0 * cy, 2.0 * cz, square - 1.5,
        factor * cx * heat, factor * cy * heat, factor * cz * heat,
    ]
    return rows, shakhov, square


def half_speeds(cx, cy, cz):
    out = []
    for c in (cx, cy, cz):
        out.append(time_step * c * (c > 0))
        out.append(-time_step * c * (c < 0))
    return out


@functools.lru_cache(None)
def stream_matrices():
    line = speed_range * (2.0 * np.arange(NVX) + 1.0 - NVX) / NVX
    cx, cy, cz = (g.reshape(-1) for g in np.meshgrid(line, line, line, indexing="ij"))
    rows, shakhov, square = functions_of(cx, cy, cz)
    weight = (2.0 * speed_range / NVX) ** 3 * math.pi ** (-1.5) * np.exp(-square)
    rows = np.stack(rows) * weight
    shakhov = np.stack(shakhov)
    speeds = half_speeds(cx, cy, cz)
    stay = 1.0 - sum(speeds)
    out = np.stack([(rows * s) @ shakhov.T for s in [stay] + speeds])
    out[np.abs(out) < 1e-13] = 0.0
    return out


def split(value):
    high = value.astype(jnp.bfloat16)
    low = (value - high.astype(jnp.float32)).astype(jnp.bfloat16)
    return high, low


def speeds_at(index):
    speed = speed_range * (2.0 * index.astype(jnp.float32) + 1.0 - NVX) / NVX
    return [time_step * speed[a : a + 1] for a in range(3)]


class Upwind:
    def __init__(self, index):
        tx, ty, tz = speeds_at(index)
        shape = (NZ, LANES)
        self.ax, self.ay, self.az = (jnp.broadcast_to(jnp.abs(t), shape) for t in (tx, ty, tz))
        self.stay = 1.0 - self.ax - self.ay - self.az
        self.px, self.py, self.pz = (jnp.broadcast_to(t, shape) > 0 for t in (tx, ty, tz))

    def across(self, rows):
        out = []
        for before, here, after in zip(rows[:-2], rows[1:-1], rows[2:]):
            in_y = jnp.where(self.py, before, after)
            in_z = jnp.where(self.pz, pltpu.roll(here, 1, axis=0), pltpu.roll(here, NZ - 1, axis=0))
            out.append(self.stay * here + self.ay * in_y + self.az * in_z)
        return out

    def stream(self, ref, x, first, count):
        mid = self.across(run_of(lambda y: ref[x + 1, rows_of(y), :], first, count))
        out = []
        for j, value in enumerate(mid):
            at = rows_of(first + j)
            out.append(value + self.ax * jnp.where(self.px, ref[x, at, :], ref[x + 2, at, :]))
        return out


def run_of(read, first, count):
    ends = [lax.rem(first + count - 1, count), lax.rem(first + RUN, count)]
    return [read(ends[0])] + [read(first + j) for j in range(RUN)] + [read(ends[1])]


def rows_of(y):
    return pl.ds(pl.multiple_of(y * NZ, NZ), NZ)


def each_run(count, body):
    @pl.loop(0, count // RUN)
    def _(i):
        body(i * RUN)


def lane_copies(ref_row, target, blocks):
    for k in range(blocks):
        at = slice(k * LANES, (k + 1) * LANES)
        target[at, :] = jnp.broadcast_to(ref_row[:, at], (LANES, LANES)).T


def roll_y(value, sign):
    cells = value.shape[1]
    return pltpu.roll(value, NZ if sign > 0 else cells - NZ, axis=1)


def roll_z(value, sign):
    cells = value.shape[1]
    zl = lax.broadcasted_iota(jnp.int32, value.shape, 1) & (NZ - 1)
    if sign > 0:
        return jnp.where(zl == 0, pltpu.roll(value, cells - (NZ - 1), axis=1), pltpu.roll(value, 1, axis=1))
    return jnp.where(zl == NZ - 1, pltpu.roll(value, NZ - 1, axis=1), pltpu.roll(value, cells - 1, axis=1))


def stream_kernel(dist_ref, index_ref, leaving_ref, read_ref, held, even, odd, done, sems, out_sems, *, vels, blocks):
    stride = blocks * SUB
    chunks = vels // LANES
    piece = LANES // PIECES
    pitch = stride + PAD
    ys = blocks * LANES // NZ
    flat = held.reshape(2 * LANES * pitch, LANES)

    def fetch(c):
        return [
            pltpu.make_async_copy(
                dist_ref.at[pl.ds(c * LANES + p * piece, piece)],
                held.at[c % 2, pl.ds(p * piece, piece), pl.ds(0, stride)],
                sems.at[c % 2, p],
            )
            for p in range(PIECES)
        ]

    def store(c):
        return pltpu.make_async_copy(done.at[c % 2], read_ref.at[c], out_sems.at[c % 2])

    def turn(c, k):
        target = odd if c % 2 else even
        for x in range(SUB):
            value = flat[pl.ds((c % 2) * LANES * pitch + k * SUB + x, LANES, stride=pitch), :]
            target[x + 1, pl.ds(pl.multiple_of(k * LANES, LANES), LANES), :] = value.T

    for c in range(min(2, chunks)):
        for copy in fetch(c):
            copy.start()
    empty = jnp.zeros((ys * NZ, LANES), jnp.float32)
    for ref in (even, odd):
        ref[0] = empty
        ref[SUB + 1] = empty
    for copy in fetch(0):
        copy.wait()

    @pl.loop(0, blocks)
    def _(k):
        turn(0, k)

    for c in range(chunks):
        turned = odd if c % 2 else even
        if c + 2 < chunks:
            for copy in fetch(c + 2):
                copy.start()
        if c + 1 < chunks:
            for copy in fetch(c + 1):
                copy.wait()
        if c >= 2:
            store(c - 2).wait()
        upwind = Upwind(index_ref[:, c * LANES : (c + 1) * LANES])

        @pl.loop(0, SUB)
        def _(x, upwind=upwind, c=c, turned=turned):
            if c + 1 < chunks and blocks == SUB:
                turn(c + 1, x)
            for first in range(0, ys, RUN):
                for j, value in enumerate(upwind.stream(turned, x, first, ys)):
                    done[c % 2, x, rows_of(first + j), :] = value

        if c + 1 < chunks and blocks != SUB:

            @pl.loop(0, blocks)
            def _(k, c=c):
                turn(c + 1, k)

        def edges(first, upwind=upwind, c=c, turned=turned):
            for j in range(RUN):
                at = rows_of(first + j)
                bottom, top = turned[1, at, :], turned[SUB, at, :]
                leaving_ref[c, 0, at, :] = jnp.where(upwind.px, top, bottom)
                leaving_ref[c, 1, at, :] = jnp.where(upwind.px, turned[SUB - 1, at, :], turned[2, at, :])

        each_run(ys, edges)
        store(c).start()
    for c in range(max(0, chunks - 2), chunks):
        store(c).wait()


def first_stream(flat, vel_index, vels, blocks):
    cells = blocks * LANES
    anywhere = pl.BlockSpec(memory_space=pl.ANY)
    vmem = pl.BlockSpec(memory_space=pltpu.VMEM)
    return pl.pallas_call(
        functools.partial(stream_kernel, vels=vels, blocks=blocks),
        in_specs=[anywhere, vmem],
        out_specs=[vmem, anywhere],
        out_shape=[
            jax.ShapeDtypeStruct((vels // LANES, 2, cells, LANES), jnp.float32),
            jax.ShapeDtypeStruct((vels // LANES, SUB, cells, LANES), jnp.float32),
        ],
        scratch_shapes=[
            pltpu.VMEM((2, LANES, blocks * SUB + PAD, LANES), jnp.float32),
            pltpu.VMEM((SUB + 2, cells, LANES), jnp.float32),
            pltpu.VMEM((SUB + 2, cells, LANES), jnp.float32),
            pltpu.VMEM((2, SUB, cells, LANES), jnp.float32),
            pltpu.SemaphoreType.DMA((2, PIECES)),
            pltpu.SemaphoreType.DMA((2,)),
        ],
        compiler_params=pltpu.CompilerParams(vmem_limit_bytes=54 * MIB),
        cost_estimate=pl.CostEstimate(
            flops=20 * vels * SUB * cells, bytes_accessed=8 * vels * SUB * cells, transcendentals=0
        ),
        name="first_stream",
    )(flat, vel_index)


def moments_kernel(me_ref, read_ref, leaving_ref, index_ref, cst_ref, *refs, vels, blocks):
    half = blocks // 2
    outs = refs[:half]
    table, wst, acc, gacc, pay = refs[half:]
    span = SETS * 16
    step = pl.program_id(0)

    @pl.when(step == 0)
    def _():
        speed = [speed_range * (2.0 * index_ref[a : a + 1, :].astype(jnp.float32) + 1.0 - NVX) / NVX for a in range(3)]
        rows, _, square = functions_of(*speed)
        weight = (2.0 * speed_range / NVX) ** 3 * math.pi ** (-1.5) * jnp.exp(-square)
        table[...] = jnp.zeros_like(table)
        for m, row in enumerate(rows):
            table[m : m + 1, :] = row * weight
        base = table[...]
        speeds = []
        for c in speed:
            speeds.append(jnp.where(c > 0, time_step * c, 0.0))
            speeds.append(jnp.where(c < 0, -time_step * c, 0.0))
        full = jnp.concatenate([base] + [base * s for s in speeds] + [jnp.zeros_like(base)], axis=0)
        for variant, factor in enumerate([None, speeds[0], speeds[1]]):
            high, low = split((full if factor is None else full * factor).T)
            wst[variant, :, 0:LANES] = high
            wst[variant, :, LANES:] = low

    wide = 2 * LANES
    at = pl.ds(pl.multiple_of(step * wide, wide), wide)
    groups = range(vels // LANES)

    def reduced(high, low, variant):
        first = jnp.dot(high, wst[variant], preferred_element_type=jnp.float32)
        second = jnp.dot(low, wst[variant, :, 0:LANES], preferred_element_type=jnp.float32)
        return (first[:, 0:LANES] + first[:, LANES:] + second).T[0:span]

    for x in range(SUB):
        total = reduced(*split(jnp.concatenate([read_ref[g, x] for g in groups], axis=1)), 0)
        for j in range(2):
            acc[2 * step + j, pl.ds(x, span, stride=SUB), :] = total[:, j * LANES : (j + 1) * LANES]
    edge = split(jnp.concatenate([leaving_ref[g, 0] for g in groups], axis=1))
    for side in range(2):
        gacc[side, :, at] = reduced(*edge, side + 1)

    @pl.when(step == pl.num_programs(0) - 1)
    def _():
        combine_moments(me_ref, cst_ref, outs, acc, gacc, pay, blocks)


def combine_moments(me_ref, cst_ref, outs, acc, gacc, pay, blocks):
    half = blocks // 2
    al = cst_ref[0, 0:SUB, :]
    beyond = cst_ref[0, SUB : SUB + 1, :]
    below = cst_ref[0, 2 * SUB - 1 : 2 * SUB, :]
    plane = lax.broadcasted_iota(jnp.int32, al.shape, 0)

    def own(i, m):
        first = (i * 16 + m) * SUB
        return jnp.concatenate([acc[k, first : first + SUB, :] for k in range(blocks)], axis=1)

    for m in range(MOM):
        sets = [own(i, m) for i in range(SETS)]
        value = al * (sets[0] - sum(sets[1:]))
        value = value + jnp.where(plane == 0, 0.0, pltpu.roll(al * sets[1], 1, axis=0))
        value = value + jnp.where(plane == SUB - 1, 0.0, pltpu.roll(al * sets[2], SUB - 1, axis=0))
        value = value + roll_y(al * sets[3], 1) + roll_y(al * sets[4], -1)
        value = value + roll_z(al * sets[5], 1) + roll_z(al * sets[6], -1)
        for k in range(blocks):
            at = slice(k * LANES, (k + 1) * LANES)
            pay[k, M1 + m * SUB : M1 + (m + 1) * SUB, :] = sets[0][:, at]
            pay[k, AA + m * SUB : AA + (m + 1) * SUB, :] = value[:, at]

    for side, (scale, edge, toward, start) in enumerate([(beyond, SUB - 1, 1, UP), (below, 0, 2, DOWN)]):
        sets = [gacc[side, i * 16 : (i + 1) * 16, :] for i in range(SETS)]
        near = scale * (sets[0] - sum(sets[1:]))
        near = near + roll_y(scale * sets[3], 1) + roll_y(scale * sets[4], -1)
        near = near + roll_z(scale * sets[5], 1) + roll_z(scale * sets[6], -1)
        out_of = jnp.concatenate(
            [acc[k, pl.ds(toward * 16 * SUB + edge, 16, stride=SUB), :] for k in range(blocks)], axis=1
        )
        near = near + al[edge : edge + 1, :] * out_of
        far = scale * sets[toward]
        for k in range(blocks):
            at = slice(k * LANES, (k + 1) * LANES)
            for j, value in enumerate((sets[0], near, far)):
                pay[k, start + j * MOM : start + (j + 1) * MOM, :] = value[0:MOM, at]
            pay[k, start + 3 * MOM : start + 3 * MOM + 1, :] = jnp.zeros((1, LANES), jnp.float32)

    mine = me_ref[0]
    for k in range(half):
        near = jnp.bitwise_xor(mine, k)
        outs[k][0:PAY, :] = pay[near]
        outs[k][PAY:, :] = pay[jnp.bitwise_xor(near, half)]


def both_moments(place, read, leaving, vel_index, cst, vels, blocks):
    cells = blocks * LANES
    vmem = pl.BlockSpec(memory_space=pltpu.VMEM)
    span = SETS * 16
    block = pl.BlockSpec((vels // LANES, SUB, 2 * LANES, LANES), lambda i: (0, 0, i, 0))
    edge = pl.BlockSpec((vels // LANES, 1, 2 * LANES, LANES), lambda i: (0, 0, i, 0))
    return pl.pallas_call(
        functools.partial(moments_kernel, vels=vels, blocks=blocks),
        grid=(blocks // 2,),
        in_specs=[pl.BlockSpec(memory_space=pltpu.SMEM), block, edge, vmem, vmem],
        out_specs=[vmem] * (blocks // 2),
        out_shape=[jax.ShapeDtypeStruct((2 * PAY, LANES), jnp.float32)] * (blocks // 2),
        scratch_shapes=[
            pltpu.VMEM((16, vels), jnp.float32),
            pltpu.VMEM((3, vels, 2 * LANES), jnp.bfloat16),
            pltpu.VMEM((blocks, span * SUB, LANES), jnp.float32),
            pltpu.VMEM((2, span, cells), jnp.float32),
            pltpu.VMEM((blocks, PAY, LANES), jnp.float32),
        ],
        compiler_params=pltpu.CompilerParams(vmem_limit_bytes=56 * MIB),
        cost_estimate=pl.CostEstimate(
            flops=2 * 336 * vels * 10 * cells, bytes_accessed=4 * vels * 10 * cells, transcendentals=0
        ),
        name="moments_of_both",
    )(place, read, leaving, vel_index, cst)


def carried_kernel(read_ref, index_ref, al_ref, *refs, blocks):
    out_ref, mid, scale = refs[-3:]
    ys = blocks * LANES // NZ

    @pl.when(pl.program_id(0) == 0)
    def _():
        for x in range(SUB):
            lane_copies(al_ref[x : x + 1, :], scale.at[x], blocks)
        empty = jnp.zeros((ys * NZ, LANES), jnp.float32)
        mid[0] = empty
        mid[SUB + 1] = empty

    upwind = Upwind(index_ref[...])

    @pl.loop(0, SUB)
    def _(x):
        def run(first):
            for j in range(RUN):
                at = rows_of(first + j)
                mid[x + 1, at, :] = scale[x, at, :] * read_ref[0, x, at, :]

        each_run(ys, run)

    @pl.loop(0, SUB)
    def _(x):
        def run(first):
            for j, value in enumerate(upwind.stream(mid, x, first, ys)):
                at = rows_of(first + j)
                out_ref[0, x, at, :] = scale[x, at, :] * value

        each_run(ys, run)


def carried(read, vel_index, al, first, count, blocks, before=None):
    groups = read.shape[0]
    cells = blocks * LANES
    start = first // LANES
    block = pl.BlockSpec((1, SUB, cells, LANES), lambda i: (i + start, 0, 0, 0))
    held = [] if before is None else [before]
    return pl.pallas_call(
        functools.partial(carried_kernel, blocks=blocks),
        grid=(count // LANES,),
        in_specs=[
            block,
            pl.BlockSpec((3, LANES), lambda i: (0, i + start)),
            pl.BlockSpec((SUB, cells), lambda i: (0, 0)),
        ]
        + [pl.BlockSpec(memory_space=pl.ANY)] * len(held),
        out_specs=block,
        out_shape=jax.ShapeDtypeStruct((groups, SUB, cells, LANES), jnp.float32),
        scratch_shapes=[
            pltpu.VMEM((SUB + 2, cells, LANES), jnp.float32),
            pltpu.VMEM((SUB, cells, LANES), jnp.float32),
        ],
        input_output_aliases={3: 0} if held else {},
        compiler_params=pltpu.CompilerParams(vmem_limit_bytes=40 * MIB),
        cost_estimate=pl.CostEstimate(flops=1, bytes_accessed=1, transcendentals=0),
        name="carried_part",
    )(read, vel_index, al, *held)


def halo_rows(refs, core, from_far, depth, blocks, put):
    swap_ref, first_ref, second_ref = refs
    ys = blocks * LANES // NZ

    @pl.loop(0, ys // 2)
    def _(y):
        at, up = rows_of(y), rows_of(y + ys // 2)
        a, b = first_ref[0, 0, at, :], second_ref[0, 0, at, :]
        put(at, jnp.where(from_far, jnp.where(core == 0, a, b), swap_ref[0, depth, at, :]))
        put(up, jnp.where(from_far, jnp.where(core == 0, b, a), swap_ref[0, depth, up, :]))


def near_kernel(core_ref, swap_ref, first_ref, second_ref, index_ref, al_ref, out_ref, halo, edge, scale, *, blocks):
    core = core_ref[0]
    ys = blocks * LANES // NZ

    @pl.when(pl.program_id(0) == 0)
    def _():
        for j, x in enumerate((0, SUB - 1, 1, SUB - 2, 2 * SUB - 1, SUB)):
            lane_copies(al_ref[x : x + 1, :], scale.at[j], blocks)

    upwind = Upwind(index_ref[...])

    def put(at, value):
        halo[at, :] = value

    halo_rows((swap_ref, first_ref, second_ref), core, upwind.px == (core == 0), 0, blocks, put)

    def scaled(pair, at):
        return jnp.where(upwind.px, scale[2 * pair, at, :], scale[2 * pair + 1, at, :])

    def start(first):
        for j in range(RUN):
            at = rows_of(first + j)
            value = scaled(0, at) * upwind.ax * halo[at, :]
            edge[at, :] = value
            out_ref[0, 1, at, :] = scaled(1, at) * upwind.ax * value

    each_run(ys, start)

    def run(first):
        inside = upwind.across(run_of(lambda y: edge[rows_of(y), :], first, ys))
        beyond = upwind.across(run_of(lambda y: halo[rows_of(y), :], first, ys))
        for j in range(RUN):
            at = rows_of(first + j)
            near = scaled(0, at)
            far = near * upwind.ax * scaled(2, at)
            out_ref[0, 0, at, :] = near * inside[j] + far * beyond[j]
            out_ref[0, 2, at, :] = far * upwind.ax

    each_run(ys, run)


def inflow_specs(cells):
    narrow = pl.BlockSpec((1, 1, cells // 2, LANES), lambda i: (i, 0, 0, 0))
    return [
        pl.BlockSpec(memory_space=pltpu.SMEM),
        pl.BlockSpec((1, 2, cells, LANES), lambda i: (i, 0, 0, 0)),
        narrow,
        narrow,
        pl.BlockSpec((3, LANES), lambda i: (0, i)),
    ]


def inflow_near(core, swap, first, second, vel_index, al16, vels, blocks):
    cells = blocks * LANES
    return pl.pallas_call(
        functools.partial(near_kernel, blocks=blocks),
        grid=(vels // LANES,),
        in_specs=inflow_specs(cells) + [pl.BlockSpec((2 * SUB, cells), lambda i: (0, 0))],
        out_specs=pl.BlockSpec((1, 3, cells, LANES), lambda i: (i, 0, 0, 0)),
        out_shape=pltpu.HBM((vels // LANES, 3, cells, LANES), jnp.float32),
        scratch_shapes=[
            pltpu.VMEM((cells, LANES), jnp.float32),
            pltpu.VMEM((cells, LANES), jnp.float32),
            pltpu.VMEM((6, cells, LANES), jnp.float32),
        ],
        compiler_params=pltpu.CompilerParams(vmem_limit_bytes=16 * MIB),
        cost_estimate=pl.CostEstimate(flops=1, bytes_accessed=1, transcendentals=0),
        name="inflow_near",
    )(core, swap, first, second, vel_index, al16)


def small_call(kernel, outs, name, specs, args, scratch=(), limit=16):
    vmem = pl.BlockSpec(memory_space=pltpu.VMEM)
    smem = pl.BlockSpec(memory_space=pltpu.SMEM)
    return pl.pallas_call(
        kernel,
        in_specs=[smem if s == "s" else vmem for s in specs],
        out_specs=[vmem] * len(outs),
        out_shape=[jax.ShapeDtypeStruct(o, jnp.float32) for o in outs],
        scratch_shapes=list(scratch),
        compiler_params=pltpu.CompilerParams(vmem_limit_bytes=limit * MIB),
        name=name,
    )(*args)


def pair_kernel(*refs):
    parts, (near_ref, far_ref) = refs[:-2], refs[-2:]
    value = parts[0][...]
    for part in parts[1:]:
        value = value + part[...]
    near_ref[...] = value[0:PAY]
    far_ref[...] = value[PAY:]


def total_kernel(*refs):
    parts, (all_ref, up_ref, down_ref) = refs[:-3], refs[-3:]
    value = parts[0][...]
    for part in parts[1:]:
        value = value + part[...]
    all_ref[...] = value
    up_ref[...] = value[UP:DOWN]
    down_ref[...] = value[M1:AA]


def mix(inverse, values):
    return [sum(inverse[k, j] * values[j] for j in range(MOM)) for k in range(MOM)]


def chunk_kernel(inv_ref, own_ref, low_ref, high_ref, send_ref):
    plane = lax.broadcasted_iota(jnp.int32, (SUB, LANES), 0)
    inverse = {(k, j): inv_ref[k, j] for k in range(MOM) for j in range(MOM)}
    inner, outer, later = [], [], []
    for m in range(MOM):

        def row(ref, at):
            return ref[at : at + 1, :]

        first = own_ref[M1 + m * SUB : M1 + (m + 1) * SUB, :]
        second = own_ref[AA + m * SUB : AA + (m + 1) * SUB, :]
        low = low_ref[M1 + m * SUB : M1 + (m + 1) * SUB, :]
        high = high_ref[m * SUB : (m + 1) * SUB, :]
        below = DOWN - M1 + m
        inner.append(
            first + jnp.where(plane == 0, row(low_ref, m), 0.0) + jnp.where(plane == SUB - 1, row(high_ref, below), 0.0)
        )
        outer.append(
            jnp.where(plane < SUB // 2, high, low)
            + jnp.where(plane == 0, row(own_ref, UP + m), 0.0)
            + jnp.where(plane == SUB - 1, row(own_ref, DOWN + m), 0.0)
        )
        later.append(
            second
            + jnp.where(plane == 0, row(low_ref, MOM + m), 0.0)
            + jnp.where(plane == 1, row(low_ref, 2 * MOM + m), 0.0)
            + jnp.where(plane == SUB - 1, row(high_ref, below + MOM), 0.0)
            + jnp.where(plane == SUB - 2, row(high_ref, below + 2 * MOM), 0.0)
        )
    local, around = mix(inverse, inner), mix(inverse, outer)
    for n in range(4):
        send_ref[n * 16 : n * 16 + SUB, :] = local[n + 1]
        send_ref[n * 16 + SUB : (n + 1) * 16, :] = around[n + 1]
        send_ref[MOVED + n * SUB : MOVED + (n + 1) * SUB, :] = inner[n + 1]
    for n, k in enumerate(STILL):
        send_ref[FIXED + n * SUB : FIXED + (n + 1) * SUB, :] = local[k]
        send_ref[EDGE + n : EDGE + n + 1, :] = around[k][0:1]
        send_ref[EDGE + 4 + n : EDGE + 5 + n, :] = around[k][SUB - 1 :]
    for m in range(MOM):
        send_ref[LATER + m * SUB : LATER + (m + 1) * SUB, :] = later[m]
    send_ref[SQUARE:SENT, :] = sum((local[m] - inner[m]) ** 2 for m in range(MOM) if not 1 <= m <= 4)


def sweeps(source):
    rows = source.shape[0]
    field = source
    for _ in range(SWEEPS):
        beside = pltpu.roll(field, 1, axis=0) + pltpu.roll(field, rows - 1, axis=0)
        beside = beside + roll_y(field, 1) + roll_y(field, -1) + roll_z(field, 1) + roll_z(field, -1)
        field = (source + coupling * beside) * (1.0 / (1.0 + 6.0 * coupling))
    return field


def fields_kernel(place_ref, inv_ref, cst_ref, *refs, blocks):
    parts = refs[:blocks]
    h1_ref, later_ref, next_ref, up_ref, down_ref, norm_ref, whole = refs[blocks:]
    mine = place_ref[0]
    for k in range(blocks):
        whole[jnp.bitwise_xor(mine, k)] = parts[k][...]

    def rows(first, count):
        return jnp.concatenate([whole[k, first : first + count, :] for k in range(blocks)], axis=1)

    def fold(value):
        return sum(value[:, k * LANES : (k + 1) * LANES] for k in range(blocks))

    square = sum(whole[k, SQUARE:SENT, :] for k in range(blocks))
    al = cst_ref[0, 0:SUB, :]
    edges = rows(EDGE, SUB)
    plane = lax.broadcasted_iota(jnp.int32, al.shape, 0)
    moved = []
    for n, m in enumerate(PICK):
        if 1 <= m <= 4:
            value = sweeps(rows((m - 1) * 16, 16))
            square = square + fold((value[0:SUB] - rows(MOVED + (m - 1) * SUB, SUB)) ** 2)
        else:
            k = STILL.index(m)
            around = jnp.where(
                plane == 0, edges[k : k + 1], jnp.where(plane == SUB - 1, edges[4 + k : 5 + k], 0.0)
            )
            value = jnp.concatenate([rows(FIXED + k * SUB, SUB), around], axis=0)
        given = cst_ref[1 if n in (0, 4) else 2] * value
        inside = given[0:SUB]
        shifted = [
            inside,
            pltpu.roll(given, 1, axis=0)[0:SUB],
            pltpu.roll(given, 2 * SUB - 1, axis=0)[0:SUB],
            roll_y(inside, 1),
            roll_y(inside, -1),
            roll_z(inside, 1),
            roll_z(inside, -1),
        ]
        for s in range(SETS):
            value = al * shifted[s]
            for k in range(blocks):
                first = (s * 8 + n) * SUB
                h1_ref[k, first : first + SUB, :] = value[:, k * LANES : (k + 1) * LANES]
        moved.append(shifted)
    norm_ref[...] = square

    matrices = stream_matrices()
    moments = []
    for m in range(MOM):
        value = rows(LATER + m * SUB, SUB)
        for s in range(SETS):
            for n in range(8):
                factor = float(matrices[s, m, n])
                if factor != 0.0:
                    value = value + factor * moved[n][s]
        later_ref[m * SUB : (m + 1) * SUB, :] = value
        moments.append(value)
    inverse = {(k, j): inv_ref[k, j] for k in range(MOM) for j in range(MOM)}
    for m, value in enumerate(mix(inverse, moments)):
        next_ref[m * SUB : (m + 1) * SUB, :] = value
        if 1 <= m <= 4:
            up_ref[(m - 1) * 4 : m * 4, :] = value[SUB // 2 :]
            down_ref[(m - 1) * 4 : m * 4, :] = value[: SUB // 2]


def last_kernel(
    place_ref, cst_ref, later_ref, next_ref, low_ref, high_ref, norm1_ref, h2_ref, out_ref, norm_ref, wide, *, blocks
):
    mine = place_ref[0]
    square = jnp.zeros((SUB, LANES), jnp.float32)
    for m in range(MOM):
        value = next_ref[m * SUB : (m + 1) * SUB, :]
        if 1 <= m <= 4:
            at = slice((m - 1) * 4, m * 4)
            value = sweeps(jnp.concatenate([value, high_ref[at, :], low_ref[at, :]], axis=0))[0:SUB]
        off = (value - later_ref[m * SUB : (m + 1) * SUB, :]) ** 2
        for k in range(blocks):
            wide[m, k] = value[:, k * LANES : (k + 1) * LANES]
            square = square + off[:, k * LANES : (k + 1) * LANES]
        out_ref[m] = wide[m, mine]
        if m in PICK:
            n = PICK.index(m)
            given = cst_ref[1 if n in (0, 4) else 2, 0:SUB, :] * value
            for k in range(blocks):
                h2_ref[k, n * SUB : (n + 1) * SUB, :] = given[:, k * LANES : (k + 1) * LANES]
    norm_ref[0:1, :] = jnp.sum(norm1_ref[...], axis=0, keepdims=True)
    norm_ref[1:2, :] = jnp.sum(square, axis=0, keepdims=True)


def finish_kernel(
    core_ref, carried_ref, inflow_ref, swap_ref, first_ref, second_ref, h1_ref, h2_ref, index_ref, out_ref,
    rows, fields, table, far, ready, sems, *, blocks
):
    group = pl.program_id(0)

    @pl.when(group == 0)
    def _():
        speed = [speed_range * (2.0 * index_ref[a : a + 1, :].astype(jnp.float32) + 1.0 - NVX) / NVX for a in range(3)]
        for n, row in enumerate(functions_of(*speed)[1]):
            table[n : n + 1, :] = row
        base = table[...]
        speeds = []
        for c in speed:
            speeds.append(jnp.where(c > 0, time_step * c, 0.0))
            speeds.append(jnp.where(c < 0, -time_step * c, 0.0))
        full = jnp.concatenate([base * (1.0 - sum(speeds))] + [base * s for s in speeds] + [base], axis=0)
        high = full.astype(jnp.bfloat16).astype(jnp.float32)
        stacked = jnp.concatenate([high, high, full - high, jnp.zeros_like(full)], axis=0).astype(jnp.bfloat16)
        for g in range(rows.shape[0]):
            rows[g] = stacked[:, g * LANES : (g + 1) * LANES]
        left = lax.broadcasted_iota(jnp.int32, (LANES, LANES), 1) < LANES // 2

        @pl.loop(0, blocks)
        def _(k):
            at = pl.ds(pl.multiple_of(k * LANES, LANES), LANES)
            for x in range(SUB):
                first = h1_ref[k, pl.ds(x, SETS * 8, stride=SUB), :]
                second = h2_ref[k, pl.ds(x, 8, stride=SUB), :]
                value = jnp.concatenate([first, second, first, second], axis=0).T
                high = value.astype(jnp.bfloat16).astype(jnp.float32)
                fields[x, at, 0:LANES] = jnp.where(left, high, value - high).astype(jnp.bfloat16)
                fields[x, at, LANES:] = jnp.where(left, high, 0.0).astype(jnp.bfloat16)

    stride = blocks * SUB
    pitch = stride + PAD
    slot = lax.rem(group, 2)
    out = ready.reshape(2 * LANES * pitch, LANES)

    def store(g):
        side = lax.rem(g, 2)
        return pltpu.make_async_copy(
            ready.at[side, :, pl.ds(0, stride)], out_ref.at[pl.ds(g * LANES, LANES)], sems.at[side]
        )

    @pl.when(group >= 2)
    def _():
        store(group - 2).wait()

    here = index_ref[0:1, pl.ds(pl.multiple_of(group * LANES, LANES), LANES)]
    px = here * 2 >= NVX
    core = core_ref[0]

    def put(at, value):
        far[at, :] = inflow_ref[0, 0, at, :] + inflow_ref[0, 2, at, :] * value

    from_far = jnp.broadcast_to(px, (NZ, LANES)) == (core == 0)
    halo_rows((swap_ref, first_ref, second_ref), core, from_far, 0, blocks, put)
    inflow = (lambda: far[...], lambda: inflow_ref[0, 1])
    for x in range(SUB):
        value = carried_ref[0, x] + jnp.dot(fields[x], rows[group], preferred_element_type=jnp.float32)
        if x in (0, 1):
            value = value + jnp.where(px, inflow[x](), 0.0)
        elif x in (SUB - 2, SUB - 1):
            value = value + jnp.where(px, 0.0, inflow[SUB - 1 - x]())
        for k in range(blocks):
            first = slot * (LANES * pitch) + k * SUB + x
            out[pl.ds(first, LANES, stride=pitch), :] = value[k * LANES : (k + 1) * LANES].T
    store(group).start()
    last = rows.shape[0] - 1

    @pl.when(group == last)
    def _():
        if last > 0:
            store(group - 1).wait()
        store(group).wait()


def finish(core, carried_part, inflow_part, swap, first, second, h1, h2, vel_index, vels, blocks):
    cells = blocks * LANES
    groups = vels // LANES
    vmem = pl.BlockSpec(memory_space=pltpu.VMEM)
    return pl.pallas_call(
        functools.partial(finish_kernel, blocks=blocks),
        grid=(groups,),
        in_specs=[
            pl.BlockSpec(memory_space=pltpu.SMEM),
            pl.BlockSpec((1, SUB, cells, LANES), lambda g: (g, 0, 0, 0)),
            pl.BlockSpec((1, 3, cells, LANES), lambda g: (g, 0, 0, 0)),
            pl.BlockSpec((1, 1, cells, LANES), lambda g: (g, 1, 0, 0)),
            pl.BlockSpec((1, 1, cells // 2, LANES), lambda g: (g, 0, 0, 0)),
            pl.BlockSpec((1, 1, cells // 2, LANES), lambda g: (g, 0, 0, 0)),
            vmem,
            vmem,
            vmem,
        ],
        out_specs=pl.BlockSpec(memory_space=pl.ANY),
        out_shape=jax.ShapeDtypeStruct((vels, blocks * SUB, LANES), jnp.float32),
        scratch_shapes=[
            pltpu.VMEM((groups, 256, LANES), jnp.bfloat16),
            pltpu.VMEM((SUB, cells, 256), jnp.bfloat16),
            pltpu.VMEM((8, vels), jnp.float32),
            pltpu.VMEM((cells, LANES), jnp.float32),
            pltpu.VMEM((2, LANES, blocks * SUB + PAD, LANES), jnp.float32),
            pltpu.SemaphoreType.DMA((2,)),
        ],
        compiler_params=pltpu.CompilerParams(vmem_limit_bytes=40 * MIB),
        cost_estimate=pl.CostEstimate(
            flops=2 * 256 * vels * blocks * SUB * LANES, bytes_accessed=8 * vels * blocks * SUB * LANES, transcendentals=0
        ),
        name="finish_dist",
    )(core, carried_part, inflow_part, swap, first, second, h1, h2, vel_index)


def ring(axis, step):
    size = lax.axis_size(axis)
    return [(i, (i + step) % size) for i in range(size)]


def shards(dist, vel_index, relax, wall_mask, macro_inverse):
    vels, width, cells = dist.shape
    blocks = cells // LANES
    peers, slabs = lax.axis_size("vel"), lax.axis_size("space")
    assert width == SUB and peers % blocks == 0 and slabs == 4 and blocks % 2 == 0
    sub = peers // blocks
    me = lax.axis_index("vel")
    place = (me // sub).astype(jnp.int32).reshape(1)
    core = (lax.axis_index("space") % 2).astype(jnp.int32).reshape(1)

    flat = dist.reshape(vels, width, blocks, LANES).transpose(0, 2, 1, 3).reshape(vels, blocks * width, LANES)
    speed = speed_range * (2.0 * vel_index.astype(jnp.float32) + 1.0 - NVX) / NVX

    wall = wall_mask > 0
    coefficients = jnp.stack(
        [
            jnp.where(wall, 0.0, 1.0 - relax),
            jnp.where(wall, 1.0, relax),
            jnp.where(wall, 0.0, relax),
        ],
        0,
    )
    from_low = lax.ppermute(coefficients[:, SUB - 1 :], "space", ring("space", 1))
    from_high = lax.ppermute(coefficients[:, :1], "space", ring("space", -1))

    leaving, read = first_stream(flat, vel_index, vels, blocks)
    (leaving, from_low, from_high) = lax.optimization_barrier((leaving, from_low, from_high))
    swap = lax.ppermute(leaving, "space", [(i, i ^ 1) for i in range(slabs)])
    cst = jnp.concatenate(
        [coefficients, from_high, jnp.zeros((3, SUB - 2, cells), jnp.float32), from_low], 1
    )

    parts = both_moments(place, read, leaving, vel_index, cst, vels, blocks)
    (swap, parts) = lax.optimization_barrier((swap, parts))

    half = cells // 2
    start = core[0] * half
    mine = lax.dynamic_slice_in_dim(leaving, start, half, 2)
    other = lax.dynamic_slice_in_dim(swap, start, half, 2)
    plus = speed[0].reshape(vels // LANES, 1, 1, LANES) > 0
    across = jnp.where(plus == (core[0] == 1), mine, other)
    (across, parts) = lax.optimization_barrier((across, parts))
    over = [(i, i ^ 2) for i in range(slabs)]
    first = [lax.ppermute(across[:, 0:1], "space", over)]

    def beside(step):
        return [(i, (i // sub ^ step) * sub + i % sub) for i in range(peers)]

    spans = [(0, vels)] if vels < 2 * LANES else [(0, vels // 2), (vels // 2, vels - vels // 2)]

    got = [parts[0]] + [lax.ppermute(parts[k], "vel", beside(k)) for k in range(1, blocks // 2)]
    carried_part = carried(read, vel_index, coefficients[0], *spans[0], blocks)
    (got[1], carried_part) = lax.optimization_barrier((got[1], carried_part))
    near, far = small_call(pair_kernel, [(PAY, LANES)] * 2, "sum_near", "v" * len(got), got)
    got = [near, lax.ppermute(far, "vel", beside(blocks // 2))]
    if len(spans) > 1:
        (al, _) = lax.optimization_barrier((coefficients[0], near))
        carried_part = carried(read, vel_index, al, *spans[1], blocks, carried_part)
        (got[1], carried_part) = lax.optimization_barrier((got[1], carried_part))
    if sub > 1:
        part = sum(got)
        got = [part]
        for k in range(1, sub):
            pairs = [(i, i // sub * sub + (i % sub + k) % sub) for i in range(peers)]
            got.append(lax.ppermute(part, "vel", pairs))
    chunk, up, down = small_call(
        total_kernel, [(PAY, LANES), (DOWN - UP, LANES), (AA - M1, LANES)], "sum_moments", "v" * len(got), got
    )
    (first[0], up, down) = lax.optimization_barrier((first[0], up, down))
    low = lax.ppermute(up, "space", ring("space", 1))
    high = lax.ppermute(down, "space", ring("space", -1))
    (send,) = small_call(
        chunk_kernel, [(SENT, LANES)], "local_fields", "svvv", (macro_inverse, chunk, low, high)
    )
    pieces = [send] + [lax.ppermute(send, "vel", beside(k)) for k in range(1, blocks // 2 + 1)]
    across1, send = lax.optimization_barrier((across[:, 1:2], send))
    first.append(lax.ppermute(across1, "space", over))
    swap_chip = [(i, i ^ 1) for i in range(slabs)]
    second = [lax.ppermute(first[0], "space", swap_chip)]
    (second[0], send) = lax.optimization_barrier((second[0], send))
    inflow_part = inflow_near(core, swap, first[0], second[0], vel_index, cst[0], vels, blocks)
    (pieces[blocks // 2], inflow_part) = lax.optimization_barrier((pieces[blocks // 2], inflow_part))
    pieces += [lax.ppermute(pieces[blocks // 2], "vel", beside(k)) for k in range(1, blocks // 2)]

    h1, later, following, up2, down2, norm1 = small_call(
        functools.partial(fields_kernel, blocks=blocks),
        [
            (blocks, SETS * 8 * SUB, LANES),
            (MOM * SUB, cells),
            (MOM * SUB, cells),
            (16, cells),
            (16, cells),
            (SUB, LANES),
        ],
        "first_fields",
        "ssv" + "v" * blocks,
        (place, macro_inverse, cst, *pieces),
        [pltpu.VMEM((blocks, SENT, LANES), jnp.float32)],
        10,
    )
    (first[1], up2) = lax.optimization_barrier((first[1], up2))
    second.append(lax.ppermute(first[1], "space", swap_chip))
    low2 = lax.ppermute(up2, "space", ring("space", 1))
    high2 = lax.ppermute(down2, "space", ring("space", -1))
    h2, owned, squares = small_call(
        functools.partial(last_kernel, blocks=blocks),
        [(blocks, 8 * SUB, LANES), (MOM, SUB, LANES), (2, LANES)],
        "last_fields",
        "svvvvvv",
        (place, cst, later, following, low2, high2, norm1),
        [pltpu.VMEM((MOM, blocks, SUB, LANES), jnp.float32)],
        10,
    )

    around = [lax.ppermute(squares, "space", ring("space", k)) for k in range(1, slabs)]
    (second[1], h2) = lax.optimization_barrier((second[1], h2))
    if sub > 1:
        owned = lax.dynamic_slice_in_dim(owned, (me % sub) * (LANES // sub), LANES // sub, 2)

    out = finish(
        core, carried_part, inflow_part, swap, first[1], second[1], h1, h2, vel_index, vels, blocks
    )
    (around[0], out) = lax.optimization_barrier((around[0], out))
    slab = lax.axis_index("space")
    every = [squares] + around
    ordered = [
        functools.reduce(lambda a, k: jnp.where((slab - k) % slabs == j, every[k], a), range(1, slabs), every[0])
        for j in range(slabs)
    ]
    norms = jnp.sqrt(jnp.sum(sum(ordered), axis=1))
    out = out.reshape(vels, blocks, width, LANES).transpose(0, 2, 1, 3).reshape(vels, width, cells)
    return (out, owned, norms)


def solution(mesh):
    return jax.shard_map(
        shards,
        mesh=mesh,
        in_specs=(P("vel", "space", None), P(None, "vel"), P("space", None), P("space", None), P()),
        out_specs=(P("vel", "space", None), P(None, "space", "vel"), P()),
        check_vma=False,
    )
```

```python
import functools
import math

import jax
import jax.numpy as jnp
import numpy as np
from jax import lax
from jax.experimental import pallas as pl
from jax.experimental.pallas import tpu as pltpu
from jax.sharding import PartitionSpec as P

NVX = 16
NZ = 16
MOM = 13
SWEEPS = 3
LANES = 128
SUB = 8
SETS = 7
PICK = (0, 1, 2, 3, 4, 10, 11, 12)

speed_range = 4.0
time_step = 0.08
coupling = 0.5
MIB = 2**20
PIECES = 8
RUN = 16
PAD = 8

UP, M1, DOWN, AA, PAY = 0, 40, 144, 184, 288
STILL = (0, 10, 11, 12)
MOVED, FIXED, EDGE, LATER, SQUARE, SENT = 64, 96, 128, 136, 240, 248


def functions_of(cx, cy, cz):
    square = cx * cx + cy * cy + cz * cz
    heat = square - 2.5
    one = cx * 0.0 + 1.0
    rows = [
        one, cx, cy, cz, 2.0 * square / 3.0 - 1.0, 2.0 * cx * cy, 2.0 * cx * cz, 2.0 * cy * cz,
        cx * cx - cy * cy, cy * cy - cz * cz, cx * heat, cy * heat, cz * heat,
    ]
    factor = 4.0 / 15.0
    shakhov = [
        one, 2.0 * cx, 2.0 * cy, 2.0 * cz, square - 1.5,
        factor * cx * heat, factor * cy * heat, factor * cz * heat,
    ]
    return rows, shakhov, square


def half_speeds(cx, cy, cz):
    out = []
    for c in (cx, cy, cz):
        out.append(time_step * c * (c > 0))
        out.append(-time_step * c * (c < 0))
    return out


@functools.lru_cache(None)
def stream_matrices():
    line = speed_range * (2.0 * np.arange(NVX) + 1.0 - NVX) / NVX
    cx, cy, cz = (g.reshape(-1) for g in np.meshgrid(line, line, line, indexing="ij"))
    rows, shakhov, square = functions_of(cx, cy, cz)
    weight = (2.0 * speed_range / NVX) ** 3 * math.pi ** (-1.5) * np.exp(-square)
    rows = np.stack(rows) * weight
    shakhov = np.stack(shakhov)
    speeds = half_speeds(cx, cy, cz)
    stay = 1.0 - sum(speeds)
    out = np.stack([(rows * s) @ shakhov.T for s in [stay] + speeds])
    out[np.abs(out) < 1e-13] = 0.0
    return out


def split(value):
    high = value.astype(jnp.bfloat16)
    low = (value - high.astype(jnp.float32)).astype(jnp.bfloat16)
    return high, low


def speeds_at(index):
    speed = speed_range * (2.0 * index.astype(jnp.float32) + 1.0 - NVX) / NVX
    return [time_step * speed[a : a + 1] for a in range(3)]


class Upwind:
    def __init__(self, index):
        tx, ty, tz = speeds_at(index)
        shape = (NZ, LANES)
        self.ax, self.ay, self.az = (jnp.broadcast_to(jnp.abs(t), shape) for t in (tx, ty, tz))
        self.stay = 1.0 - self.ax - self.ay - self.az
        self.px, self.py, self.pz = (jnp.broadcast_to(t, shape) > 0 for t in (tx, ty, tz))

    def across(self, rows):
        out = []
        for before, here, after in zip(rows[:-2], rows[1:-1], rows[2:]):
            in_y = jnp.where(self.py, before, after)
            in_z = jnp.where(self.pz, pltpu.roll(here, 1, axis=0), pltpu.roll(here, NZ - 1, axis=0))
            out.append(self.stay * here + self.ay * in_y + self.az * in_z)
        return out

    def stream(self, ref, x, first, count):
        mid = self.across(run_of(lambda y: ref[x + 1, rows_of(y), :], first, count))
        out = []
        for j, value in enumerate(mid):
            at = rows_of(first + j)
            out.append(value + self.ax * jnp.where(self.px, ref[x, at, :], ref[x + 2, at, :]))
        return out


def run_of(read, first, count):
    ends = [lax.rem(first + count - 1, count), lax.rem(first + RUN, count)]
    return [read(ends[0])] + [read(first + j) for j in range(RUN)] + [read(ends[1])]


def rows_of(y):
    return pl.ds(pl.multiple_of(y * NZ, NZ), NZ)


def each_run(count, body):
    @pl.loop(0, count // RUN)
    def _(i):
        body(i * RUN)


def lane_copies(ref_row, target, blocks):
    for k in range(blocks):
        at = slice(k * LANES, (k + 1) * LANES)
        target[at, :] = jnp.broadcast_to(ref_row[:, at], (LANES, LANES)).T


def roll_y(value, sign):
    cells = value.shape[1]
    return pltpu.roll(value, NZ if sign > 0 else cells - NZ, axis=1)


def roll_z(value, sign):
    cells = value.shape[1]
    zl = lax.broadcasted_iota(jnp.int32, value.shape, 1) & (NZ - 1)
    if sign > 0:
        return jnp.where(zl == 0, pltpu.roll(value, cells - (NZ - 1), axis=1), pltpu.roll(value, 1, axis=1))
    return jnp.where(zl == NZ - 1, pltpu.roll(value, NZ - 1, axis=1), pltpu.roll(value, cells - 1, axis=1))


def stream_kernel(dist_ref, index_ref, leaving_ref, read_ref, held, even, odd, done, sems, out_sems, *, vels, blocks):
    stride = blocks * SUB
    chunks = vels // LANES
    piece = LANES // PIECES
    pitch = stride + PAD
    ys = blocks * LANES // NZ
    flat = held.reshape(2 * LANES * pitch, LANES)

    def fetch(c):
        return [
            pltpu.make_async_copy(
                dist_ref.at[pl.ds(c * LANES + p * piece, piece)],
                held.at[c % 2, pl.ds(p * piece, piece), pl.ds(0, stride)],
                sems.at[c % 2, p],
            )
            for p in range(PIECES)
        ]

    def store(c):
        return pltpu.make_async_copy(done.at[c % 2], read_ref.at[c], out_sems.at[c % 2])

    def turn(c, k):
        target = odd if c % 2 else even
        for x in range(SUB):
            value = flat[pl.ds((c % 2) * LANES * pitch + k * SUB + x, LANES, stride=pitch), :]
            target[x + 1, pl.ds(pl.multiple_of(k * LANES, LANES), LANES), :] = value.T

    for c in range(min(2, chunks)):
        for copy in fetch(c):
            copy.start()
    empty = jnp.zeros((ys * NZ, LANES), jnp.float32)
    for ref in (even, odd):
        ref[0] = empty
        ref[SUB + 1] = empty
    for copy in fetch(0):
        copy.wait()

    @pl.loop(0, blocks)
    def _(k):
        turn(0, k)

    for c in range(chunks):
        turned = odd if c % 2 else even
        if c + 2 < chunks:
            for copy in fetch(c + 2):
                copy.start()
        if c + 1 < chunks:
            for copy in fetch(c + 1):
                copy.wait()
        if c >= 2:
            store(c - 2).wait()
        upwind = Upwind(index_ref[:, c * LANES : (c + 1) * LANES])

        @pl.loop(0, SUB)
        def _(x, upwind=upwind, c=c, turned=turned):
            if c + 1 < chunks and blocks == SUB:
                turn(c + 1, x)
            for first in range(0, ys, RUN):
                for j, value in enumerate(upwind.stream(turned, x, first, ys)):
                    done[c % 2, x, rows_of(first + j), :] = value

        if c + 1 < chunks and blocks != SUB:

            @pl.loop(0, blocks)
            def _(k, c=c):
                turn(c + 1, k)

        def edges(first, upwind=upwind, c=c, turned=turned):
            for j in range(RUN):
                at = rows_of(first + j)
                bottom, top = turned[1, at, :], turned[SUB, at, :]
                leaving_ref[c, 0, at, :] = jnp.where(upwind.px, top, bottom)
                leaving_ref[c, 1, at, :] = jnp.where(upwind.px, turned[SUB - 1, at, :], turned[2, at, :])

        each_run(ys, edges)
        store(c).start()
    for c in range(max(0, chunks - 2), chunks):
        store(c).wait()


def first_stream(flat, vel_index, vels, blocks):
    cells = blocks * LANES
    anywhere = pl.BlockSpec(memory_space=pl.ANY)
    vmem = pl.BlockSpec(memory_space=pltpu.VMEM)
    return pl.pallas_call(
        functools.partial(stream_kernel, vels=vels, blocks=blocks),
        in_specs=[anywhere, vmem],
        out_specs=[vmem, anywhere],
        out_shape=[
            jax.ShapeDtypeStruct((vels // LANES, 2, cells, LANES), jnp.float32),
            jax.ShapeDtypeStruct((vels // LANES, SUB, cells, LANES), jnp.float32),
        ],
        scratch_shapes=[
            pltpu.VMEM((2, LANES, blocks * SUB + PAD, LANES), jnp.float32),
            pltpu.VMEM((SUB + 2, cells, LANES), jnp.float32),
            pltpu.VMEM((SUB + 2, cells, LANES), jnp.float32),
            pltpu.VMEM((2, SUB, cells, LANES), jnp.float32),
            pltpu.SemaphoreType.DMA((2, PIECES)),
            pltpu.SemaphoreType.DMA((2,)),
        ],
        compiler_params=pltpu.CompilerParams(vmem_limit_bytes=54 * MIB),
        cost_estimate=pl.CostEstimate(
            flops=20 * vels * SUB * cells, bytes_accessed=8 * vels * SUB * cells, transcendentals=0
        ),
        name="first_stream",
    )(flat, vel_index)


def moments_kernel(me_ref, read_ref, leaving_ref, index_ref, cst_ref, *refs, vels, blocks):
    half = blocks // 2
    outs = refs[:half]
    table, wst, acc, gacc, pay = refs[half:]
    span = SETS * 16
    step = pl.program_id(0)

    @pl.when(step == 0)
    def _():
        speed = [speed_range * (2.0 * index_ref[a : a + 1, :].astype(jnp.float32) + 1.0 - NVX) / NVX for a in range(3)]
        rows, _, square = functions_of(*speed)
        weight = (2.0 * speed_range / NVX) ** 3 * math.pi ** (-1.5) * jnp.exp(-square)
        table[...] = jnp.zeros_like(table)
        for m, row in enumerate(rows):
            table[m : m + 1, :] = row * weight
        base = table[...]
        speeds = []
        for c in speed:
            speeds.append(jnp.where(c > 0, time_step * c, 0.0))
            speeds.append(jnp.where(c < 0, -time_step * c, 0.0))
        full = jnp.concatenate([base] + [base * s for s in speeds] + [jnp.zeros_like(base)], axis=0)
        for variant, factor in enumerate([None, speeds[0], speeds[1]]):
            high, low = split((full if factor is None else full * factor).T)
            wst[variant, :, 0:LANES] = high
            wst[variant, :, LANES:] = low

    wide = 2 * LANES
    at = pl.ds(pl.multiple_of(step * wide, wide), wide)
    groups = range(vels // LANES)

    def reduced(high, low, variant):
        first = jnp.dot(high, wst[variant], preferred_element_type=jnp.float32)
        second = jnp.dot(low, wst[variant, :, 0:LANES], preferred_element_type=jnp.float32)
        return (first[:, 0:LANES] + first[:, LANES:] + second).T[0:span]

    for x in range(SUB):
        total = reduced(*split(jnp.concatenate([read_ref[g, x] for g in groups], axis=1)), 0)
        for j in range(2):
            acc[2 * step + j, pl.ds(x, span, stride=SUB), :] = total[:, j * LANES : (j + 1) * LANES]
    edge = split(jnp.concatenate([leaving_ref[g, 0] for g in groups], axis=1))
    for side in range(2):
        gacc[side, :, at] = reduced(*edge, side + 1)

    @pl.when(step == pl.num_programs(0) - 1)
    def _():
        combine_moments(me_ref, cst_ref, outs, acc, gacc, pay, blocks)


def combine_moments(me_ref, cst_ref, outs, acc, gacc, pay, blocks):
    half = blocks // 2
    al = cst_ref[0, 0:SUB, :]
    beyond = cst_ref[0, SUB : SUB + 1, :]
    below = cst_ref[0, 2 * SUB - 1 : 2 * SUB, :]
    plane = lax.broadcasted_iota(jnp.int32, al.shape, 0)

    def own(i, m):
        first = (i * 16 + m) * SUB
        return jnp.concatenate([acc[k, first : first + SUB, :] for k in range(blocks)], axis=1)

    for m in range(MOM):
        sets = [own(i, m) for i in range(SETS)]
        value = al * (sets[0] - sum(sets[1:]))
        value = value + jnp.where(plane == 0, 0.0, pltpu.roll(al * sets[1], 1, axis=0))
        value = value + jnp.where(plane == SUB - 1, 0.0, pltpu.roll(al * sets[2], SUB - 1, axis=0))
        value = value + roll_y(al * sets[3], 1) + roll_y(al * sets[4], -1)
        value = value + roll_z(al * sets[5], 1) + roll_z(al * sets[6], -1)
        for k in range(blocks):
            at = slice(k * LANES, (k + 1) * LANES)
            pay[k, M1 + m * SUB : M1 + (m + 1) * SUB, :] = sets[0][:, at]
            pay[k, AA + m * SUB : AA + (m + 1) * SUB, :] = value[:, at]

    for side, (scale, edge, toward, start) in enumerate([(beyond, SUB - 1, 1, UP), (below, 0, 2, DOWN)]):
        sets = [gacc[side, i * 16 : (i + 1) * 16, :] for i in range(SETS)]
        near = scale * (sets[0] - sum(sets[1:]))
        near = near + roll_y(scale * sets[3], 1) + roll_y(scale * sets[4], -1)
        near = near + roll_z(scale * sets[5], 1) + roll_z(scale * sets[6], -1)
        out_of = jnp.concatenate(
            [acc[k, pl.ds(toward * 16 * SUB + edge, 16, stride=SUB), :] for k in range(blocks)], axis=1
        )
        near = near + al[edge : edge + 1, :] * out_of
        far = scale * sets[toward]
        for k in range(blocks):
            at = slice(k * LANES, (k + 1) * LANES)
            for j, value in enumerate((sets[0], near, far)):
                pay[k, start + j * MOM : start + (j + 1) * MOM, :] = value[0:MOM, at]
            pay[k, start + 3 * MOM : start + 3 * MOM + 1, :] = jnp.zeros((1, LANES), jnp.float32)

    mine = me_ref[0]
    for k in range(half):
        near = jnp.bitwise_xor(mine, k)
        outs[k][0:PAY, :] = pay[near]
        outs[k][PAY:, :] = pay[jnp.bitwise_xor(near, half)]


def both_moments(place, read, leaving, vel_index, cst, vels, blocks):
    cells = blocks * LANES
    vmem = pl.BlockSpec(memory_space=pltpu.VMEM)
    span = SETS * 16
    block = pl.BlockSpec((vels // LANES, SUB, 2 * LANES, LANES), lambda i: (0, 0, i, 0))
    edge = pl.BlockSpec((vels // LANES, 1, 2 * LANES, LANES), lambda i: (0, 0, i, 0))
    return pl.pallas_call(
        functools.partial(moments_kernel, vels=vels, blocks=blocks),
        grid=(blocks // 2,),
        in_specs=[pl.BlockSpec(memory_space=pltpu.SMEM), block, edge, vmem, vmem],
        out_specs=[vmem] * (blocks // 2),
        out_shape=[jax.ShapeDtypeStruct((2 * PAY, LANES), jnp.float32)] * (blocks // 2),
        scratch_shapes=[
            pltpu.VMEM((16, vels), jnp.float32),
            pltpu.VMEM((3, vels, 2 * LANES), jnp.bfloat16),
            pltpu.VMEM((blocks, span * SUB, LANES), jnp.float32),
            pltpu.VMEM((2, span, cells), jnp.float32),
            pltpu.VMEM((blocks, PAY, LANES), jnp.float32),
        ],
        compiler_params=pltpu.CompilerParams(vmem_limit_bytes=56 * MIB),
        cost_estimate=pl.CostEstimate(
            flops=2 * 336 * vels * 10 * cells, bytes_accessed=4 * vels * 10 * cells, transcendentals=0
        ),
        name="moments_of_both",
    )(place, read, leaving, vel_index, cst)


def carried_kernel(read_ref, index_ref, al_ref, *refs, blocks, start, count):
    out_ref, source, ready, mid, scale, in_sems, out_sems = refs[-7:]
    ys = blocks * LANES // NZ

    def fetch(g, x):
        return pltpu.make_async_copy(read_ref.at[start + g, x], source.at[g, x], in_sems.at[g, x])

    def store(g, x):
        return pltpu.make_async_copy(ready.at[g, x], out_ref.at[start + g, x], out_sems.at[g, x])

    for g in range(count):
        for x in range(SUB):
            fetch(g, x).start()
    for x in range(SUB):
        lane_copies(al_ref[x : x + 1, :], scale.at[x], blocks)
    empty = jnp.zeros((ys * NZ, LANES), jnp.float32)
    mid[0] = empty
    mid[SUB + 1] = empty
    for g in range(count):
        upwind = Upwind(index_ref[:, (start + g) * LANES : (start + g + 1) * LANES])

        @pl.loop(0, SUB)
        def _(x, g=g):
            fetch(g, x).wait()

            def run(first):
                for j in range(RUN):
                    at = rows_of(first + j)
                    mid[x + 1, at, :] = scale[x, at, :] * source[g, x, at, :]

            each_run(ys, run)

        @pl.loop(0, SUB)
        def _(x, g=g, upwind=upwind):
            def run(first):
                for j, value in enumerate(upwind.stream(mid, x, first, ys)):
                    at = rows_of(first + j)
                    ready[g, x, at, :] = scale[x, at, :] * value

            each_run(ys, run)
            store(g, x).start()

    for g in range(count):
        for x in range(SUB):
            store(g, x).wait()


def carried(read, vel_index, al, first, vels, blocks, before=None):
    groups = read.shape[0]
    cells = blocks * LANES
    count = vels // LANES
    anywhere = pl.BlockSpec(memory_space=pl.ANY)
    vmem = pl.BlockSpec(memory_space=pltpu.VMEM)
    held = [] if before is None else [before]
    return pl.pallas_call(
        functools.partial(carried_kernel, blocks=blocks, start=first // LANES, count=count),
        in_specs=[anywhere, vmem, vmem] + [anywhere] * len(held),
        out_specs=anywhere,
        out_shape=jax.ShapeDtypeStruct((groups, SUB, cells, LANES), jnp.float32),
        scratch_shapes=[
            pltpu.VMEM((count, SUB, cells, LANES), jnp.float32),
            pltpu.VMEM((count, SUB, cells, LANES), jnp.float32),
            pltpu.VMEM((SUB + 2, cells, LANES), jnp.float32),
            pltpu.VMEM((SUB, cells, LANES), jnp.float32),
            pltpu.SemaphoreType.DMA((count, SUB)),
            pltpu.SemaphoreType.DMA((count, SUB)),
        ],
        input_output_aliases={3: 0} if held else {},
        compiler_params=pltpu.CompilerParams(vmem_limit_bytes=44 * MIB),
        cost_estimate=pl.CostEstimate(flops=1, bytes_accessed=1, transcendentals=0),
        name="carried_part",
    )(read, vel_index, al, *held)


def halo_rows(refs, core, from_far, depth, blocks, put):
    swap_ref, first_ref, second_ref = refs
    ys = blocks * LANES // NZ

    @pl.loop(0, ys // 2)
    def _(y):
        at, up = rows_of(y), rows_of(y + ys // 2)
        a, b = first_ref[0, 0, at, :], second_ref[0, 0, at, :]
        put(at, jnp.where(from_far, jnp.where(core == 0, a, b), swap_ref[0, depth, at, :]))
        put(up, jnp.where(from_far, jnp.where(core == 0, b, a), swap_ref[0, depth, up, :]))


def near_kernel(core_ref, swap_ref, first_ref, second_ref, index_ref, al_ref, out_ref, halo, edge, scale, *, blocks):
    core = core_ref[0]
    ys = blocks * LANES // NZ

    @pl.when(pl.program_id(0) == 0)
    def _():
        for j, x in enumerate((0, SUB - 1, 1, SUB - 2, 2 * SUB - 1, SUB)):
            lane_copies(al_ref[x : x + 1, :], scale.at[j], blocks)

    upwind = Upwind(index_ref[...])

    def put(at, value):
        halo[at, :] = value

    halo_rows((swap_ref, first_ref, second_ref), core, upwind.px == (core == 0), 0, blocks, put)

    def scaled(pair, at):
        return jnp.where(upwind.px, scale[2 * pair, at, :], scale[2 * pair + 1, at, :])

    def start(first):
        for j in range(RUN):
            at = rows_of(first + j)
            value = scaled(0, at) * upwind.ax * halo[at, :]
            edge[at, :] = value
            out_ref[0, 1, at, :] = scaled(1, at) * upwind.ax * value

    each_run(ys, start)

    def run(first):
        inside = upwind.across(run_of(lambda y: edge[rows_of(y), :], first, ys))
        beyond = upwind.across(run_of(lambda y: halo[rows_of(y), :], first, ys))
        for j in range(RUN):
            at = rows_of(first + j)
            near = scaled(0, at)
            far = near * upwind.ax * scaled(2, at)
            out_ref[0, 0, at, :] = near * inside[j] + far * beyond[j]
            out_ref[0, 2, at, :] = far * upwind.ax

    each_run(ys, run)


def inflow_specs(cells):
    narrow = pl.BlockSpec((1, 1, cells // 2, LANES), lambda i: (i, 0, 0, 0))
    return [
        pl.BlockSpec(memory_space=pltpu.SMEM),
        pl.BlockSpec((1, 2, cells, LANES), lambda i: (i, 0, 0, 0)),
        narrow,
        narrow,
        pl.BlockSpec((3, LANES), lambda i: (0, i)),
    ]


def inflow_near(core, swap, first, second, vel_index, al16, vels, blocks):
    cells = blocks * LANES
    return pl.pallas_call(
        functools.partial(near_kernel, blocks=blocks),
        grid=(vels // LANES,),
        in_specs=inflow_specs(cells) + [pl.BlockSpec((2 * SUB, cells), lambda i: (0, 0))],
        out_specs=pl.BlockSpec((1, 3, cells, LANES), lambda i: (i, 0, 0, 0)),
        out_shape=pltpu.HBM((vels // LANES, 3, cells, LANES), jnp.float32),
        scratch_shapes=[
            pltpu.VMEM((cells, LANES), jnp.float32),
            pltpu.VMEM((cells, LANES), jnp.float32),
            pltpu.VMEM((6, cells, LANES), jnp.float32),
        ],
        compiler_params=pltpu.CompilerParams(vmem_limit_bytes=16 * MIB),
        cost_estimate=pl.CostEstimate(flops=1, bytes_accessed=1, transcendentals=0),
        name="inflow_near",
    )(core, swap, first, second, vel_index, al16)


def small_call(kernel, outs, name, specs, args, scratch=(), limit=16):
    vmem = pl.BlockSpec(memory_space=pltpu.VMEM)
    smem = pl.BlockSpec(memory_space=pltpu.SMEM)
    return pl.pallas_call(
        kernel,
        in_specs=[smem if s == "s" else vmem for s in specs],
        out_specs=[vmem] * len(outs),
        out_shape=[jax.ShapeDtypeStruct(o, jnp.float32) for o in outs],
        scratch_shapes=list(scratch),
        compiler_params=pltpu.CompilerParams(vmem_limit_bytes=limit * MIB),
        name=name,
    )(*args)


def pair_kernel(*refs):
    parts, (near_ref, far_ref) = refs[:-2], refs[-2:]
    value = parts[0][...]
    for part in parts[1:]:
        value = value + part[...]
    near_ref[...] = value[0:PAY]
    far_ref[...] = value[PAY:]


def total_kernel(*refs):
    parts, (all_ref, up_ref, down_ref) = refs[:-3], refs[-3:]
    value = parts[0][...]
    for part in parts[1:]:
        value = value + part[...]
    all_ref[...] = value
    up_ref[...] = value[UP:DOWN]
    down_ref[...] = value[M1:AA]


def mix(inverse, values):
    return [sum(inverse[k, j] * values[j] for j in range(MOM)) for k in range(MOM)]


def chunk_kernel(inv_ref, own_ref, low_ref, high_ref, send_ref):
    plane = lax.broadcasted_iota(jnp.int32, (SUB, LANES), 0)
    inverse = {(k, j): inv_ref[k, j] for k in range(MOM) for j in range(MOM)}
    inner, outer, later = [], [], []
    for m in range(MOM):

        def row(ref, at):
            return ref[at : at + 1, :]

        first = own_ref[M1 + m * SUB : M1 + (m + 1) * SUB, :]
        second = own_ref[AA + m * SUB : AA + (m + 1) * SUB, :]
        low = low_ref[M1 + m * SUB : M1 + (m + 1) * SUB, :]
        high = high_ref[m * SUB : (m + 1) * SUB, :]
        below = DOWN - M1 + m
        inner.append(
            first + jnp.where(plane == 0, row(low_ref, m), 0.0) + jnp.where(plane == SUB - 1, row(high_ref, below), 0.0)
        )
        outer.append(
            jnp.where(plane < SUB // 2, high, low)
            + jnp.where(plane == 0, row(own_ref, UP + m), 0.0)
            + jnp.where(plane == SUB - 1, row(own_ref, DOWN + m), 0.0)
        )
        later.append(
            second
            + jnp.where(plane == 0, row(low_ref, MOM + m), 0.0)
            + jnp.where(plane == 1, row(low_ref, 2 * MOM + m), 0.0)
            + jnp.where(plane == SUB - 1, row(high_ref, below + MOM), 0.0)
            + jnp.where(plane == SUB - 2, row(high_ref, below + 2 * MOM), 0.0)
        )
    local, around = mix(inverse, inner), mix(inverse, outer)
    for n in range(4):
        send_ref[n * 16 : n * 16 + SUB, :] = local[n + 1]
        send_ref[n * 16 + SUB : (n + 1) * 16, :] = around[n + 1]
        send_ref[MOVED + n * SUB : MOVED + (n + 1) * SUB, :] = inner[n + 1]
    for n, k in enumerate(STILL):
        send_ref[FIXED + n * SUB : FIXED + (n + 1) * SUB, :] = local[k]
        send_ref[EDGE + n : EDGE + n + 1, :] = around[k][0:1]
        send_ref[EDGE + 4 + n : EDGE + 5 + n, :] = around[k][SUB - 1 :]
    for m in range(MOM):
        send_ref[LATER + m * SUB : LATER + (m + 1) * SUB, :] = later[m]
    send_ref[SQUARE:SENT, :] = sum((local[m] - inner[m]) ** 2 for m in range(MOM) if not 1 <= m <= 4)


def sweeps(source):
    rows = source.shape[0]
    field = source
    for _ in range(SWEEPS):
        beside = pltpu.roll(field, 1, axis=0) + pltpu.roll(field, rows - 1, axis=0)
        beside = beside + roll_y(field, 1) + roll_y(field, -1) + roll_z(field, 1) + roll_z(field, -1)
        field = (source + coupling * beside) * (1.0 / (1.0 + 6.0 * coupling))
    return field


def fields_kernel(place_ref, inv_ref, cst_ref, *refs, blocks):
    parts = refs[:blocks]
    h1_ref, later_ref, next_ref, up_ref, down_ref, norm_ref, whole = refs[blocks:]
    mine = place_ref[0]
    for k in range(blocks):
        whole[jnp.bitwise_xor(mine, k)] = parts[k][...]

    def rows(first, count):
        return jnp.concatenate([whole[k, first : first + count, :] for k in range(blocks)], axis=1)

    def fold(value):
        return sum(value[:, k * LANES : (k + 1) * LANES] for k in range(blocks))

    square = sum(whole[k, SQUARE:SENT, :] for k in range(blocks))
    al = cst_ref[0, 0:SUB, :]
    edges = rows(EDGE, SUB)
    plane = lax.broadcasted_iota(jnp.int32, al.shape, 0)
    moved = []
    for n, m in enumerate(PICK):
        if 1 <= m <= 4:
            value = sweeps(rows((m - 1) * 16, 16))
            square = square + fold((value[0:SUB] - rows(MOVED + (m - 1) * SUB, SUB)) ** 2)
        else:
            k = STILL.index(m)
            around = jnp.where(
                plane == 0, edges[k : k + 1], jnp.where(plane == SUB - 1, edges[4 + k : 5 + k], 0.0)
            )
            value = jnp.concatenate([rows(FIXED + k * SUB, SUB), around], axis=0)
        given = cst_ref[1 if n in (0, 4) else 2] * value
        inside = given[0:SUB]
        shifted = [
            inside,
            pltpu.roll(given, 1, axis=0)[0:SUB],
            pltpu.roll(given, 2 * SUB - 1, axis=0)[0:SUB],
            roll_y(inside, 1),
            roll_y(inside, -1),
            roll_z(inside, 1),
            roll_z(inside, -1),
        ]
        for s in range(SETS):
            value = al * shifted[s]
            for k in range(blocks):
                first = (s * 8 + n) * SUB
                h1_ref[k, first : first + SUB, :] = value[:, k * LANES : (k + 1) * LANES]
        moved.append(shifted)
    norm_ref[...] = square

    matrices = stream_matrices()
    moments = []
    for m in range(MOM):
        value = rows(LATER + m * SUB, SUB)
        for s in range(SETS):
            for n in range(8):
                factor = float(matrices[s, m, n])
                if factor != 0.0:
                    value = value + factor * moved[n][s]
        later_ref[m * SUB : (m + 1) * SUB, :] = value
        moments.append(value)
    inverse = {(k, j): inv_ref[k, j] for k in range(MOM) for j in range(MOM)}
    for m, value in enumerate(mix(inverse, moments)):
        next_ref[m * SUB : (m + 1) * SUB, :] = value
        if 1 <= m <= 4:
            up_ref[(m - 1) * 4 : m * 4, :] = value[SUB // 2 :]
            down_ref[(m - 1) * 4 : m * 4, :] = value[: SUB // 2]


def last_kernel(
    place_ref, cst_ref, later_ref, next_ref, low_ref, high_ref, norm1_ref, h2_ref, out_ref, norm_ref, wide, *, blocks
):
    mine = place_ref[0]
    square = jnp.zeros((SUB, LANES), jnp.float32)
    for m in range(MOM):
        value = next_ref[m * SUB : (m + 1) * SUB, :]
        if 1 <= m <= 4:
            at = slice((m - 1) * 4, m * 4)
            value = sweeps(jnp.concatenate([value, high_ref[at, :], low_ref[at, :]], axis=0))[0:SUB]
        off = (value - later_ref[m * SUB : (m + 1) * SUB, :]) ** 2
        for k in range(blocks):
            wide[m, k] = value[:, k * LANES : (k + 1) * LANES]
            square = square + off[:, k * LANES : (k + 1) * LANES]
        out_ref[m] = wide[m, mine]
        if m in PICK:
            n = PICK.index(m)
            given = cst_ref[1 if n in (0, 4) else 2, 0:SUB, :] * value
            for k in range(blocks):
                h2_ref[k, n * SUB : (n + 1) * SUB, :] = given[:, k * LANES : (k + 1) * LANES]
    norm_ref[0:1, :] = jnp.sum(norm1_ref[...], axis=0, keepdims=True)
    norm_ref[1:2, :] = jnp.sum(square, axis=0, keepdims=True)


def finish_kernel(
    core_ref, carried_ref, inflow_ref, swap_ref, first_ref, second_ref, h1_ref, h2_ref, index_ref, out_ref,
    rows, fields, table, far, ready, sems, *, blocks
):
    group = pl.program_id(0)

    @pl.when(group == 0)
    def _():
        speed = [speed_range * (2.0 * index_ref[a : a + 1, :].astype(jnp.float32) + 1.0 - NVX) / NVX for a in range(3)]
        for n, row in enumerate(functions_of(*speed)[1]):
            table[n : n + 1, :] = row
        base = table[...]
        speeds = []
        for c in speed:
            speeds.append(jnp.where(c > 0, time_step * c, 0.0))
            speeds.append(jnp.where(c < 0, -time_step * c, 0.0))
        full = jnp.concatenate([base * (1.0 - sum(speeds))] + [base * s for s in speeds] + [base], axis=0)
        high = full.astype(jnp.bfloat16).astype(jnp.float32)
        stacked = jnp.concatenate([high, high, full - high, jnp.zeros_like(full)], axis=0).astype(jnp.bfloat16)
        for g in range(rows.shape[0]):
            rows[g] = stacked[:, g * LANES : (g + 1) * LANES]
        left = lax.broadcasted_iota(jnp.int32, (LANES, LANES), 1) < LANES // 2

        @pl.loop(0, blocks)
        def _(k):
            at = pl.ds(pl.multiple_of(k * LANES, LANES), LANES)
            for x in range(SUB):
                first = h1_ref[k, pl.ds(x, SETS * 8, stride=SUB), :]
                second = h2_ref[k, pl.ds(x, 8, stride=SUB), :]
                value = jnp.concatenate([first, second, first, second], axis=0).T
                high = value.astype(jnp.bfloat16).astype(jnp.float32)
                fields[x, at, 0:LANES] = jnp.where(left, high, value - high).astype(jnp.bfloat16)
                fields[x, at, LANES:] = jnp.where(left, high, 0.0).astype(jnp.bfloat16)

    stride = blocks * SUB
    pitch = stride + PAD
    slot = lax.rem(group, 2)
    out = ready.reshape(2 * LANES * pitch, LANES)

    def store(g):
        side = lax.rem(g, 2)
        return pltpu.make_async_copy(
            ready.at[side, :, pl.ds(0, stride)], out_ref.at[pl.ds(g * LANES, LANES)], sems.at[side]
        )

    @pl.when(group >= 2)
    def _():
        store(group - 2).wait()

    here = index_ref[0:1, pl.ds(pl.multiple_of(group * LANES, LANES), LANES)]
    px = here * 2 >= NVX
    core = core_ref[0]

    def put(at, value):
        far[at, :] = inflow_ref[0, 0, at, :] + inflow_ref[0, 2, at, :] * value

    from_far = jnp.broadcast_to(px, (NZ, LANES)) == (core == 0)
    halo_rows((swap_ref, first_ref, second_ref), core, from_far, 0, blocks, put)
    inflow = (lambda: far[...], lambda: inflow_ref[0, 1])
    for x in range(SUB):
        value = carried_ref[0, x] + jnp.dot(fields[x], rows[group], preferred_element_type=jnp.float32)
        if x in (0, 1):
            value = value + jnp.where(px, inflow[x](), 0.0)
        elif x in (SUB - 2, SUB - 1):
            value = value + jnp.where(px, 0.0, inflow[SUB - 1 - x]())
        for k in range(blocks):
            first = slot * (LANES * pitch) + k * SUB + x
            out[pl.ds(first, LANES, stride=pitch), :] = value[k * LANES : (k + 1) * LANES].T
    store(group).start()
    last = rows.shape[0] - 1

    @pl.when(group == last)
    def _():
        if last > 0:
            store(group - 1).wait()
        store(group).wait()


def finish(core, carried_part, inflow_part, swap, first, second, h1, h2, vel_index, vels, blocks):
    cells = blocks * LANES
    groups = vels // LANES
    vmem = pl.BlockSpec(memory_space=pltpu.VMEM)
    return pl.pallas_call(
        functools.partial(finish_kernel, blocks=blocks),
        grid=(groups,),
        in_specs=[
            pl.BlockSpec(memory_space=pltpu.SMEM),
            pl.BlockSpec((1, SUB, cells, LANES), lambda g: (g, 0, 0, 0)),
            pl.BlockSpec((1, 3, cells, LANES), lambda g: (g, 0, 0, 0)),
            pl.BlockSpec((1, 1, cells, LANES), lambda g: (g, 1, 0, 0)),
            pl.BlockSpec((1, 1, cells // 2, LANES), lambda g: (g, 0, 0, 0)),
            pl.BlockSpec((1, 1, cells // 2, LANES), lambda g: (g, 0, 0, 0)),
            vmem,
            vmem,
            vmem,
        ],
        out_specs=pl.BlockSpec(memory_space=pl.ANY),
        out_shape=jax.ShapeDtypeStruct((vels, blocks * SUB, LANES), jnp.float32),
        scratch_shapes=[
            pltpu.VMEM((groups, 256, LANES), jnp.bfloat16),
            pltpu.VMEM((SUB, cells, 256), jnp.bfloat16),
            pltpu.VMEM((8, vels), jnp.float32),
            pltpu.VMEM((cells, LANES), jnp.float32),
            pltpu.VMEM((2, LANES, blocks * SUB + PAD, LANES), jnp.float32),
            pltpu.SemaphoreType.DMA((2,)),
        ],
        compiler_params=pltpu.CompilerParams(vmem_limit_bytes=40 * MIB),
        cost_estimate=pl.CostEstimate(
            flops=2 * 256 * vels * blocks * SUB * LANES, bytes_accessed=8 * vels * blocks * SUB * LANES, transcendentals=0
        ),
        name="finish_dist",
    )(core, carried_part, inflow_part, swap, first, second, h1, h2, vel_index)


def ring(axis, step):
    size = lax.axis_size(axis)
    return [(i, (i + step) % size) for i in range(size)]


def shards(dist, vel_index, relax, wall_mask, macro_inverse):
    vels, width, cells = dist.shape
    blocks = cells // LANES
    peers, slabs = lax.axis_size("vel"), lax.axis_size("space")
    assert width == SUB and peers % blocks == 0 and slabs == 4 and blocks % 2 == 0
    sub = peers // blocks
    me = lax.axis_index("vel")
    place = (me // sub).astype(jnp.int32).reshape(1)
    core = (lax.axis_index("space") % 2).astype(jnp.int32).reshape(1)

    flat = dist.reshape(vels, width, blocks, LANES).transpose(0, 2, 1, 3).reshape(vels, blocks * width, LANES)
    speed = speed_range * (2.0 * vel_index.astype(jnp.float32) + 1.0 - NVX) / NVX

    wall = wall_mask > 0
    coefficients = jnp.stack(
        [
            jnp.where(wall, 0.0, 1.0 - relax),
            jnp.where(wall, 1.0, relax),
            jnp.where(wall, 0.0, relax),
        ],
        0,
    )
    from_low = lax.ppermute(coefficients[:, SUB - 1 :], "space", ring("space", 1))
    from_high = lax.ppermute(coefficients[:, :1], "space", ring("space", -1))

    leaving, read = first_stream(flat, vel_index, vels, blocks)
    (leaving, from_low, from_high) = lax.optimization_barrier((leaving, from_low, from_high))
    swap = lax.ppermute(leaving, "space", [(i, i ^ 1) for i in range(slabs)])
    cst = jnp.concatenate(
        [coefficients, from_high, jnp.zeros((3, SUB - 2, cells), jnp.float32), from_low], 1
    )

    parts = both_moments(place, read, leaving, vel_index, cst, vels, blocks)
    (swap, parts) = lax.optimization_barrier((swap, parts))

    half = cells // 2
    start = core[0] * half
    mine = lax.dynamic_slice_in_dim(leaving, start, half, 2)
    other = lax.dynamic_slice_in_dim(swap, start, half, 2)
    plus = speed[0].reshape(vels // LANES, 1, 1, LANES) > 0
    across = jnp.where(plus == (core[0] == 1), mine, other)
    (across, parts) = lax.optimization_barrier((across, parts))
    over = [(i, i ^ 2) for i in range(slabs)]
    first = [lax.ppermute(across[:, 0:1], "space", over)]

    def beside(step):
        return [(i, (i // sub ^ step) * sub + i % sub) for i in range(peers)]

    spans = [(0, vels)] if vels < 2 * LANES else [(0, vels // 2), (vels // 2, vels - vels // 2)]

    got = [parts[0]] + [lax.ppermute(parts[k], "vel", beside(k)) for k in range(1, blocks // 2)]
    carried_part = carried(read, vel_index, coefficients[0], *spans[0], blocks)
    (got[1], carried_part) = lax.optimization_barrier((got[1], carried_part))
    near, far = small_call(pair_kernel, [(PAY, LANES)] * 2, "sum_near", "v" * len(got), got)
    got = [near, lax.ppermute(far, "vel", beside(blocks // 2))]
    if len(spans) > 1:
        (al, _) = lax.optimization_barrier((coefficients[0], near))
        carried_part = carried(read, vel_index, al, *spans[1], blocks, carried_part)
        (got[1], carried_part) = lax.optimization_barrier((got[1], carried_part))
    if sub > 1:
        part = sum(got)
        got = [part]
        for k in range(1, sub):
            pairs = [(i, i // sub * sub + (i % sub + k) % sub) for i in range(peers)]
            got.append(lax.ppermute(part, "vel", pairs))
    chunk, up, down = small_call(
        total_kernel, [(PAY, LANES), (DOWN - UP, LANES), (AA - M1, LANES)], "sum_moments", "v" * len(got), got
    )
    (first[0], up, down) = lax.optimization_barrier((first[0], up, down))
    low = lax.ppermute(up, "space", ring("space", 1))
    high = lax.ppermute(down, "space", ring("space", -1))
    (send,) = small_call(
        chunk_kernel, [(SENT, LANES)], "local_fields", "svvv", (macro_inverse, chunk, low, high)
    )
    pieces = [send] + [lax.ppermute(send, "vel", beside(k)) for k in range(1, blocks // 2 + 1)]
    across1, send = lax.optimization_barrier((across[:, 1:2], send))
    first.append(lax.ppermute(across1, "space", over))
    swap_chip = [(i, i ^ 1) for i in range(slabs)]
    second = [lax.ppermute(first[0], "space", swap_chip)]
    (second[0], send) = lax.optimization_barrier((second[0], send))
    inflow_part = inflow_near(core, swap, first[0], second[0], vel_index, cst[0], vels, blocks)
    (pieces[blocks // 2], inflow_part) = lax.optimization_barrier((pieces[blocks // 2], inflow_part))
    pieces += [lax.ppermute(pieces[blocks // 2], "vel", beside(k)) for k in range(1, blocks // 2)]

    h1, later, following, up2, down2, norm1 = small_call(
        functools.partial(fields_kernel, blocks=blocks),
        [
            (blocks, SETS * 8 * SUB, LANES),
            (MOM * SUB, cells),
            (MOM * SUB, cells),
            (16, cells),
            (16, cells),
            (SUB, LANES),
        ],
        "first_fields",
        "ssv" + "v" * blocks,
        (place, macro_inverse, cst, *pieces),
        [pltpu.VMEM((blocks, SENT, LANES), jnp.float32)],
        10,
    )
    (first[1], up2) = lax.optimization_barrier((first[1], up2))
    second.append(lax.ppermute(first[1], "space", swap_chip))
    low2 = lax.ppermute(up2, "space", ring("space", 1))
    high2 = lax.ppermute(down2, "space", ring("space", -1))
    h2, owned, squares = small_call(
        functools.partial(last_kernel, blocks=blocks),
        [(blocks, 8 * SUB, LANES), (MOM, SUB, LANES), (2, LANES)],
        "last_fields",
        "svvvvvv",
        (place, cst, later, following, low2, high2, norm1),
        [pltpu.VMEM((MOM, blocks, SUB, LANES), jnp.float32)],
        10,
    )

    around = [lax.ppermute(squares, "space", ring("space", k)) for k in range(1, slabs)]
    (second[1], h2) = lax.optimization_barrier((second[1], h2))
    if sub > 1:
        owned = lax.dynamic_slice_in_dim(owned, (me % sub) * (LANES // sub), LANES // sub, 2)

    out = finish(
        core, carried_part, inflow_part, swap, first[1], second[1], h1, h2, vel_index, vels, blocks
    )
    (around[0], out) = lax.optimization_barrier((around[0], out))
    slab = lax.axis_index("space")
    every = [squares] + around
    ordered = [
        functools.reduce(lambda a, k: jnp.where((slab - k) % slabs == j, every[k], a), range(1, slabs), every[0])
        for j in range(slabs)
    ]
    norms = jnp.sqrt(jnp.sum(sum(ordered), axis=1))
    out = out.reshape(vels, blocks, width, LANES).transpose(0, 2, 1, 3).reshape(vels, width, cells)
    return (out, owned, norms)


def solution(mesh):
    return jax.shard_map(
        shards,
        mesh=mesh,
        in_specs=(P("vel", "space", None), P(None, "vel"), P("space", None), P("space", None), P()),
        out_specs=(P("vel", "space", None), P(None, "space", "vel"), P()),
        check_vma=False,
    )
```

```python
import functools
import math

import jax
import jax.numpy as jnp
import numpy as np
from jax import lax
from jax.experimental import pallas as pl
from jax.experimental.pallas import tpu as pltpu
from jax.sharding import PartitionSpec as P

NVX = 16
NZ = 16
MOM = 13
SWEEPS = 3
LANES = 128
SUB = 8
SETS = 7
PICK = (0, 1, 2, 3, 4, 10, 11, 12)

speed_range = 4.0
time_step = 0.08
coupling = 0.5
MIB = 2**20
PIECES = 8
RUN = 16
PAD = 8

UP, M1, DOWN, AA, PAY = 0, 40, 144, 184, 288
STILL = (0, 10, 11, 12)
MOVED, FIXED, EDGE, LATER, SQUARE, SENT = 64, 96, 128, 136, 240, 248


def functions_of(cx, cy, cz):
    square = cx * cx + cy * cy + cz * cz
    heat = square - 2.5
    one = cx * 0.0 + 1.0
    rows = [
        one, cx, cy, cz, 2.0 * square / 3.0 - 1.0, 2.0 * cx * cy, 2.0 * cx * cz, 2.0 * cy * cz,
        cx * cx - cy * cy, cy * cy - cz * cz, cx * heat, cy * heat, cz * heat,
    ]
    factor = 4.0 / 15.0
    shakhov = [
        one, 2.0 * cx, 2.0 * cy, 2.0 * cz, square - 1.5,
        factor * cx * heat, factor * cy * heat, factor * cz * heat,
    ]
    return rows, shakhov, square


def half_speeds(cx, cy, cz):
    out = []
    for c in (cx, cy, cz):
        out.append(time_step * c * (c > 0))
        out.append(-time_step * c * (c < 0))
    return out


@functools.lru_cache(None)
def stream_matrices():
    line = speed_range * (2.0 * np.arange(NVX) + 1.0 - NVX) / NVX
    cx, cy, cz = (g.reshape(-1) for g in np.meshgrid(line, line, line, indexing="ij"))
    rows, shakhov, square = functions_of(cx, cy, cz)
    weight = (2.0 * speed_range / NVX) ** 3 * math.pi ** (-1.5) * np.exp(-square)
    rows = np.stack(rows) * weight
    shakhov = np.stack(shakhov)
    speeds = half_speeds(cx, cy, cz)
    stay = 1.0 - sum(speeds)
    out = np.stack([(rows * s) @ shakhov.T for s in [stay] + speeds])
    out[np.abs(out) < 1e-13] = 0.0
    return out


def split(value):
    high = value.astype(jnp.bfloat16)
    low = (value - high.astype(jnp.float32)).astype(jnp.bfloat16)
    return high, low


def speeds_at(index):
    speed = speed_range * (2.0 * index.astype(jnp.float32) + 1.0 - NVX) / NVX
    return [time_step * speed[a : a + 1] for a in range(3)]


class Upwind:
    def __init__(self, index):
        tx, ty, tz = speeds_at(index)
        shape = (NZ, LANES)
        self.ax, self.ay, self.az = (jnp.broadcast_to(jnp.abs(t), shape) for t in (tx, ty, tz))
        self.stay = 1.0 - self.ax - self.ay - self.az
        self.px, self.py, self.pz = (jnp.broadcast_to(t, shape) > 0 for t in (tx, ty, tz))

    def across(self, rows):
        out = []
        for before, here, after in zip(rows[:-2], rows[1:-1], rows[2:]):
            in_y = jnp.where(self.py, before, after)
            in_z = jnp.where(self.pz, pltpu.roll(here, 1, axis=0), pltpu.roll(here, NZ - 1, axis=0))
            out.append(self.stay * here + self.ay * in_y + self.az * in_z)
        return out

    def stream(self, ref, x, first, count):
        mid = self.across(run_of(lambda y: ref[x + 1, rows_of(y), :], first, count))
        out = []
        for j, value in enumerate(mid):
            at = rows_of(first + j)
            out.append(value + self.ax * jnp.where(self.px, ref[x, at, :], ref[x + 2, at, :]))
        return out


def run_of(read, first, count):
    ends = [lax.rem(first + count - 1, count), lax.rem(first + RUN, count)]
    return [read(ends[0])] + [read(first + j) for j in range(RUN)] + [read(ends[1])]


def rows_of(y):
    return pl.ds(pl.multiple_of(y * NZ, NZ), NZ)


def each_run(count, body):
    @pl.loop(0, count // RUN)
    def _(i):
        body(i * RUN)


def lane_copies(ref_row, target, blocks):
    for k in range(blocks):
        at = slice(k * LANES, (k + 1) * LANES)
        target[at, :] = jnp.broadcast_to(ref_row[:, at], (LANES, LANES)).T


def roll_y(value, sign):
    cells = value.shape[1]
    return pltpu.roll(value, NZ if sign > 0 else cells - NZ, axis=1)


def roll_z(value, sign):
    cells = value.shape[1]
    zl = lax.broadcasted_iota(jnp.int32, value.shape, 1) & (NZ - 1)
    if sign > 0:
        return jnp.where(zl == 0, pltpu.roll(value, cells - (NZ - 1), axis=1), pltpu.roll(value, 1, axis=1))
    return jnp.where(zl == NZ - 1, pltpu.roll(value, NZ - 1, axis=1), pltpu.roll(value, cells - 1, axis=1))


def stream_kernel(dist_ref, index_ref, leaving_ref, read_ref, held, even, odd, done, sems, out_sems, *, vels, blocks):
    stride = blocks * SUB
    chunks = vels // LANES
    piece = LANES // PIECES
    pitch = stride + PAD
    ys = blocks * LANES // NZ
    flat = held.reshape(2 * LANES * pitch, LANES)

    def fetch(c):
        return [
            pltpu.make_async_copy(
                dist_ref.at[pl.ds(c * LANES + p * piece, piece)],
                held.at[c % 2, pl.ds(p * piece, piece), pl.ds(0, stride)],
                sems.at[c % 2, p],
            )
            for p in range(PIECES)
        ]

    def store(c):
        return pltpu.make_async_copy(done.at[c % 2], read_ref.at[c], out_sems.at[c % 2])

    def turn(c, k):
        target = odd if c % 2 else even
        for x in range(SUB):
            value = flat[pl.ds((c % 2) * LANES * pitch + k * SUB + x, LANES, stride=pitch), :]
            target[x + 1, pl.ds(pl.multiple_of(k * LANES, LANES), LANES), :] = value.T

    for c in range(min(2, chunks)):
        for copy in fetch(c):
            copy.start()
    empty = jnp.zeros((ys * NZ, LANES), jnp.float32)
    for ref in (even, odd):
        ref[0] = empty
        ref[SUB + 1] = empty
    for copy in fetch(0):
        copy.wait()

    @pl.loop(0, blocks)
    def _(k):
        turn(0, k)

    for c in range(chunks):
        turned = odd if c % 2 else even
        if c + 2 < chunks:
            for copy in fetch(c + 2):
                copy.start()
        if c + 1 < chunks:
            for copy in fetch(c + 1):
                copy.wait()
        if c >= 2:
            store(c - 2).wait()
        upwind = Upwind(index_ref[:, c * LANES : (c + 1) * LANES])

        @pl.loop(0, SUB)
        def _(x, upwind=upwind, c=c, turned=turned):
            if c + 1 < chunks and blocks == SUB:
                turn(c + 1, x)
            for first in range(0, ys, RUN):
                for j, value in enumerate(upwind.stream(turned, x, first, ys)):
                    done[c % 2, x, rows_of(first + j), :] = value

        if c + 1 < chunks and blocks != SUB:

            @pl.loop(0, blocks)
            def _(k, c=c):
                turn(c + 1, k)

        def edges(first, upwind=upwind, c=c, turned=turned):
            for j in range(RUN):
                at = rows_of(first + j)
                bottom, top = turned[1, at, :], turned[SUB, at, :]
                leaving_ref[c, 0, at, :] = jnp.where(upwind.px, top, bottom)
                leaving_ref[c, 1, at, :] = jnp.where(upwind.px, turned[SUB - 1, at, :], turned[2, at, :])

        each_run(ys, edges)
        store(c).start()
    for c in range(max(0, chunks - 2), chunks):
        store(c).wait()


def first_stream(flat, vel_index, vels, blocks):
    cells = blocks * LANES
    anywhere = pl.BlockSpec(memory_space=pl.ANY)
    vmem = pl.BlockSpec(memory_space=pltpu.VMEM)
    return pl.pallas_call(
        functools.partial(stream_kernel, vels=vels, blocks=blocks),
        in_specs=[anywhere, vmem],
        out_specs=[vmem, anywhere],
        out_shape=[
            jax.ShapeDtypeStruct((vels // LANES, 2, cells, LANES), jnp.float32),
            jax.ShapeDtypeStruct((vels // LANES, SUB, cells, LANES), jnp.float32),
        ],
        scratch_shapes=[
            pltpu.VMEM((2, LANES, blocks * SUB + PAD, LANES), jnp.float32),
            pltpu.VMEM((SUB + 2, cells, LANES), jnp.float32),
            pltpu.VMEM((SUB + 2, cells, LANES), jnp.float32),
            pltpu.VMEM((2, SUB, cells, LANES), jnp.float32),
            pltpu.SemaphoreType.DMA((2, PIECES)),
            pltpu.SemaphoreType.DMA((2,)),
        ],
        compiler_params=pltpu.CompilerParams(vmem_limit_bytes=54 * MIB),
        cost_estimate=pl.CostEstimate(
            flops=20 * vels * SUB * cells, bytes_accessed=8 * vels * SUB * cells, transcendentals=0
        ),
        name="first_stream",
    )(flat, vel_index)


def moments_kernel(me_ref, read_ref, leaving_ref, index_ref, cst_ref, *refs, vels, blocks):
    half = blocks // 2
    outs = refs[:half]
    table, wst, acc, gacc, pay = refs[half:]
    span = SETS * 16
    step = pl.program_id(0)

    @pl.when(step == 0)
    def _():
        speed = [speed_range * (2.0 * index_ref[a : a + 1, :].astype(jnp.float32) + 1.0 - NVX) / NVX for a in range(3)]
        rows, _, square = functions_of(*speed)
        weight = (2.0 * speed_range / NVX) ** 3 * math.pi ** (-1.5) * jnp.exp(-square)
        table[...] = jnp.zeros_like(table)
        for m, row in enumerate(rows):
            table[m : m + 1, :] = row * weight
        base = table[...]
        speeds = []
        for c in speed:
            speeds.append(jnp.where(c > 0, time_step * c, 0.0))
            speeds.append(jnp.where(c < 0, -time_step * c, 0.0))
        full = jnp.concatenate([base] + [base * s for s in speeds] + [jnp.zeros_like(base)], axis=0)
        for variant, factor in enumerate([None, speeds[0], speeds[1]]):
            high, low = split((full if factor is None else full * factor).T)
            wst[variant, :, 0:LANES] = high
            wst[variant, :, LANES:] = low

    wide = 2 * LANES
    at = pl.ds(pl.multiple_of(step * wide, wide), wide)
    groups = range(vels // LANES)

    def reduced(high, low, variant):
        first = jnp.dot(high, wst[variant], preferred_element_type=jnp.float32)
        second = jnp.dot(low, wst[variant, :, 0:LANES], preferred_element_type=jnp.float32)
        return (first[:, 0:LANES] + first[:, LANES:] + second).T[0:span]

    for x in range(SUB):
        total = reduced(*split(jnp.concatenate([read_ref[g, x] for g in groups], axis=1)), 0)
        for j in range(2):
            acc[2 * step + j, pl.ds(x, span, stride=SUB), :] = total[:, j * LANES : (j + 1) * LANES]
    edge = split(jnp.concatenate([leaving_ref[g, 0] for g in groups], axis=1))
    for side in range(2):
        gacc[side, :, at] = reduced(*edge, side + 1)

    @pl.when(step == pl.num_programs(0) - 1)
    def _():
        combine_moments(me_ref, cst_ref, outs, acc, gacc, pay, blocks)


def combine_moments(me_ref, cst_ref, outs, acc, gacc, pay, blocks):
    half = blocks // 2
    al = cst_ref[0, 0:SUB, :]
    beyond = cst_ref[0, SUB : SUB + 1, :]
    below = cst_ref[0, 2 * SUB - 1 : 2 * SUB, :]
    plane = lax.broadcasted_iota(jnp.int32, al.shape, 0)

    def own(i, m):
        first = (i * 16 + m) * SUB
        return jnp.concatenate([acc[k, first : first + SUB, :] for k in range(blocks)], axis=1)

    for m in range(MOM):
        sets = [own(i, m) for i in range(SETS)]
        value = al * (sets[0] - sum(sets[1:]))
        value = value + jnp.where(plane == 0, 0.0, pltpu.roll(al * sets[1], 1, axis=0))
        value = value + jnp.where(plane == SUB - 1, 0.0, pltpu.roll(al * sets[2], SUB - 1, axis=0))
        value = value + roll_y(al * sets[3], 1) + roll_y(al * sets[4], -1)
        value = value + roll_z(al * sets[5], 1) + roll_z(al * sets[6], -1)
        for k in range(blocks):
            at = slice(k * LANES, (k + 1) * LANES)
            pay[k, M1 + m * SUB : M1 + (m + 1) * SUB, :] = sets[0][:, at]
            pay[k, AA + m * SUB : AA + (m + 1) * SUB, :] = value[:, at]

    for side, (scale, edge, toward, start) in enumerate([(beyond, SUB - 1, 1, UP), (below, 0, 2, DOWN)]):
        sets = [gacc[side, i * 16 : (i + 1) * 16, :] for i in range(SETS)]
        near = scale * (sets[0] - sum(sets[1:]))
        near = near + roll_y(scale * sets[3], 1) + roll_y(scale * sets[4], -1)
        near = near + roll_z(scale * sets[5], 1) + roll_z(scale * sets[6], -1)
        out_of = jnp.concatenate(
            [acc[k, pl.ds(toward * 16 * SUB + edge, 16, stride=SUB), :] for k in range(blocks)], axis=1
        )
        near = near + al[edge : edge + 1, :] * out_of
        far = scale * sets[toward]
        for k in range(blocks):
            at = slice(k * LANES, (k + 1) * LANES)
            for j, value in enumerate((sets[0], near, far)):
                pay[k, start + j * MOM : start + (j + 1) * MOM, :] = value[0:MOM, at]
            pay[k, start + 3 * MOM : start + 3 * MOM + 1, :] = jnp.zeros((1, LANES), jnp.float32)

    mine = me_ref[0]
    for k in range(half):
        near = jnp.bitwise_xor(mine, k)
        outs[k][0:PAY, :] = pay[near]
        outs[k][PAY:, :] = pay[jnp.bitwise_xor(near, half)]


def both_moments(place, read, leaving, vel_index, cst, vels, blocks):
    cells = blocks * LANES
    vmem = pl.BlockSpec(memory_space=pltpu.VMEM)
    span = SETS * 16
    block = pl.BlockSpec((vels // LANES, SUB, 2 * LANES, LANES), lambda i: (0, 0, i, 0))
    edge = pl.BlockSpec((vels // LANES, 1, 2 * LANES, LANES), lambda i: (0, 0, i, 0))
    return pl.pallas_call(
        functools.partial(moments_kernel, vels=vels, blocks=blocks),
        grid=(blocks // 2,),
        in_specs=[pl.BlockSpec(memory_space=pltpu.SMEM), block, edge, vmem, vmem],
        out_specs=[vmem] * (blocks // 2),
        out_shape=[jax.ShapeDtypeStruct((2 * PAY, LANES), jnp.float32)] * (blocks // 2),
        scratch_shapes=[
            pltpu.VMEM((16, vels), jnp.float32),
            pltpu.VMEM((3, vels, 2 * LANES), jnp.bfloat16),
            pltpu.VMEM((blocks, span * SUB, LANES), jnp.float32),
            pltpu.VMEM((2, span, cells), jnp.float32),
            pltpu.VMEM((blocks, PAY, LANES), jnp.float32),
        ],
        compiler_params=pltpu.CompilerParams(vmem_limit_bytes=56 * MIB),
        cost_estimate=pl.CostEstimate(
            flops=2 * 336 * vels * 10 * cells, bytes_accessed=4 * vels * 10 * cells, transcendentals=0
        ),
        name="moments_of_both",
    )(place, read, leaving, vel_index, cst)


def carried_kernel(read_ref, index_ref, al_ref, *refs, blocks, start, count):
    out_ref, source, ready, mid, scale, in_sems, out_sems = refs[-7:]
    ys = blocks * LANES // NZ

    def fetch(g, x):
        return pltpu.make_async_copy(read_ref.at[start + g, x], source.at[g, x], in_sems.at[g, x])

    def store(g, x):
        return pltpu.make_async_copy(ready.at[g, x], out_ref.at[start + g, x], out_sems.at[g, x])

    for g in range(count):
        for x in range(SUB):
            fetch(g, x).start()
    for x in range(SUB):
        lane_copies(al_ref[x : x + 1, :], scale.at[x], blocks)
    empty = jnp.zeros((ys * NZ, LANES), jnp.float32)
    mid[0] = empty
    mid[SUB + 1] = empty
    for g in range(count):
        upwind = Upwind(index_ref[:, (start + g) * LANES : (start + g + 1) * LANES])

        @pl.loop(0, SUB)
        def _(x, g=g):
            fetch(g, x).wait()

            def run(first):
                for j in range(RUN):
                    at = rows_of(first + j)
                    mid[x + 1, at, :] = scale[x, at, :] * source[g, x, at, :]

            each_run(ys, run)

        @pl.loop(0, SUB)
        def _(x, g=g, upwind=upwind):
            def run(first):
                for j, value in enumerate(upwind.stream(mid, x, first, ys)):
                    at = rows_of(first + j)
                    ready[g, x, at, :] = scale[x, at, :] * value

            each_run(ys, run)
            store(g, x).start()

    for g in range(count):
        for x in range(SUB):
            store(g, x).wait()


def carried(read, vel_index, al, first, vels, blocks, before=None):
    groups = read.shape[0]
    cells = blocks * LANES
    count = vels // LANES
    anywhere = pl.BlockSpec(memory_space=pl.ANY)
    vmem = pl.BlockSpec(memory_space=pltpu.VMEM)
    held = [] if before is None else [before]
    return pl.pallas_call(
        functools.partial(carried_kernel, blocks=blocks, start=first // LANES, count=count),
        in_specs=[anywhere, vmem, vmem] + [anywhere] * len(held),
        out_specs=anywhere,
        out_shape=jax.ShapeDtypeStruct((groups, SUB, cells, LANES), jnp.float32),
        scratch_shapes=[
            pltpu.VMEM((count, SUB, cells, LANES), jnp.float32),
            pltpu.VMEM((count, SUB, cells, LANES), jnp.float32),
            pltpu.VMEM((SUB + 2, cells, LANES), jnp.float32),
            pltpu.VMEM((SUB, cells, LANES), jnp.float32),
            pltpu.SemaphoreType.DMA((count, SUB)),
            pltpu.SemaphoreType.DMA((count, SUB)),
        ],
        input_output_aliases={3: 0} if held else {},
        compiler_params=pltpu.CompilerParams(vmem_limit_bytes=44 * MIB),
        cost_estimate=pl.CostEstimate(flops=1, bytes_accessed=1, transcendentals=0),
        name="carried_part",
    )(read, vel_index, al, *held)


def halo_rows(refs, core, from_far, depth, blocks, put):
    swap_ref, first_ref, second_ref = refs
    ys = blocks * LANES // NZ

    @pl.loop(0, ys // 2)
    def _(y):
        at, up = rows_of(y), rows_of(y + ys // 2)
        a, b = first_ref[0, 0, at, :], second_ref[0, 0, at, :]
        put(at, jnp.where(from_far, jnp.where(core == 0, a, b), swap_ref[0, depth, at, :]))
        put(up, jnp.where(from_far, jnp.where(core == 0, b, a), swap_ref[0, depth, up, :]))


def near_kernel(core_ref, swap_ref, first_ref, second_ref, index_ref, al_ref, out_ref, halo, edge, scale, *, blocks):
    core = core_ref[0]
    ys = blocks * LANES // NZ

    @pl.when(pl.program_id(0) == 0)
    def _():
        for j, x in enumerate((0, SUB - 1, 1, SUB - 2, 2 * SUB - 1, SUB)):
            lane_copies(al_ref[x : x + 1, :], scale.at[j], blocks)

    upwind = Upwind(index_ref[...])

    def put(at, value):
        halo[at, :] = value

    halo_rows((swap_ref, first_ref, second_ref), core, upwind.px == (core == 0), 0, blocks, put)

    def scaled(pair, at):
        return jnp.where(upwind.px, scale[2 * pair, at, :], scale[2 * pair + 1, at, :])

    def start(first):
        for j in range(RUN):
            at = rows_of(first + j)
            value = scaled(0, at) * upwind.ax * halo[at, :]
            edge[at, :] = value
            out_ref[0, 1, at, :] = scaled(1, at) * upwind.ax * value

    each_run(ys, start)

    def run(first):
        inside = upwind.across(run_of(lambda y: edge[rows_of(y), :], first, ys))
        beyond = upwind.across(run_of(lambda y: halo[rows_of(y), :], first, ys))
        for j in range(RUN):
            at = rows_of(first + j)
            near = scaled(0, at)
            far = near * upwind.ax * scaled(2, at)
            out_ref[0, 0, at, :] = near * inside[j] + far * beyond[j]
            out_ref[0, 2, at, :] = far * upwind.ax

    each_run(ys, run)


def inflow_specs(cells):
    narrow = pl.BlockSpec((1, 1, cells // 2, LANES), lambda i: (i, 0, 0, 0))
    return [
        pl.BlockSpec(memory_space=pltpu.SMEM),
        pl.BlockSpec((1, 2, cells, LANES), lambda i: (i, 0, 0, 0)),
        narrow,
        narrow,
        pl.BlockSpec((3, LANES), lambda i: (0, i)),
    ]


def inflow_near(core, swap, first, second, vel_index, al16, vels, blocks):
    cells = blocks * LANES
    return pl.pallas_call(
        functools.partial(near_kernel, blocks=blocks),
        grid=(vels // LANES,),
        in_specs=inflow_specs(cells) + [pl.BlockSpec((2 * SUB, cells), lambda i: (0, 0))],
        out_specs=pl.BlockSpec((1, 3, cells, LANES), lambda i: (i, 0, 0, 0)),
        out_shape=pltpu.HBM((vels // LANES, 3, cells, LANES), jnp.float32),
        scratch_shapes=[
            pltpu.VMEM((cells, LANES), jnp.float32),
            pltpu.VMEM((cells, LANES), jnp.float32),
            pltpu.VMEM((6, cells, LANES), jnp.float32),
        ],
        compiler_params=pltpu.CompilerParams(vmem_limit_bytes=16 * MIB),
        cost_estimate=pl.CostEstimate(flops=1, bytes_accessed=1, transcendentals=0),
        name="inflow_near",
    )(core, swap, first, second, vel_index, al16)


def small_call(kernel, outs, name, specs, args, scratch=(), limit=16):
    vmem = pl.BlockSpec(memory_space=pltpu.VMEM)
    smem = pl.BlockSpec(memory_space=pltpu.SMEM)
    return pl.pallas_call(
        kernel,
        in_specs=[smem if s == "s" else vmem for s in specs],
        out_specs=[vmem] * len(outs),
        out_shape=[jax.ShapeDtypeStruct(o, jnp.float32) for o in outs],
        scratch_shapes=list(scratch),
        compiler_params=pltpu.CompilerParams(vmem_limit_bytes=limit * MIB),
        name=name,
    )(*args)


def pair_kernel(*refs):
    parts, (near_ref, far_ref) = refs[:-2], refs[-2:]
    value = parts[0][...]
    for part in parts[1:]:
        value = value + part[...]
    near_ref[...] = value[0:PAY]
    far_ref[...] = value[PAY:]


def total_kernel(*refs):
    parts, (all_ref, up_ref, down_ref) = refs[:-3], refs[-3:]
    value = parts[0][...]
    for part in parts[1:]:
        value = value + part[...]
    all_ref[...] = value
    up_ref[...] = value[UP:DOWN]
    down_ref[...] = value[M1:AA]


def mix(inverse, values):
    return [sum(inverse[k, j] * values[j] for j in range(MOM)) for k in range(MOM)]


def chunk_kernel(inv_ref, own_ref, low_ref, high_ref, send_ref):
    plane = lax.broadcasted_iota(jnp.int32, (SUB, LANES), 0)
    inverse = {(k, j): inv_ref[k, j] for k in range(MOM) for j in range(MOM)}
    inner, outer, later = [], [], []
    for m in range(MOM):

        def row(ref, at):
            return ref[at : at + 1, :]

        first = own_ref[M1 + m * SUB : M1 + (m + 1) * SUB, :]
        second = own_ref[AA + m * SUB : AA + (m + 1) * SUB, :]
        low = low_ref[M1 + m * SUB : M1 + (m + 1) * SUB, :]
        high = high_ref[m * SUB : (m + 1) * SUB, :]
        below = DOWN - M1 + m
        inner.append(
            first + jnp.where(plane == 0, row(low_ref, m), 0.0) + jnp.where(plane == SUB - 1, row(high_ref, below), 0.0)
        )
        outer.append(
            jnp.where(plane < SUB // 2, high, low)
            + jnp.where(plane == 0, row(own_ref, UP + m), 0.0)
            + jnp.where(plane == SUB - 1, row(own_ref, DOWN + m), 0.0)
        )
        later.append(
            second
            + jnp.where(plane == 0, row(low_ref, MOM + m), 0.0)
            + jnp.where(plane == 1, row(low_ref, 2 * MOM + m), 0.0)
            + jnp.where(plane == SUB - 1, row(high_ref, below + MOM), 0.0)
            + jnp.where(plane == SUB - 2, row(high_ref, below + 2 * MOM), 0.0)
        )
    local, around = mix(inverse, inner), mix(inverse, outer)
    for n in range(4):
        send_ref[n * 16 : n * 16 + SUB, :] = local[n + 1]
        send_ref[n * 16 + SUB : (n + 1) * 16, :] = around[n + 1]
        send_ref[MOVED + n * SUB : MOVED + (n + 1) * SUB, :] = inner[n + 1]
    for n, k in enumerate(STILL):
        send_ref[FIXED + n * SUB : FIXED + (n + 1) * SUB, :] = local[k]
        send_ref[EDGE + n : EDGE + n + 1, :] = around[k][0:1]
        send_ref[EDGE + 4 + n : EDGE + 5 + n, :] = around[k][SUB - 1 :]
    for m in range(MOM):
        send_ref[LATER + m * SUB : LATER + (m + 1) * SUB, :] = later[m]
    send_ref[SQUARE:SENT, :] = sum((local[m] - inner[m]) ** 2 for m in range(MOM) if not 1 <= m <= 4)


def sweeps(source):
    rows = source.shape[0]
    field = source
    for _ in range(SWEEPS):
        beside = pltpu.roll(field, 1, axis=0) + pltpu.roll(field, rows - 1, axis=0)
        beside = beside + roll_y(field, 1) + roll_y(field, -1) + roll_z(field, 1) + roll_z(field, -1)
        field = (source + coupling * beside) * (1.0 / (1.0 + 6.0 * coupling))
    return field


def fields_kernel(place_ref, inv_ref, cst_ref, *refs, blocks):
    parts = refs[:blocks]
    h1_ref, later_ref, next_ref, up_ref, down_ref, norm_ref, whole = refs[blocks:]
    mine = place_ref[0]
    for k in range(blocks):
        whole[jnp.bitwise_xor(mine, k)] = parts[k][...]

    def rows(first, count):
        return jnp.concatenate([whole[k, first : first + count, :] for k in range(blocks)], axis=1)

    def fold(value):
        return sum(value[:, k * LANES : (k + 1) * LANES] for k in range(blocks))

    square = sum(whole[k, SQUARE:SENT, :] for k in range(blocks))
    al = cst_ref[0, 0:SUB, :]
    edges = rows(EDGE, SUB)
    plane = lax.broadcasted_iota(jnp.int32, al.shape, 0)
    moved = []
    for n, m in enumerate(PICK):
        if 1 <= m <= 4:
            value = sweeps(rows((m - 1) * 16, 16))
            square = square + fold((value[0:SUB] - rows(MOVED + (m - 1) * SUB, SUB)) ** 2)
        else:
            k = STILL.index(m)
            around = jnp.where(
                plane == 0, edges[k : k + 1], jnp.where(plane == SUB - 1, edges[4 + k : 5 + k], 0.0)
            )
            value = jnp.concatenate([rows(FIXED + k * SUB, SUB), around], axis=0)
        given = cst_ref[1 if n in (0, 4) else 2] * value
        inside = given[0:SUB]
        shifted = [
            inside,
            pltpu.roll(given, 1, axis=0)[0:SUB],
            pltpu.roll(given, 2 * SUB - 1, axis=0)[0:SUB],
            roll_y(inside, 1),
            roll_y(inside, -1),
            roll_z(inside, 1),
            roll_z(inside, -1),
        ]
        for s in range(SETS):
            value = al * shifted[s]
            for k in range(blocks):
                first = (s * 8 + n) * SUB
                h1_ref[k, first : first + SUB, :] = value[:, k * LANES : (k + 1) * LANES]
        moved.append(shifted)
    norm_ref[...] = square

    matrices = stream_matrices()
    moments = []
    for m in range(MOM):
        value = rows(LATER + m * SUB, SUB)
        for s in range(SETS):
            for n in range(8):
                factor = float(matrices[s, m, n])
                if factor != 0.0:
                    value = value + factor * moved[n][s]
        later_ref[m * SUB : (m + 1) * SUB, :] = value
        moments.append(value)
    inverse = {(k, j): inv_ref[k, j] for k in range(MOM) for j in range(MOM)}
    for m, value in enumerate(mix(inverse, moments)):
        next_ref[m * SUB : (m + 1) * SUB, :] = value
        if 1 <= m <= 4:
            up_ref[(m - 1) * 4 : m * 4, :] = value[SUB // 2 :]
            down_ref[(m - 1) * 4 : m * 4, :] = value[: SUB // 2]


def last_kernel(
    place_ref, cst_ref, later_ref, next_ref, low_ref, high_ref, norm1_ref, h2_ref, out_ref, norm_ref, wide, *, blocks
):
    mine = place_ref[0]
    square = jnp.zeros((SUB, LANES), jnp.float32)
    for m in range(MOM):
        value = next_ref[m * SUB : (m + 1) * SUB, :]
        if 1 <= m <= 4:
            at = slice((m - 1) * 4, m * 4)
            value = sweeps(jnp.concatenate([value, high_ref[at, :], low_ref[at, :]], axis=0))[0:SUB]
        off = (value - later_ref[m * SUB : (m + 1) * SUB, :]) ** 2
        for k in range(blocks):
            wide[m, k] = value[:, k * LANES : (k + 1) * LANES]
            square = square + off[:, k * LANES : (k + 1) * LANES]
        out_ref[m] = wide[m, mine]
        if m in PICK:
            n = PICK.index(m)
            given = cst_ref[1 if n in (0, 4) else 2, 0:SUB, :] * value
            for k in range(blocks):
                h2_ref[k, n * SUB : (n + 1) * SUB, :] = given[:, k * LANES : (k + 1) * LANES]
    norm_ref[0:1, :] = jnp.sum(norm1_ref[...], axis=0, keepdims=True)
    norm_ref[1:2, :] = jnp.sum(square, axis=0, keepdims=True)


def finish_kernel(
    core_ref, carried_ref, inflow_ref, swap_ref, first_ref, second_ref, h1_ref, h2_ref, index_ref, out_ref,
    rows, fields, table, far, ready, sems, *, blocks
):
    group = pl.program_id(0)

    @pl.when(group == 0)
    def _():
        speed = [speed_range * (2.0 * index_ref[a : a + 1, :].astype(jnp.float32) + 1.0 - NVX) / NVX for a in range(3)]
        for n, row in enumerate(functions_of(*speed)[1]):
            table[n : n + 1, :] = row
        base = table[...]
        speeds = []
        for c in speed:
            speeds.append(jnp.where(c > 0, time_step * c, 0.0))
            speeds.append(jnp.where(c < 0, -time_step * c, 0.0))
        full = jnp.concatenate([base * (1.0 - sum(speeds))] + [base * s for s in speeds] + [base], axis=0)
        high = full.astype(jnp.bfloat16).astype(jnp.float32)
        stacked = jnp.concatenate([high, high, full - high, jnp.zeros_like(full)], axis=0).astype(jnp.bfloat16)
        for g in range(rows.shape[0]):
            rows[g] = stacked[:, g * LANES : (g + 1) * LANES]
        left = lax.broadcasted_iota(jnp.int32, (LANES, LANES), 1) < LANES // 2

        @pl.loop(0, blocks)
        def _(k):
            at = pl.ds(pl.multiple_of(k * LANES, LANES), LANES)
            for x in range(SUB):
                first = h1_ref[k, pl.ds(x, SETS * 8, stride=SUB), :]
                second = h2_ref[k, pl.ds(x, 8, stride=SUB), :]
                value = jnp.concatenate([first, second, first, second], axis=0).T
                high = value.astype(jnp.bfloat16).astype(jnp.float32)
                fields[x, at, 0:LANES] = jnp.where(left, high, value - high).astype(jnp.bfloat16)
                fields[x, at, LANES:] = jnp.where(left, high, 0.0).astype(jnp.bfloat16)

    stride = blocks * SUB
    pitch = stride + PAD
    slot = lax.rem(group, 2)
    out = ready.reshape(2 * LANES * pitch, LANES)

    def store(g):
        side = lax.rem(g, 2)
        return pltpu.make_async_copy(
            ready.at[side, :, pl.ds(0, stride)], out_ref.at[pl.ds(g * LANES, LANES)], sems.at[side]
        )

    @pl.when(group >= 2)
    def _():
        store(group - 2).wait()

    here = index_ref[0:1, pl.ds(pl.multiple_of(group * LANES, LANES), LANES)]
    px = here * 2 >= NVX
    core = core_ref[0]

    def put(at, value):
        far[at, :] = inflow_ref[0, 0, at, :] + inflow_ref[0, 2, at, :] * value

    from_far = jnp.broadcast_to(px, (NZ, LANES)) == (core == 0)
    halo_rows((swap_ref, first_ref, second_ref), core, from_far, 0, blocks, put)
    inflow = (lambda: far[...], lambda: inflow_ref[0, 1])
    for x in range(SUB):
        value = carried_ref[0, x] + jnp.dot(fields[x], rows[group], preferred_element_type=jnp.float32)
        if x in (0, 1):
            value = value + jnp.where(px, inflow[x](), 0.0)
        elif x in (SUB - 2, SUB - 1):
            value = value + jnp.where(px, 0.0, inflow[SUB - 1 - x]())
        for k in range(blocks):
            first = slot * (LANES * pitch) + k * SUB + x
            out[pl.ds(first, LANES, stride=pitch), :] = value[k * LANES : (k + 1) * LANES].T
    store(group).start()
    last = rows.shape[0] - 1

    @pl.when(group == last)
    def _():
        if last > 0:
            store(group - 1).wait()
        store(group).wait()


def finish(core, carried_part, inflow_part, swap, first, second, h1, h2, vel_index, vels, blocks):
    cells = blocks * LANES
    groups = vels // LANES
    vmem = pl.BlockSpec(memory_space=pltpu.VMEM)
    return pl.pallas_call(
        functools.partial(finish_kernel, blocks=blocks),
        grid=(groups,),
        in_specs=[
            pl.BlockSpec(memory_space=pltpu.SMEM),
            pl.BlockSpec((1, SUB, cells, LANES), lambda g: (g, 0, 0, 0)),
            pl.BlockSpec((1, 3, cells, LANES), lambda g: (g, 0, 0, 0)),
            pl.BlockSpec((1, 1, cells, LANES), lambda g: (g, 1, 0, 0)),
            pl.BlockSpec((1, 1, cells // 2, LANES), lambda g: (g, 0, 0, 0)),
            pl.BlockSpec((1, 1, cells // 2, LANES), lambda g: (g, 0, 0, 0)),
            vmem,
            vmem,
            vmem,
        ],
        out_specs=pl.BlockSpec(memory_space=pl.ANY),
        out_shape=jax.ShapeDtypeStruct((vels, blocks * SUB, LANES), jnp.float32),
        scratch_shapes=[
            pltpu.VMEM((groups, 256, LANES), jnp.bfloat16),
            pltpu.VMEM((SUB, cells, 256), jnp.bfloat16),
            pltpu.VMEM((8, vels), jnp.float32),
            pltpu.VMEM((cells, LANES), jnp.float32),
            pltpu.VMEM((2, LANES, blocks * SUB + PAD, LANES), jnp.float32),
            pltpu.SemaphoreType.DMA((2,)),
        ],
        compiler_params=pltpu.CompilerParams(vmem_limit_bytes=40 * MIB),
        cost_estimate=pl.CostEstimate(
            flops=2 * 256 * vels * blocks * SUB * LANES, bytes_accessed=8 * vels * blocks * SUB * LANES, transcendentals=0
        ),
        name="finish_dist",
    )(core, carried_part, inflow_part, swap, first, second, h1, h2, vel_index)


def ring(axis, step):
    size = lax.axis_size(axis)
    return [(i, (i + step) % size) for i in range(size)]


def shards(dist, vel_index, relax, wall_mask, macro_inverse):
    vels, width, cells = dist.shape
    blocks = cells // LANES
    peers, slabs = lax.axis_size("vel"), lax.axis_size("space")
    assert width == SUB and peers % blocks == 0 and slabs == 4 and blocks % 2 == 0
    sub = peers // blocks
    me = lax.axis_index("vel")
    place = (me // sub).astype(jnp.int32).reshape(1)
    core = (lax.axis_index("space") % 2).astype(jnp.int32).reshape(1)

    flat = dist.reshape(vels, width, blocks, LANES).transpose(0, 2, 1, 3).reshape(vels, blocks * width, LANES)
    speed = speed_range * (2.0 * vel_index.astype(jnp.float32) + 1.0 - NVX) / NVX

    wall = wall_mask > 0
    coefficients = jnp.stack(
        [
            jnp.where(wall, 0.0, 1.0 - relax),
            jnp.where(wall, 1.0, relax),
            jnp.where(wall, 0.0, relax),
        ],
        0,
    )
    from_low = lax.ppermute(coefficients[:, SUB - 1 :], "space", ring("space", 1))
    from_high = lax.ppermute(coefficients[:, :1], "space", ring("space", -1))

    leaving, read = first_stream(flat, vel_index, vels, blocks)
    (leaving, from_low, from_high) = lax.optimization_barrier((leaving, from_low, from_high))
    swap = lax.ppermute(leaving, "space", [(i, i ^ 1) for i in range(slabs)])
    cst = jnp.concatenate(
        [coefficients, from_high, jnp.zeros((3, SUB - 2, cells), jnp.float32), from_low], 1
    )

    parts = both_moments(place, read, leaving, vel_index, cst, vels, blocks)
    (swap, parts) = lax.optimization_barrier((swap, parts))

    half = cells // 2
    start = core[0] * half
    mine = lax.dynamic_slice_in_dim(leaving, start, half, 2)
    other = lax.dynamic_slice_in_dim(swap, start, half, 2)
    plus = speed[0].reshape(vels // LANES, 1, 1, LANES) > 0
    across = jnp.where(plus == (core[0] == 1), mine, other)
    (across, parts) = lax.optimization_barrier((across, parts))
    over = [(i, i ^ 2) for i in range(slabs)]
    first = [lax.ppermute(across[:, 0:1], "space", over)]

    def beside(step):
        return [(i, (i // sub ^ step) * sub + i % sub) for i in range(peers)]

    most = vels // LANES * 3 // 4 * LANES
    spans = [(0, vels)] if vels < 2 * LANES else [(0, most), (most, vels - most)]

    got = [parts[0]] + [lax.ppermute(parts[k], "vel", beside(k)) for k in range(1, blocks // 2)]
    carried_part = carried(read, vel_index, coefficients[0], *spans[0], blocks)
    (got[1], carried_part) = lax.optimization_barrier((got[1], carried_part))
    near, far = small_call(pair_kernel, [(PAY, LANES)] * 2, "sum_near", "v" * len(got), got)
    got = [near, lax.ppermute(far, "vel", beside(blocks // 2))]
    if len(spans) > 1:
        (al, _) = lax.optimization_barrier((coefficients[0], near))
        carried_part = carried(read, vel_index, al, *spans[1], blocks, carried_part)
        (got[1], carried_part) = lax.optimization_barrier((got[1], carried_part))
    if sub > 1:
        part = sum(got)
        got = [part]
        for k in range(1, sub):
            pairs = [(i, i // sub * sub + (i % sub + k) % sub) for i in range(peers)]
            got.append(lax.ppermute(part, "vel", pairs))
    chunk, up, down = small_call(
        total_kernel, [(PAY, LANES), (DOWN - UP, LANES), (AA - M1, LANES)], "sum_moments", "v" * len(got), got
    )
    (first[0], up, down) = lax.optimization_barrier((first[0], up, down))
    low = lax.ppermute(up, "space", ring("space", 1))
    high = lax.ppermute(down, "space", ring("space", -1))
    (send,) = small_call(
        chunk_kernel, [(SENT, LANES)], "local_fields", "svvv", (macro_inverse, chunk, low, high)
    )
    pieces = [send] + [lax.ppermute(send, "vel", beside(k)) for k in range(1, blocks // 2 + 1)]
    across1, send = lax.optimization_barrier((across[:, 1:2], send))
    first.append(lax.ppermute(across1, "space", over))
    swap_chip = [(i, i ^ 1) for i in range(slabs)]
    second = [lax.ppermute(first[0], "space", swap_chip)]
    (second[0], send) = lax.optimization_barrier((second[0], send))
    inflow_part = inflow_near(core, swap, first[0], second[0], vel_index, cst[0], vels, blocks)
    (pieces[blocks // 2], inflow_part) = lax.optimization_barrier((pieces[blocks // 2], inflow_part))
    pieces += [lax.ppermute(pieces[blocks // 2], "vel", beside(k)) for k in range(1, blocks // 2)]

    h1, later, following, up2, down2, norm1 = small_call(
        functools.partial(fields_kernel, blocks=blocks),
        [
            (blocks, SETS * 8 * SUB, LANES),
            (MOM * SUB, cells),
            (MOM * SUB, cells),
            (16, cells),
            (16, cells),
            (SUB, LANES),
        ],
        "first_fields",
        "ssv" + "v" * blocks,
        (place, macro_inverse, cst, *pieces),
        [pltpu.VMEM((blocks, SENT, LANES), jnp.float32)],
        10,
    )
    (first[1], up2) = lax.optimization_barrier((first[1], up2))
    second.append(lax.ppermute(first[1], "space", swap_chip))
    low2 = lax.ppermute(up2, "space", ring("space", 1))
    high2 = lax.ppermute(down2, "space", ring("space", -1))
    h2, owned, squares = small_call(
        functools.partial(last_kernel, blocks=blocks),
        [(blocks, 8 * SUB, LANES), (MOM, SUB, LANES), (2, LANES)],
        "last_fields",
        "svvvvvv",
        (place, cst, later, following, low2, high2, norm1),
        [pltpu.VMEM((MOM, blocks, SUB, LANES), jnp.float32)],
        10,
    )

    around = [lax.ppermute(squares, "space", ring("space", k)) for k in range(1, slabs)]
    (second[1], h2) = lax.optimization_barrier((second[1], h2))
    if sub > 1:
        owned = lax.dynamic_slice_in_dim(owned, (me % sub) * (LANES // sub), LANES // sub, 2)

    out = finish(
        core, carried_part, inflow_part, swap, first[1], second[1], h1, h2, vel_index, vels, blocks
    )
    (around[0], out) = lax.optimization_barrier((around[0], out))
    slab = lax.axis_index("space")
    every = [squares] + around
    ordered = [
        functools.reduce(lambda a, k: jnp.where((slab - k) % slabs == j, every[k], a), range(1, slabs), every[0])
        for j in range(slabs)
    ]
    norms = jnp.sqrt(jnp.sum(sum(ordered), axis=1))
    out = out.reshape(vels, blocks, width, LANES).transpose(0, 2, 1, 3).reshape(vels, width, cells)
    return (out, owned, norms)


def solution(mesh):
    return jax.shard_map(
        shards,
        mesh=mesh,
        in_specs=(P("vel", "space", None), P(None, "vel"), P("space", None), P("space", None), P()),
        out_specs=(P("vel", "space", None), P(None, "space", "vel"), P()),
        check_vma=False,
    )
```
